32 devices in a mesh: batch: 8 (over z, y), rows: 4 (over x, core).
Axes of the slice: x: 2, y: 2, z: 4, core: 2. Of those that a mesh axis runs over, the one named last changes fastest.
Arguments:
- large_in: bfloat16 [192, 4, 4, 14, 384], P('batch', 'rows'), may hold values from -6 to 6
- small_in: bfloat16 [576, 4, 2, 6, 384], P('batch', 'rows'), may hold values from -6 to 6
- large_cot: bfloat16 [192, 4, 4, 14, 384], P('batch', 'rows'), may hold values from -6 to 6
- small_cot: bfloat16 [576, 4, 2, 6, 384], P('batch', 'rows'), may hold values from -6 to 6
- crop_counts: int32 [8, 2], P('batch'), may hold values from 12 to 72, as said below
- band_bounds: int32 [2, 5], replicated, may hold values from 0 to 14, as said below
- row_interp: float32 [6, 14], replicated, may hold values from 0 to 0.5
- col_interp: float32 [4, 8], replicated, may hold values from 0 to 0.5
- norm1_gain: float32 [2, 384], replicated, may hold values from 0.5 to 1.5
- norm1_bias: float32 [2, 384], replicated, may hold values from -2 to 2
- filters: float32 [2, 2, 14, 8, 384], replicated, may hold values from -4 to 4
- norm2_gain: float32 [2, 384], replicated, may hold values from 0.5 to 1.5
- norm2_bias: float32 [2, 384], replicated, may hold values from -2 to 2
- fc1_weight: bfloat16 [2, 384, 1536], replicated, may hold values from -0.3125 to 0.3125
- fc1_bias: float32 [2, 1536], replicated, may hold values from -2 to 2
- fc2_weight: bfloat16 [2, 1536, 384], replicated, may hold values from -0.15625 to 0.15625
- fc2_bias: float32 [2, 384], replicated, may hold values from -2 to 2
Outputs:
- large_out: float32 [192, 4, 4, 14, 384], P('batch', 'rows')
- small_out: float32 [576, 4, 2, 6, 384], P('batch', 'rows')
- large_grad: float32 [192, 4, 4, 14, 384], P('batch', 'rows')
- small_grad: float32 [576, 4, 2, 6, 384], P('batch', 'rows')
- grad_norm1_gain: float32 [2, 384], replicated
- grad_norm1_bias: float32 [2, 384], replicated
- grad_filters: float32 [2, 2, 14, 8, 384], replicated
- grad_norm2_gain: float32 [2, 384], replicated
- grad_norm2_bias: float32 [2, 384], replicated
- grad_fc1_weight: float32 [2, 384, 1536], replicated
- grad_fc1_bias: float32 [2, 1536], replicated
- grad_fc2_weight: float32 [2, 1536, 384], replicated
- grad_fc2_bias: float32 [2, 384], replicated
The draws below stay inside these ranges and needn't reach their ends.
Inputs may be any that keep to these rules, and one draw needn't show every extreme that they name: `crop_counts`: row b gives the live large and live small crops on each device of batch index b: at least half of 24 and of 72; in every draw some batch index has all 24 and 72 live. `band_bounds`: row 0 cuts the 14 rows of a large crop into one band per rows index, row 1 the 6 rows of a small crop: entry j is band j's first row, the last entry is the grid's height. Large bands hold 1 to 4 rows, small ones 0 to 2, and in each row some band holds exactly its most.
All inputs are finite; a program needn't handle non-finite values.
Results may differ from the reference program's by a relative error of at most 0.025.
The reference program's roundings to bfloat16 on the way count: a program that leaves them out, or rounds other values in their place, can miss the bound.
Values may be sent and summed in bfloat16 or wider, within the bound.
A program may use at most 256 MiB of HBM per device.

```python
import math
import jax
import jax.numpy as jnp
from jax import lax

D = 384
FF = 1536
HL = 14
WL = 14
FL = 8
HS = 6
WS = 6
FS = 4
BL = 4
BS = 2
KL = 16
KS = 8
LAYERS = 2
LS = 24
SS = 72
IMAGES_L = 192
IMAGES_S = 576
N_BATCH = 8
N_ROWS = 4


def draw_crop_counts(key, part):
    key = jax.random.fold_in(key, 11)
    large_live = jax.random.randint(jax.random.fold_in(key, 1), (N_BATCH,), max(1, LS // 2), LS + 1)
    small_live = jax.random.randint(jax.random.fold_in(key, 2), (N_BATCH,), max(1, SS // 2), SS + 1)
    chosen = jax.random.randint(jax.random.fold_in(key, 3), (), 0, N_BATCH)
    picked = jnp.arange(N_BATCH, dtype=jnp.int32) == chosen
    large_live = jnp.where(picked, LS, large_live)
    small_live = jnp.where(picked, SS, small_live)
    return jnp.stack([large_live, small_live], axis=1).astype(jnp.int32)


def band_lengths(key, grid_height, most_rows, least_rows):
    places = jnp.arange(N_ROWS, dtype=jnp.int32)
    widest = jax.random.randint(jax.random.fold_in(key, 0), (), 0, N_ROWS)
    lengths = jnp.where(places == widest, most_rows, least_rows).astype(jnp.int32)
    for step_number in range(grid_height - least_rows * N_ROWS - (most_rows - least_rows)):
        scores = jax.random.randint(jax.random.fold_in(key, step_number + 1), (N_ROWS,), 0, 1 << 20) * N_ROWS + places
        scores = jnp.where(lengths < most_rows, scores, -1)
        lengths = lengths + (places == jnp.argmax(scores)).astype(jnp.int32)
    return jnp.concatenate([jnp.zeros((1,), jnp.int32), jnp.cumsum(lengths).astype(jnp.int32)])


def draw_band_bounds(key, part):
    key = jax.random.fold_in(key, 17)
    large_bounds = band_lengths(jax.random.fold_in(key, 1), HL, BL, 1)
    small_bounds = band_lengths(jax.random.fold_in(key, 2), HS, BS, 0)
    return jnp.stack([large_bounds, small_bounds]).astype(jnp.int32)


def block_scale(rng, extent, cuts, smallest, top_value):
    factor_of, own = 1.0, jax.random.fold_in(rng, 6)
    for axis_at, parts in cuts:
        draws = jnp.exp(jax.random.uniform(jax.random.fold_in(own, axis_at), (parts,), jnp.float32, smallest / len(cuts), top_value / len(cuts)))
        factor_of = factor_of * jnp.repeat(draws, extent[axis_at] // parts).reshape([-1 if axis == axis_at else 1 for axis in range(len(extent))])
    return factor_of


def normal_values(own_key, extent, width, bound, cuts=(), kind=jnp.bfloat16):
    gain = block_scale(own_key, extent, cuts, -0.22, 0.18) if cuts else 1.0
    array = jax.random.normal(own_key, extent, jnp.float32) * width * gain
    return jnp.minimum(jnp.maximum(array, -bound), bound).astype(kind)


def setup_inputs(seed: int = 0) -> dict:
    keys = jax.random.split(jax.random.key(seed), 18)
    return {
        "large_in": normal_values(keys[0], (IMAGES_L, N_ROWS, BL, WL, D), 1.0, 6.0, ((0, 8), (1, 4))),
        "small_in": normal_values(keys[1], (IMAGES_S, N_ROWS, BS, WS, D), 1.0, 6.0, ((0, 8), (1, 4))),
        "large_cot": normal_values(keys[2], (IMAGES_L, N_ROWS, BL, WL, D), 1.0, 6.0, ((0, 8), (1, 4))),
        "small_cot": normal_values(keys[3], (IMAGES_S, N_ROWS, BS, WS, D), 1.0, 6.0, ((0, 8), (1, 4))),
        "crop_counts": draw_crop_counts(jax.random.fold_in(keys[17], 71), 0),
        "band_bounds": draw_band_bounds(jax.random.fold_in(keys[17], 71), 0),
        "row_interp": jnp.clip(jax.random.uniform(keys[6], (HS, HL), jnp.float32, 0.0, 0.5), 0.0, 0.5),
        "col_interp": jnp.clip(jax.random.uniform(keys[7], (FS, FL), jnp.float32, 0.0, 0.5), 0.0, 0.5),
        "norm1_gain": jnp.clip(1.0 + 0.1 * jax.random.normal(keys[8], (LAYERS, D), jnp.float32), 0.5, 1.5),
        "norm1_bias": normal_values(keys[9], (LAYERS, D), 0.3, 2.0, (), jnp.float32),
        "filters": normal_values(keys[10], (LAYERS, 2, HL, FL, D), 0.7, 4.0, (), jnp.float32),
        "norm2_gain": jnp.clip(1.0 + 0.1 * jax.random.normal(keys[11], (LAYERS, D), jnp.float32), 0.5, 1.5),
        "norm2_bias": normal_values(keys[12], (LAYERS, D), 0.3, 2.0, (), jnp.float32),
        "fc1_weight": normal_values(keys[13], (LAYERS, D, FF), D ** -0.5, 0.3125),
        "fc1_bias": normal_values(keys[14], (LAYERS, FF), 0.3, 2.0, (), jnp.float32),
        "fc2_weight": normal_values(keys[15], (LAYERS, FF, D), FF ** -0.5, 0.15625),
        "fc2_bias": normal_values(keys[16], (LAYERS, D), 0.3, 2.0, (), jnp.float32),
    }


EPSILON = 1e-06
HIGHEST = lax.Precision.HIGHEST

@jax.custom_vjp
def low(v):
    return lax.optimization_barrier(v.astype(jnp.bfloat16)).astype(jnp.float32)

@jax.custom_vjp
def low_back(v):
    return v

def low_keep(v):
    return (low(v), None)

def low_pass(kept, grad):
    return (grad,)

def back_keep(v):
    return (v, None)

def back_low(kept, grad):
    return (low(grad),)
low.defvjp(low_keep, low_pass)
low_back.defvjp(back_keep, back_low)

def spectral_tables(first_row, band_rows, grid_height, grid_width, col_count, padded, slot_count):
    row_freq = jnp.arange(padded, dtype=jnp.int32)[:, None, None, None]
    col_freq = jnp.arange(col_count, dtype=jnp.int32)[None, :, None, None]
    slot_ids = jnp.arange(slot_count, dtype=jnp.int32)[None, None, :, None]
    columns = jnp.arange(grid_width, dtype=jnp.int32)[None, None, None, :]
    phase = (row_freq * (first_row + slot_ids) * grid_width + col_freq * columns * grid_height) % (grid_height * grid_width)
    angle = phase.astype(jnp.float32) * jnp.float32(2.0 * math.pi / (grid_height * grid_width))
    inside = ((row_freq < grid_height) & (slot_ids < band_rows)).astype(jnp.float32) * jnp.float32(1.0 / math.sqrt(grid_height * grid_width))
    forward = jnp.stack([jnp.cos(angle) * inside, -jnp.sin(angle) * inside])
    folding = jnp.where((col_freq == 0) | (2 * col_freq == grid_width), 1.0, 2.0).astype(jnp.float32)
    return (forward, forward * folding)

def layer_norm(values, norm_gain, norm_bias):
    centred = values - lax.optimization_barrier(jnp.mean(values, axis=-1, keepdims=True))
    variance = lax.optimization_barrier(jnp.mean(centred * centred, axis=-1, keepdims=True))
    return centred * lax.rsqrt(variance + EPSILON) * norm_gain + norm_bias

def dense(values, matrix):
    product = jnp.dot(values.reshape(-1, values.shape[-1]), matrix, precision=HIGHEST, preferred_element_type=jnp.float32)
    return product.reshape(values.shape[:-1] + (matrix.shape[1],))

def spectral(normed, forward, inverse, spectral_filter):
    band_terms = jnp.einsum('jcklsw,ijswd->ijckld', forward, normed, precision=HIGHEST)
    spectrum = low_back(lax.optimization_barrier(jnp.sum(low(band_terms), axis=1)))
    real_part = spectrum[:, 0] * spectral_filter[0] - spectrum[:, 1] * spectral_filter[1]
    imag_part = spectrum[:, 0] * spectral_filter[1] + spectrum[:, 1] * spectral_filter[0]
    filtered = low(jnp.stack([real_part, imag_part], axis=1))
    shared = low_back(jnp.broadcast_to(filtered[:, None], (filtered.shape[0], forward.shape[0]) + filtered.shape[1:]))
    return low_back(jnp.einsum('jcklsw,ijckld->ijswd', inverse, shared, precision=HIGHEST))

def residual_block(values, weights, forward, inverse, spectral_filter):
    gain_one, bias_one, gain_two, bias_two, weight_one, bias_hidden, weight_two, bias_out = weights
    normed = low(layer_norm(values, gain_one, bias_one))
    mixed = spectral(normed, forward, inverse, spectral_filter)
    second = low(layer_norm(mixed, gain_two, bias_two))
    hidden = low_back(dense(second, weight_one) + bias_hidden)
    active = low(jax.nn.gelu(hidden, approximate=False))
    branch = low_back(dense(active, weight_two) + bias_out)
    return values + branch

def pad_rows(spectral_filter, padded):
    return jnp.pad(spectral_filter, ((0, 0), (0, padded - spectral_filter.shape[1]), (0, 0), (0, 0)))

def network(params, large_crops, small_crops, large_mask, small_mask, tables, row_mix, col_mix):
    gains_one, biases_one, all_filters, gains_two, biases_two, weights_one, biases_hidden, weights_two, biases_out = params
    for layer_index in range(LAYERS):
        weights = (gains_one[layer_index], biases_one[layer_index], gains_two[layer_index], biases_two[layer_index], weights_one[layer_index], biases_hidden[layer_index], weights_two[layer_index], biases_out[layer_index])
        small_filter = jnp.einsum('ka,cabd,lb->ckld', row_mix, all_filters[layer_index], col_mix, precision=HIGHEST)
        large_crops = residual_block(large_crops, weights, tables[0], tables[1], pad_rows(all_filters[layer_index], KL))
        small_crops = residual_block(small_crops, weights, tables[2], tables[3], pad_rows(small_filter, KS))
    return (large_crops * large_mask, small_crops * small_mask)

def band_tables(bounds_row, grid_height, grid_width, col_count, padded, slot_count):
    first_rows = bounds_row[:-1]
    band_rows = bounds_row[1:] - bounds_row[:-1]
    forward, inverse = jax.vmap(lambda start_row, rows_in: spectral_tables(start_row, rows_in, grid_height, grid_width, col_count, padded, slot_count))(first_rows, band_rows)
    live_slots = (jnp.arange(slot_count, dtype=jnp.int32)[None, :] < band_rows[:, None]).astype(jnp.float32)
    return (low(forward), low(inverse), live_slots)

def reference(large_in, small_in, large_cot, small_cot, crop_counts, band_bounds, row_interp, col_interp, norm1_gain, norm1_bias, filters, norm2_gain, norm2_bias, fc1_weight, fc1_bias, fc2_weight, fc2_bias):
    params = tuple((member.astype(jnp.float32) for member in (norm1_gain, norm1_bias, filters, norm2_gain, norm2_bias, fc1_weight, fc1_bias, fc2_weight, fc2_bias)))
    forward_large, inverse_large, slots_large = band_tables(band_bounds[0], HL, WL, FL, KL, BL)
    forward_small, inverse_small, slots_small = band_tables(band_bounds[1], HS, WS, FS, KS, BS)
    tables = (forward_large, inverse_large, forward_small, inverse_small)
    row_mix = row_interp.astype(jnp.float32)
    col_mix = col_interp.astype(jnp.float32)

    def per_batch(totals, batch_items):
        large_crops, small_crops, large_cots, small_cots, counts_here = batch_items
        live_large = (jnp.arange(LS, dtype=jnp.int32) < counts_here[0]).astype(jnp.float32)
        live_small = (jnp.arange(SS, dtype=jnp.int32) < counts_here[1]).astype(jnp.float32)
        large_mask = live_large[:, None, None, None, None] * slots_large[None, :, :, None, None]
        small_mask = live_small[:, None, None, None, None] * slots_small[None, :, :, None, None]

        def forward_fn(weights, large_vals, small_vals):
            return network(weights, large_vals, small_vals, large_mask, small_mask, tables, row_mix, col_mix)
        outputs, backward_fn = jax.vjp(forward_fn, params, large_crops.astype(jnp.float32), small_crops.astype(jnp.float32))
        weight_grads, large_grads, small_grads = backward_fn((large_cots.astype(jnp.float32), small_cots.astype(jnp.float32)))
        totals = jax.tree.map(lambda running, addend: running + addend, totals, weight_grads)
        return (totals, (outputs[0], outputs[1], large_grads, small_grads))
    initial = tuple((jnp.zeros_like(member) for member in params))
    batched = (large_in.reshape((N_BATCH, LS) + large_in.shape[1:]), small_in.reshape((N_BATCH, SS) + small_in.shape[1:]), large_cot.reshape((N_BATCH, LS) + large_cot.shape[1:]), small_cot.reshape((N_BATCH, SS) + small_cot.shape[1:]), crop_counts)
    totals, stacked = lax.scan(per_batch, initial, batched)
    large_out, small_out, large_grad, small_grad = stacked
    return (large_out.reshape(large_in.shape), small_out.reshape(small_in.shape), large_grad.reshape(large_in.shape), small_grad.reshape(small_in.shape), totals[0], totals[1], totals[2], totals[3], totals[4], totals[5], totals[6], totals[7], totals[8])
```

```python
import math
from functools import partial
import numpy as np
import jax
import jax.numpy as jnp
from jax import lax
from jax.experimental import pallas as pl
from jax.experimental.pallas import tpu as pltpu
from jax.sharding import PartitionSpec as P

D, FF = 384, 1536
HL, WL, FL = 14, 14, 8
HS, WS, FS = 6, 6, 4
BL, BS = 4, 2
LAYERS = 2
EPS = 1e-6
TL, TS = HL * WL, HS * WS
PER = 3
T = TL + PER * TS
CUT, END = 192, 208
NL, NS = HL * FL, HS * FS
BAND = 96
CH = 512
CB = 512
SMALL = 512
MESH = pl.DeviceIdType.MESH
VMEM_LIMIT = 60 * 2**20
F32, BF16 = jnp.float32, jnp.bfloat16
HIGHEST = lax.Precision.HIGHEST


def table(height, width, count):
    k = np.arange(height)[:, None, None, None]
    l = np.arange(count)[None, :, None, None]
    s = np.arange(height)[None, None, :, None]
    w = np.arange(width)[None, None, None, :]
    phase = (k * s * width + l * w * height) % (height * width)
    angle = phase.astype(np.float32) * np.float32(2.0 * math.pi / (height * width))
    scale = np.float32(1.0 / math.sqrt(height * width))
    both = np.stack([np.cos(angle) * scale, -np.sin(angle) * scale])
    return both.reshape(2, height * count, height * width).astype(jnp.bfloat16).astype(np.float32)


def tables():
    large = np.zeros((2 * NL, END), np.float32)
    large[:, :TL] = table(HL, WL, FL).reshape(2 * NL, TL)
    one = table(HS, WS, FS)
    small = np.zeros((2, PER, NS, T - CUT), np.float32)
    for at in range(PER):
        small[:, at, :, TL - CUT + at * TS : TL - CUT + (at + 1) * TS] = one
    small = small.reshape(2 * PER * NS, T - CUT)
    return [jnp.asarray(t, BF16) for t in (large, small, large.T, small.T)]


def normal(x):
    mean = jnp.mean(x, axis=-1, keepdims=True)
    centred = x - mean
    scale = lax.rsqrt(jnp.mean(centred * centred, axis=-1, keepdims=True) + EPS)
    return centred * scale, scale


def normal_back(grad, gain, unit, scale):
    inner = grad * gain
    first = jnp.mean(inner, axis=-1, keepdims=True)
    second = jnp.mean(inner * unit, axis=-1, keepdims=True)
    return (inner - first - unit * second) * scale


def dot(a, b):
    return jnp.dot(a, b, preferred_element_type=F32)


def dot_nt(a, b):
    return lax.dot_general(a, b, (((1,), (1,)), ((), ())), preferred_element_type=F32)


def dot_tn(a, b):
    return lax.dot_general(a, b, (((0,), (0,)), ((), ())), preferred_element_type=F32)


def analyse(large_table, small_table, values):
    return dot(large_table, values[:END]), dot(small_table, values[CUT:])


def synthesise(large_back, small_back, large, small):
    a, b = dot(large_back, large), dot(small_back, small)
    return jnp.concatenate([a[:CUT], a[CUT:] + b[: END - CUT], b[END - CUT :]], axis=0)


def thrice(x):
    return jnp.concatenate([x] * PER, axis=0)


def gelu_both(h):
    cdf = 0.5 + 0.5 * lax.erf(h * np.float32(math.sqrt(0.5)))
    dens = jnp.exp(h * h * np.float32(-0.5)) * np.float32(1 / math.sqrt(2 * math.pi))
    return h * cdf, cdf + h * dens


def live_rows(live, group):
    t = lax.broadcasted_iota(jnp.int32, (T, 1), 0)
    mask = jnp.where(t < TL, live[group, 0], live[group, PER])
    for at in range(PER - 1):
        mask = jnp.where((t >= TL + at * TS) & (t < TL + (at + 1) * TS), live[group, 1 + at], mask)
    return mask


def whole(shape):
    return pl.BlockSpec(shape, lambda *a: (0,) * len(shape))


def scalars():
    return pl.BlockSpec(memory_space=pltpu.SMEM)


def forward_kernel(row_count, groups, pair, packed_in, packed_cot, live, pick, place, gain1, bias1, filt_l, filt_s, gain2, bias2,
                   w1, b1, w2, b2, tl, ts, tlb, tsb, outs, xs, zs, spec, vs, gs, ps, do,
                   slots, own_sem, send_sem, recv_sem):
    step = pl.program_id(0)
    batch, row = lax.axis_index("batch"), lax.axis_index("rows")
    last = groups // pair - 1

    def remote(which, m, g):
        to = (row + m) % row_count
        given = (packed_in, packed_cot)[which]
        return pltpu.make_async_remote_copy(
            src_ref=given.at[to * groups + g], dst_ref=slots.at[which, m, g],
            send_sem=send_sem.at[which, m - 1, g], recv_sem=recv_sem.at[which, m - 1, g],
            device_id=(batch, to), device_id_type=MESH)

    def mine(which, g):
        given = (packed_in, packed_cot)[which]
        return pltpu.make_async_copy(given.at[row * groups + g], slots.at[which, 0, g], own_sem.at[which, g])

    @pl.when(step == 0)
    def _():
        barrier = pltpu.get_barrier_semaphore()
        for m in range(1, row_count):
            pl.semaphore_signal(barrier, inc=1, device_id=(batch, (row + m) % row_count), device_id_type=MESH)
        for which in range(2):
            @pl.loop(0, groups)
            def _(g):
                mine(which, g).start()
        pl.semaphore_wait(barrier, row_count - 1)
        for which in range(2):
            @pl.loop(0, groups)
            def _(g):
                for m in range(1, row_count):
                    remote(which, m, g).start()

    def take(which, g):
        mine(which, g).wait()
        for m in range(1, row_count):
            remote(which, m, g).wait_recv()
        return dot(pick[...], jnp.concatenate([slots[which, m, g] for m in range(row_count)], axis=0))

    x = [take(0, step * pair + j) for j in range(pair)]
    for n in range(LAYERS):
        v = []
        for j in range(pair):
            xs[n, j] = x[j]
            u, _ = normal(x[j])
            u = (u * gain1[n : n + 1] + bias1[n : n + 1]).astype(BF16)
            xl, xsm = analyse(tl[...], ts[...], u)
            spec[n, j, : 2 * NL] = xl
            spec[n, j, 2 * NL :] = xsm
            lr, li = xl[:NL], xl[NL:]
            sr, si = xsm[: PER * NS], xsm[PER * NS :]
            gr, gi = filt_l[n, 0], filt_l[n, 1]
            yl = jnp.concatenate([lr * gr - li * gi, lr * gi + li * gr], axis=0).astype(BF16)
            gr, gi = thrice(filt_s[n, 0]), thrice(filt_s[n, 1])
            ys = jnp.concatenate([sr * gr - si * gi, sr * gi + si * gr], axis=0).astype(BF16)
            z = synthesise(tlb[...], tsb[...], yl, ys)
            zs[n, j] = z
            q, _ = normal(z)
            q = (q * gain2[n : n + 1] + bias2[n : n + 1]).astype(BF16)
            vs[n, j] = q
            v.append(q)
        v = jnp.concatenate(v, axis=0)
        total = jnp.concatenate(x, axis=0) + b2[n : n + 1]
        for c in range(0, FF, CH):
            h = dot(v, w1[n, :, c : c + CH]) + b1[n : n + 1, c : c + CH]
            g, slope = gelu_both(h)
            g = g.astype(BF16)
            slope = slope.astype(BF16)
            for j in range(pair):
                gs[n, j, :, c : c + CH] = g[j * T : (j + 1) * T]
                ps[n, j, :, c : c + CH] = slope[j * T : (j + 1) * T]
            total = total + dot(g, w2[n, c : c + CH, :])
        x = [total[j * T : (j + 1) * T] for j in range(pair)]
    for j in range(pair):
        spread = dot(place[...], (x[j] * live_rows(live, step * pair + j)).astype(BF16)).astype(BF16)
        for m in range(row_count):
            outs[m, j] = spread[m * BAND : (m + 1) * BAND]

    @pl.when(step == last)
    def _():
        for g in range(groups):
            do[g] = (take(1, g) * live_rows(live, g)).astype(BF16)
        for which in range(2):
            @pl.loop(0, groups)
            def _(g):
                for m in range(1, row_count):
                    remote(which, m, g).wait_send()


def forward(mesh, groups, pair, packed_in, packed_cot, live, small):
    rows = mesh.shape["rows"]
    sizes = [(T, D, F32), (T, D, F32), (2 * NL + 2 * PER * NS, D, F32), (T, D, BF16), (T, FF, BF16), (T, FF, BF16)]
    hbm = pl.BlockSpec(memory_space=pl.ANY)
    return pl.pallas_call(
        partial(forward_kernel, rows, groups, pair),
        grid=(groups // pair,),
        in_specs=[hbm, hbm, scalars()] + [whole(a.shape) for a in small],
        out_specs=[pl.BlockSpec((rows, pair, BAND, D), lambda i: (0, i, 0, 0))]
        + [pl.BlockSpec((LAYERS, pair, a, b), lambda i: (0, i, 0, 0)) for a, b, _ in sizes]
        + [whole((groups, T, D))],
        out_shape=[jax.ShapeDtypeStruct((rows, groups, BAND, D), BF16)]
        + [jax.ShapeDtypeStruct((LAYERS, groups, a, b), t) for a, b, t in sizes]
        + [jax.ShapeDtypeStruct((groups, T, D), BF16)],
        scratch_shapes=[pltpu.VMEM((2, rows, groups, BAND, D), BF16), pltpu.SemaphoreType.DMA((2, groups)),
                        pltpu.SemaphoreType.DMA((2, rows - 1, groups)), pltpu.SemaphoreType.DMA((2, rows - 1, groups))],
        compiler_params=pltpu.CompilerParams(collective_id=1, has_side_effects=True, vmem_limit_bytes=VMEM_LIMIT),
        name="forward",
    )(packed_in, packed_cot, live, *small)


LOW = 2


def add_rows(target, at_target, base, sources, count):
    step = next(s for s in (128, 96, 64, 48, 32, 16) if count % s == 0)

    @pl.loop(0, count // step)
    def _(i):
        at = pl.multiple_of(i * step, 16)
        rows = pl.ds(pl.multiple_of(base + at, 16), step)
        total = at_target[rows, :].astype(F32)
        for ref in sources:
            total = total + ref[pl.ds(at, step), :].astype(F32)
        target[rows, :] = total.astype(BF16)


class Sum:
    def __init__(self, mesh_rows, mesh_batch, acc, full, out, count, bufs, sems, save_sem):
        self.batch, self.row = lax.axis_index("batch"), lax.axis_index("rows")
        self.x_n, self.z_n = mesh_rows // 2, mesh_batch // LOW
        self.acc, self.full, self.out, self.count, self.bufs, self.sems, self.save_sem = acc, full, out, count, bufs, sems, save_sem
        core, x, z, y = self.row % 2, self.row // 2, self.batch // LOW, self.batch % LOW
        self.size = kinds(mesh_rows, mesh_batch)
        self.me = [core, y, z * self.x_n + x]

    def other(self, level, step):
        core, x, z, y = self.row % 2, self.row // 2, self.batch // LOW, self.batch % LOW
        at = (self.me[level] + step) % self.size[level]
        if level == 0:
            return (self.batch, x * 2 + at), at
        if level == 1:
            return (z * LOW + at, self.row), at
        return ((at // self.x_n) * LOW + y, (at % self.x_n) * 2 + core), at

    def region(self, part, level):
        base, count = part * self.count, self.count
        for i in range(level):
            count //= self.size[i]
            base = base + self.me[i] * count
        return base, count

    def rows(self, base, count):
        return pl.ds(pl.multiple_of(base, 16), count)

    def down(self, part, level, step):
        base, count = self.region(part, level)
        device, at = self.other(level, step)
        chunk = count // self.size[level]
        return pltpu.make_async_remote_copy(
            src_ref=self.acc.at[self.rows(base + at * chunk, chunk)], dst_ref=self.bufs[level].at[part, step - 1],
            send_sem=self.sems[level].at[0, part, step - 1], recv_sem=self.sems[level].at[1, part, step - 1],
            device_id=device, device_id_type=MESH)

    def up(self, part, level, step, arriving=False):
        base, count = self.region(part, level + 1)
        device, _ = self.other(level, step)
        if arriving:
            low, _ = self.region(part, level)
            base = low + (self.me[level] - step + self.size[level]) % self.size[level] * count
        rows = self.rows(base, count)
        return pltpu.make_async_remote_copy(
            src_ref=self.full.at[rows], dst_ref=self.full.at[rows],
            send_sem=self.sems[level].at[2, part, step - 1], recv_sem=self.sems[level].at[3, part, step - 1],
            device_id=device, device_id_type=MESH)

    def save(self, part):
        rows = self.rows(part * self.count, self.count)
        return pltpu.make_async_copy(self.full.at[rows], self.out.at[rows], self.save_sem.at[part])

    def stage(self, part, k):
        if 1 <= k <= 3:
            level = k - 1
            for step in range(1, self.size[level]):
                self.down(part, level, step).wait()
            base, count = self.region(part, level + 1)
            add_rows(self.full if k == 3 else self.acc, self.acc, base,
                     [self.bufs[level].at[part, s] for s in range(self.size[level] - 1)], count)
        if k < 3:
            for step in range(1, self.size[k]):
                self.down(part, k, step).start()
        if k >= 4:
            level = 6 - k
            for step in range(1, self.size[level]):
                self.up(part, level, step).wait_send()
                self.up(part, level, step, True).wait_recv()
        if 3 <= k < 6:
            for step in range(1, self.size[5 - k]):
                self.up(part, 5 - k, step).start()
        if k == 6:
            self.save(part).start()


def kinds(mesh_rows, mesh_batch):
    size = [2, LOW, (mesh_rows // 2) * (mesh_batch // LOW)]
    return size


def columns(mesh_rows, mesh_batch):
    sizes = {w: w * padded(mesh_rows, mesh_batch, 2 * D * (CB // w)) for w in (256, 128)}
    return min(sizes, key=sizes.get)


def padded(mesh_rows, mesh_batch, count):
    unit = 16 * math.prod(kinds(mesh_rows, mesh_batch))
    return -(-count // unit) * unit


def sum_scratch(mesh_rows, mesh_batch, parts, count, width):
    size = kinds(mesh_rows, mesh_batch)
    shapes = [pltpu.VMEM((parts * count, width), BF16)] * 2
    for n in size:
        count //= n
        shapes.append(pltpu.VMEM((parts, n - 1, count, width), BF16))
    return shapes + [pltpu.SemaphoreType.DMA((4, parts, n - 1)) for n in size] + [pltpu.SemaphoreType.DMA((parts,))]


def backward_kernel(row_count, batch_count, groups, pair, live, pick, place, gain1, filt_l, filt_s, gain2, w1, w2, tl, ts, tlb, tsb,
                    mix, fold, outs, do_in, xs, zs, spec, vs, gs, ps,
                    out_land, grad_land, weights_out, small_out,
                    dx, dv, do, dot_, vt, dh, gslots, dvec, dhid, dfl, dfs, out_sem, grad_sem, own_sem, *sums):
    i = pl.program_id(0)
    batch, row = lax.axis_index("batch"), lax.axis_index("rows")
    chunks, pairs = FF // CB, groups // pair
    per = chunks + pairs
    compute_steps = LAYERS * per
    layer, q = LAYERS - 1 - i // per, i % per
    width = columns(row_count, batch_count)
    part_rows = padded(row_count, batch_count, 2 * D * (CB // width))
    small_rows = padded(row_count, batch_count, SMALL)
    weights = Sum(row_count, batch_count, sums[0], sums[1], weights_out, part_rows, sums[2:5], sums[5:8], sums[8])
    small = Sum(row_count, batch_count, sums[9], sums[10], small_out, small_rows, sums[11:14], sums[14:17], sums[17])

    def send_out(m, g):
        return pltpu.make_async_remote_copy(
            src_ref=outs.at[m, g], dst_ref=out_land.at[m, g], send_sem=out_sem.at[0, m - 1, g], recv_sem=out_sem.at[1, m - 1, g],
            device_id=(batch, (row - m + row_count) % row_count), device_id_type=MESH)

    def send_grad(m, g):
        return pltpu.make_async_remote_copy(
            src_ref=gslots.at[m, g], dst_ref=grad_land.at[m, g], send_sem=grad_sem.at[0, m - 1, g], recv_sem=grad_sem.at[1, m - 1, g],
            device_id=(batch, (row - m + row_count) % row_count), device_id_type=MESH)

    def keep_out():
        return pltpu.make_async_copy(outs.at[0], out_land.at[0], own_sem.at[0])

    def keep_grad():
        return pltpu.make_async_copy(gslots.at[0], grad_land.at[0], own_sem.at[1])

    @pl.when(i == 0)
    def _():
        barrier = pltpu.get_barrier_semaphore()
        greeted = 0
        for m in range(1, row_count):
            pl.semaphore_signal(barrier, inc=1, device_id=(batch, (row + m) % row_count), device_id_type=MESH)
            greeted += 1
        for level in (1, 2):
            for step in range(1, weights.size[level]):
                pl.semaphore_signal(barrier, inc=1, device_id=weights.other(level, step)[0], device_id_type=MESH)
                greeted += 1
        keep_out().start()
        if part_rows > 2 * D * (CB // width):
            weights.acc[...] = jnp.zeros_like(weights.acc)
        for g in range(groups):
            dx[g] = do_in[g].astype(F32)
        for ref in (dvec, dfl, dfs):
            ref[...] = jnp.zeros_like(ref)
        pl.semaphore_wait(barrier, greeted)

    @pl.when(i < groups)
    def _():
        for m in range(1, row_count):
            send_out(m, i).start()

    @pl.when((i < compute_steps) & (q == 0))
    def _():
        for g in range(groups):
            rows = pl.ds(g * T, T)
            low = dx[g].astype(BF16)
            do[g] = low
            dvec[layer, 4:5] += jnp.sum(low.astype(F32), axis=0, keepdims=True)
        dot_[...] = do[...].reshape(groups * T, D).T
        vt[:D] = vs[0].reshape(groups * T, D).T
        vt[D:] = jnp.ones((16, groups * T), BF16)
        dv[...] = jnp.zeros_like(dv)

    @pl.when((i < compute_steps) & (q < chunks))
    def _():
        for g in range(0, groups, pair):
            rows = slice(g * T, (g + pair) * T)
            some = do[g : g + pair].reshape(pair * T, D)
            slope = ps[0, g : g + pair].reshape(pair * T, CB)
            part = (dot_nt(some, w2[0]) * slope.astype(F32)).astype(BF16)
            dh[rows] = part
            dv[g : g + pair] += dot_nt(part, w1[0]).reshape(pair, T, D)
        part = (LAYERS - 1 - layer) * chunks + q
        base = part * part_rows
        one = dot(vt[...], dh[...])
        dhid[layer, :, pl.ds(pl.multiple_of(q * CB, CB), CB)] = one[D : D + 1]
        two = dot(dot_[...], gs[0].reshape(groups * T, CB))
        for c in range(CB // width):
            cols = slice(c * width, (c + 1) * width)
            weights.acc[weights.rows(base + c * D, D), :] = one[:D, cols].astype(BF16)
            weights.acc[weights.rows(base + (CB // width + c) * D, D), :] = two[:, cols].astype(BF16)

    @pl.when((i < compute_steps) & (q >= chunks))
    def _():
        for j in range(pair):
            g = (q - chunks) * pair + j
            dvg = dv[g]
            u, scale = normal(zs[0, j])
            row_sum = lambda a: jnp.sum(a, axis=0, keepdims=True)
            dvec[layer, 2:3] += row_sum(dvg * u)
            dvec[layer, 3:4] += row_sum(dvg)
            dz = normal_back(dvg, gain2[0], u, scale).astype(BF16)
            yl, ysm = analyse(tl[...], ts[...], dz)
            lr, li = yl[:NL], yl[NL:]
            sr, si = ysm[: PER * NS], ysm[PER * NS :]
            xr, xi = spec[0, j, :NL], spec[0, j, NL : 2 * NL]
            dfl[layer, :NL] += lr * xr + li * xi
            dfl[layer, NL:] += li * xr - lr * xi
            gr, gi = filt_l[0, 0], filt_l[0, 1]
            dl = jnp.concatenate([lr * gr + li * gi, li * gr - lr * gi], axis=0).astype(BF16)
            xr, xi = spec[0, j, 2 * NL : 2 * NL + PER * NS], spec[0, j, 2 * NL + PER * NS :]
            once = lambda a: a[:NS] + a[NS : 2 * NS] + a[2 * NS :]
            dfs[layer, :NS] += once(sr * xr + si * xi)
            dfs[layer, NS:] += once(si * xr - sr * xi)
            gr, gi = thrice(filt_s[0, 0]), thrice(filt_s[0, 1])
            ds = jnp.concatenate([sr * gr + si * gi, si * gr - sr * gi], axis=0).astype(BF16)
            du = synthesise(tlb[...], tsb[...], dl, ds)
            u, scale = normal(xs[0, j])
            dvec[layer, 0:1] += row_sum(du * u)
            dvec[layer, 1:2] += row_sum(du)
            grad = dx[g] + normal_back(du, gain1[0], u, scale)
            dx[g] = grad

            @pl.when(layer == 0)
            def _():
                spread = dot(place[...], grad.astype(BF16)).astype(BF16)
                for m in range(row_count):
                    gslots[m, g] = spread[m * BAND : (m + 1) * BAND]
                for m in range(1, row_count):
                    send_grad(m, g).start()

    @pl.when(i == compute_steps - 1)
    def _():
        small.acc[...] = jnp.zeros_like(small.acc)
        exact = partial(jnp.dot, preferred_element_type=F32, precision=HIGHEST)
        for n in range(LAYERS):
            for c in range(2):
                at = (n * 2 + c) * NL
                small.acc[at : at + NL, :] = (dfl[n, c * NL : (c + 1) * NL] * fold[...]
                                              + exact(mix[...], dfs[n, c * NS : (c + 1) * NS])).astype(BF16)
        at = LAYERS * 2 * NL
        rest = [dvec[n, k : k + 1] for n in range(LAYERS) for k in range(5)]
        rest += [dhid[n, :, c : c + D] for n in range(LAYERS) for c in range(0, FF, D)]
        rest.append(jnp.zeros((-len(rest) % 16, D), F32))
        rest = jnp.concatenate(rest, axis=0).astype(BF16)
        small.acc[at : at + rest.shape[0], :] = rest
        keep_grad().start()

    for k in range(6, -1, -1):
        made = i - k

        @pl.when((made >= 0) & (made < compute_steps) & (made % per < chunks))
        def _():
            weights.stage(made // per * chunks + made % per, k)

        @pl.when(made == compute_steps - 1)
        def _():
            small.stage(0, k)

    @pl.when(i == pl.num_programs(0) - 1)
    def _():
        keep_out().wait()
        keep_grad().wait()
        for m in range(1, row_count):
            @pl.loop(0, groups)
            def _(g):
                send_out(m, g).wait()
                send_grad(m, g).wait()
        for part in range(LAYERS * chunks):
            weights.save(part).wait()
        small.save(0).wait()


def backward(mesh, groups, pair, live, small, tabs, mix, fold, outs, do, saved):
    rows, batch = mesh.shape["rows"], mesh.shape["batch"]
    pick, place, gain1, filt_l, filt_s, gain2, w1, w2 = small
    chunks, pairs = FF // CB, groups // pair
    per, last = chunks + pairs, LAYERS - 1
    steps = LAYERS * per + 6
    layer = lambda i: jnp.maximum(last - i // per, 0)
    when = lambda i: jnp.where(i < LAYERS * per, i % per, per - 1)
    chunk = lambda i: jnp.minimum(when(i), chunks - 1)
    place_of = lambda i: jnp.maximum(when(i) - chunks, 0)
    per_layer = lambda a: pl.BlockSpec((1,) + a.shape[1:], lambda i: (layer(i),) + (0,) * (a.ndim - 1))
    by_pair = lambda a: pl.BlockSpec((1, pair) + a.shape[2:], lambda i: (layer(i), place_of(i), 0, 0))
    by_chunk = lambda a: pl.BlockSpec((1, groups, T, CB), lambda i: (layer(i), 0, 0, chunk(i)))
    gain1, gain2 = gain1[:, None], gain2[:, None]
    xs, zs, spec, vs, gs, ps = saved
    hbm = pl.BlockSpec(memory_space=pl.ANY)
    width = columns(rows, batch)
    part_rows, small_rows = padded(rows, batch, 2 * D * (CB // width)), padded(rows, batch, SMALL)
    dma = pltpu.SemaphoreType.DMA
    return pl.pallas_call(
        partial(backward_kernel, rows, batch, groups, pair),
        grid=(steps,),
        in_specs=[scalars(), whole(pick.shape), whole(place.shape)] + [per_layer(a) for a in (gain1, filt_l, filt_s, gain2)]
        + [pl.BlockSpec((1, D, CB), lambda i: (layer(i), 0, chunk(i))), pl.BlockSpec((1, CB, D), lambda i: (layer(i), chunk(i), 0))]
        + [whole(a.shape) for a in (*tabs, mix, fold)] + [hbm, whole(do.shape)]
        + [by_pair(xs), by_pair(zs), by_pair(spec), per_layer(vs), by_chunk(gs), by_chunk(ps)],
        out_specs=[hbm] * 4,
        out_shape=[jax.ShapeDtypeStruct((rows, groups, BAND, D), BF16)] * 2
        + [jax.ShapeDtypeStruct((LAYERS * chunks * part_rows, width), BF16), jax.ShapeDtypeStruct((small_rows, D), BF16)],
        scratch_shapes=[pltpu.VMEM((groups, T, D), F32), pltpu.VMEM((groups, T, D), F32), pltpu.VMEM((groups, T, D), BF16),
                        pltpu.VMEM((D, groups * T), BF16), pltpu.VMEM((D + 16, groups * T), BF16),
                        pltpu.VMEM((groups * T, CB), BF16), pltpu.VMEM((rows, groups, BAND, D), BF16),
                        pltpu.VMEM((LAYERS, 5, D), F32), pltpu.VMEM((LAYERS, 1, FF), F32),
                        pltpu.VMEM((LAYERS, 2 * NL, D), F32), pltpu.VMEM((LAYERS, 2 * NS, D), F32),
                        dma((2, rows - 1, groups)), dma((2, rows - 1, groups)), dma((2,))]
        + sum_scratch(rows, batch, LAYERS * chunks, part_rows, width) + sum_scratch(rows, batch, 1, small_rows, D),
        compiler_params=pltpu.CompilerParams(collective_id=2, has_side_effects=True, vmem_limit_bytes=VMEM_LIMIT),
        name="backward",
    )(live, pick, place, gain1, filt_l, filt_s, gain2, w1, w2, *tabs, mix, fold, outs, do, xs, zs, spec, vs, gs, ps)


def unpack_kernel(order, outs, grads, weights, small, large_out, small_crops, large_grad, small_grad, dw1, dw2,
                  dfilter, dvec, dhid):
    i = pl.program_id(0)
    for given, large, little in ((outs, large_out, small_crops), (grads, large_grad, small_grad)):
        for g in range(given.shape[1]):
            block = given[0, g].astype(F32)
            for s in range(BL):
                large[g, 0, s] = block[s * WL : (s + 1) * WL]
            for p in range(PER):
                for s in range(BS):
                    at = BL * WL + (p * BS + s) * WS
                    little[g * PER + p, 0, s] = block[at : at + WS]
    width = weights.shape[1]
    parts = CB // width
    for c in range(parts):
        cols = slice(c * width, (c + 1) * width)
        dw1[0, :, cols] = weights[c * D : (c + 1) * D, :].astype(F32)
        dw2[0, cols, :] = weights[(parts + c) * D : (parts + c + 1) * D, :].astype(F32).T

    @pl.when(i == 0)
    def _():
        at = LAYERS * 2 * NL
        for n in range(LAYERS):
            for c in range(2):
                dfilter[n, c] = small[(n * 2 + c) * NL : (n * 2 + c + 1) * NL].astype(F32)
        rest = small[at : at + 32].astype(F32)
        for n in range(LAYERS):
            for k in range(5):
                dvec[k, n : n + 1] = rest[n * 5 + k : n * 5 + k + 1]
            for c in range(FF // D):
                r = LAYERS * 5 + n * (FF // D) + c
                dhid[n : n + 1, c * D : (c + 1) * D] = rest[r : r + 1]


def unpack(mesh, groups, outs, grads, weights, small):
    rows = mesh.shape["rows"]
    me = lax.axis_index("rows")
    crops = rows * groups
    chunks = FF // CB
    parts = LAYERS * chunks
    steps = max(rows, parts)
    order = (jnp.arange(rows, dtype=jnp.int32) - me) % rows
    dev = lambda i: jnp.minimum(i, rows - 1)
    part = lambda i: jnp.minimum(i, parts - 1)
    part_rows = weights.shape[0] // parts
    given = pl.BlockSpec((1, groups, BAND, D), lambda i, order: (order[dev(i)], 0, 0, 0))
    large = pl.BlockSpec((groups, 1, BL, WL, D), lambda i, order: (dev(i), 0, 0, 0, 0))
    little = pl.BlockSpec((groups * PER, 1, BS, WS, D), lambda i, order: (dev(i), 0, 0, 0, 0))
    every = lambda shape: pl.BlockSpec(shape, lambda i, order: (0,) * len(shape))
    large_shape = jax.ShapeDtypeStruct((crops, 1, BL, WL, D), F32)
    little_shape = jax.ShapeDtypeStruct((crops * PER, 1, BS, WS, D), F32)
    shapes = [(LAYERS, 2, NL, D), (5, LAYERS, D), (LAYERS, FF)]
    return pl.pallas_call(
        unpack_kernel,
        grid_spec=pltpu.PrefetchScalarGridSpec(
            num_scalar_prefetch=1, grid=(steps,),
            in_specs=[given, given, pl.BlockSpec((part_rows, weights.shape[1]), lambda i, order: (part(i), 0)), every(small.shape)],
            out_specs=[large, little, large, little,
                       pl.BlockSpec((1, D, CB), lambda i, order: (LAYERS - 1 - part(i) // chunks, 0, part(i) % chunks)),
                       pl.BlockSpec((1, CB, D), lambda i, order: (LAYERS - 1 - part(i) // chunks, part(i) % chunks, 0))]
            + [every(s) for s in shapes]),
        out_shape=[large_shape, little_shape, large_shape, little_shape,
                   jax.ShapeDtypeStruct((LAYERS, D, FF), F32), jax.ShapeDtypeStruct((LAYERS, FF, D), F32)]
        + [jax.ShapeDtypeStruct(s, F32) for s in shapes],
        compiler_params=pltpu.CompilerParams(vmem_limit_bytes=VMEM_LIMIT),
        name="unpack",
    )(order, outs, grads, weights, small)


def token_columns(rows, band_bounds, me):
    t = np.arange(T)
    small = t >= TL
    at = np.where(small, (t - TL) % TS, t)
    wide = np.where(small, WS, WL)
    r, w = jnp.asarray(at // wide, jnp.int32), at % wide
    crop = np.where(small, (t - TL) // TS, 0)
    start = jnp.asarray(np.where(small, BL * WL + crop * BS * WS + w, w), jnp.int32)
    band = (me - jnp.arange(rows, dtype=jnp.int32)) % rows
    first, end = jnp.where(small[:, None], band_bounds[1][band], band_bounds[0][band]), jnp.where(
        small[:, None], band_bounds[1][band + 1], band_bounds[0][band + 1])
    inside = (r[:, None] >= first) & (r[:, None] < end)
    column = start[:, None] + (r[:, None] - first) * jnp.asarray(wide, jnp.int32)[:, None]
    return jnp.where(inside, column, -1)


def local(mesh, large_in, small_in, large_cot, small_cot, crop_counts, band_bounds, row_interp, col_interp,
          norm1_gain, norm1_bias, filters, norm2_gain, norm2_bias, fc1_weight, fc1_bias, fc2_weight, fc2_bias):
    rows = mesh.shape["rows"]
    me = lax.axis_index("rows")
    crops = large_in.shape[0]
    groups = crops // rows
    pair = 2 if groups % 2 == 0 else 1
    tabs = tables()
    column = token_columns(rows, band_bounds, me)
    pick = (column[:, :, None] == jnp.arange(BAND, dtype=jnp.int32)).astype(BF16).reshape(T, rows * BAND)
    place = (column.T[:, None, :] == jnp.arange(BAND, dtype=jnp.int32)[None, :, None]).astype(BF16).reshape(rows * BAND, T)
    at = me * groups + jnp.arange(groups, dtype=jnp.int32)
    live = jnp.concatenate([(at < crop_counts[0, 0])[:, None],
                            (at[:, None] * PER + jnp.arange(PER, dtype=jnp.int32)) < crop_counts[0, 1]], axis=1)
    live = live.astype(F32)

    def pack(large, small):
        return jnp.concatenate([large.reshape(crops, BL * WL, D), small.reshape(crops, PER * BS * WS, D),
                                jnp.zeros((crops, BAND - BL * WL - PER * BS * WS, D), large.dtype)], axis=1)

    small_filter = jnp.einsum("ka,ncabd,lb->nckld", row_interp, filters, col_interp, precision=HIGHEST)
    fold_l = np.where((np.arange(FL) == 0) | (2 * np.arange(FL) == WL), 1.0, 2.0).astype(np.float32)
    fold_s = np.where((np.arange(FS) == 0) | (2 * np.arange(FS) == WS), 1.0, 2.0).astype(np.float32)
    filt_l = (filters * fold_l[:, None]).reshape(LAYERS, 2, NL, D)
    filt_s = (small_filter * fold_s[:, None]).reshape(LAYERS, 2, NS, D)
    mix = jnp.einsum("ka,lb->abkl", row_interp, col_interp * fold_s[:, None]).reshape(NL, NS)
    fold = jnp.asarray(np.tile(fold_l, HL)[:, None])

    outs, *saved, do = forward(mesh, groups, pair, pack(large_in, small_in), pack(large_cot, small_cot), live,
                               (pick, place, norm1_gain, norm1_bias, filt_l, filt_s, norm2_gain, norm2_bias,
                                fc1_weight, fc1_bias, fc2_weight, fc2_bias, *tabs))
    outs, grads, weights, small = backward(
        mesh, groups, pair, live, (pick, place, norm1_gain, filt_l, filt_s, norm2_gain, fc1_weight, fc2_weight), tabs,
        mix, fold, outs, do, saved)
    large_out, small_out, large_grad, small_grad, dw1, dw2, dfilter, dvec, dhid = unpack(
        mesh, groups, outs, grads, weights, small)
    return (large_out, small_out, large_grad, small_grad, dvec[0], dvec[1], dfilter.reshape(filters.shape), dvec[2], dvec[3],
            dw1, dhid, dw2, dvec[4])


def solution(mesh):
    split = P("batch", "rows", None, None, None)
    return jax.shard_map(partial(local, mesh), mesh=mesh, in_specs=(split,) * 4 + (P("batch", None),) + (P(),) * 12,
                         out_specs=(split,) * 4 + (P(),) * 9, check_vma=False)
```

```python
import math
from functools import partial
import numpy as np
import jax
import jax.numpy as jnp
from jax import lax
from jax.experimental import pallas as pl
from jax.experimental.pallas import tpu as pltpu
from jax.sharding import PartitionSpec as P

D, FF = 384, 1536
HL, WL, FL = 14, 14, 8
HS, WS, FS = 6, 6, 4
BL, BS = 4, 2
LAYERS = 2
EPS = 1e-6
TL, TS = HL * WL, HS * WS
PER = 3
T = TL + PER * TS
CUT, END = 192, 208
NL, NS = HL * FL, HS * FS
BAND = 96
CH = 512
CB = 512
SMALL = 512
PLAN = {
    (0, 0): [(-3, 0)],
    (0, 9): [(0, 0), (-3, 1)],
    (1, 2): [(0, 1), (-3, 2)],
    (1, 9): [(1, 0)],
    (2, 0): [(-3, 3)],
    (2, 2): [(1, 1)],
    (2, 9): [(0, 2), (2, 0)],
    (3, 0): [(-3, 4)],
    (3, 2): [(2, 1)],
    (3, 9): [(-3, 5)],
    (4, 0): [(1, 2)],
    (4, 9): [(0, 3)],
    (5, 1): [(2, 2)],
    (6, 1): [(1, 3)],
    (6, 9): [(0, 4), (3, 0)],
    (7, 2): [(2, 3), (3, 1)],
    (7, 9): [(4, 0)],
    (8, 0): [(1, 4), (0, 5)],
    (8, 1): [(4, 1)],
    (8, 9): [(0, 6), (3, 2), (5, 0)],
    (9, 0): [(2, 4)],
    (9, 1): [(1, 5), (5, 1), (-2, 0)],
    (10, 0): [(1, 6), (4, 2)],
    (10, 1): [(-2, 1)],
    (10, 9): [(3, 3)],
    (11, 0): [(2, 5)],
    (11, 2): [(-2, 2)],
    (11, 9): [(2, 6), (5, 2), (-1, 0), (4, 3), (-1, 1), (3, 4), (-1, 2), (-2, 3), (5, 3), (3, 5), (4, 4), (-2, 4), (3, 6), (-1, 3), (5, 4), (-2, 5), (4, 5), (4, 6), (-1, 4), (5, 5), (5, 6), (-1, 5), (-1, 6)],
}
MESH = pl.DeviceIdType.MESH
VMEM_LIMIT = 60 * 2**20
F32, BF16 = jnp.float32, jnp.bfloat16
HIGHEST = lax.Precision.HIGHEST


def table(height, width, count):
    k = np.arange(height)[:, None, None, None]
    l = np.arange(count)[None, :, None, None]
    s = np.arange(height)[None, None, :, None]
    w = np.arange(width)[None, None, None, :]
    phase = (k * s * width + l * w * height) % (height * width)
    angle = phase.astype(np.float32) * np.float32(2.0 * math.pi / (height * width))
    scale = np.float32(1.0 / math.sqrt(height * width))
    both = np.stack([np.cos(angle) * scale, -np.sin(angle) * scale])
    return both.reshape(2, height * count, height * width).astype(jnp.bfloat16).astype(np.float32)


def tables():
    large = np.zeros((2 * NL, END), np.float32)
    large[:, :TL] = table(HL, WL, FL).reshape(2 * NL, TL)
    one = table(HS, WS, FS)
    small = np.zeros((2, PER, NS, T - CUT), np.float32)
    for at in range(PER):
        small[:, at, :, TL - CUT + at * TS : TL - CUT + (at + 1) * TS] = one
    small = small.reshape(2 * PER * NS, T - CUT)
    return [jnp.asarray(t, BF16) for t in (large, small, large.T, small.T)]


def normal(x):
    mean = jnp.mean(x, axis=-1, keepdims=True)
    centred = x - mean
    scale = lax.rsqrt(jnp.mean(centred * centred, axis=-1, keepdims=True) + EPS)
    return centred * scale, scale


def normal_back(grad, gain, unit, scale):
    inner = grad * gain
    first = jnp.mean(inner, axis=-1, keepdims=True)
    second = jnp.mean(inner * unit, axis=-1, keepdims=True)
    return (inner - first - unit * second) * scale


def dot(a, b):
    return jnp.dot(a, b, preferred_element_type=F32)


def dot_nt(a, b):
    return lax.dot_general(a, b, (((1,), (1,)), ((), ())), preferred_element_type=F32)


def dot_tn(a, b):
    return lax.dot_general(a, b, (((0,), (0,)), ((), ())), preferred_element_type=F32)


def analyse(large_table, small_table, values):
    return dot(large_table, values[:END]), dot(small_table, values[CUT:])


def synthesise(large_back, small_back, large, small):
    a, b = dot(large_back, large), dot(small_back, small)
    return jnp.concatenate([a[:CUT], a[CUT:] + b[: END - CUT], b[END - CUT :]], axis=0)


def thrice(x):
    return jnp.concatenate([x] * PER, axis=0)


def gelu_both(h):
    cdf = 0.5 + 0.5 * lax.erf(h * np.float32(math.sqrt(0.5)))
    dens = jnp.exp(h * h * np.float32(-0.5)) * np.float32(1 / math.sqrt(2 * math.pi))
    return h * cdf, cdf + h * dens


def live_rows(counts, group):
    t = lax.broadcasted_iota(jnp.int32, (T, 1), 0)
    place, limit = jnp.full((T, 1), group), jnp.where(t < TL, counts[0, 0], counts[0, 1])
    for at in range(PER):
        place = jnp.where(t >= TL + at * TS, group * PER + at, place)
    return jnp.where(place < limit, 1.0, 0.0)


def whole(shape):
    return pl.BlockSpec(shape, lambda *a: (0,) * len(shape))


def scalars():
    return pl.BlockSpec(memory_space=pltpu.SMEM)


def forward_kernel(row_count, groups, pair, packed_in, packed_cot, counts, bounds, filters, gain1, bias1, gain2, bias2,
                   w1, b1, w2, b2, tl, ts, tlb, tsb, need, slot, row_interp, col_interp, row_s, row_l, col_s, col_l, fold,
                   outs, xs, zs, spec, vs, gs, ps, do, place, filt_l, filt_s, mix,
                   pick, slots, own_sem, send_sem, recv_sem):
    step = pl.program_id(0)
    batch, row = lax.axis_index("batch"), lax.axis_index("rows")
    last = groups // pair - 1

    def remote(which, m, g):
        to = lax.rem(row + m, row_count)
        given = (packed_in, packed_cot)[which]
        return pltpu.make_async_remote_copy(
            src_ref=given.at[to * groups + g], dst_ref=slots.at[which, m, g],
            send_sem=send_sem.at[which, m - 1, g], recv_sem=recv_sem.at[which, m - 1, g],
            device_id=(batch, to), device_id_type=MESH)

    def mine(which, g):
        given = (packed_in, packed_cot)[which]
        return pltpu.make_async_copy(given.at[row * groups + g], slots.at[which, 0, g], own_sem.at[which, g])

    @pl.when(step == 0)
    def _():
        barrier = pltpu.get_barrier_semaphore()
        for m in range(1, row_count):
            pl.semaphore_signal(barrier, inc=1, device_id=(batch, lax.rem(row + m, row_count)), device_id_type=MESH)
        for which in range(2):
            @pl.loop(0, groups)
            def _(g):
                mine(which, g).start()
        pl.semaphore_wait(barrier, row_count - 1)
        for which in range(2):
            @pl.loop(0, groups)
            def _(g):
                for m in range(1, row_count):
                    remote(which, m, g).start()
        for m in range(row_count):
            band = lax.rem(row + (row_count - m), row_count)
            large = lax.broadcasted_iota(jnp.int32, (T, BAND), 0) < TL
            first = jnp.where(large, bounds[0, band], bounds[1, band])
            size = jnp.where(large, bounds[0, band + 1], bounds[1, band + 1]) - first
            hit = (need[...] == first) & (slot[...] < size)
            hit = jnp.where(hit, 1.0, 0.0)
            pick[:, m * BAND : (m + 1) * BAND] = hit.astype(BF16)
            place[m * BAND : (m + 1) * BAND, :] = hit.T.astype(BF16)
        exact = partial(jnp.dot, preferred_element_type=F32, precision=HIGHEST)
        both = exact(exact(row_s[...], row_interp[...]), row_l[...]) * exact(exact(col_s[...], col_interp[...]), col_l[...])
        mix[...] = both
        for n in range(LAYERS):
            for c in range(2):
                filt_l[n, c] = filters[n, c] * fold[...]
                filt_s[n, c] = exact(both, filters[n, c])

    def live(g):
        return live_rows(counts, row * groups + g)

    def take(which, g):
        mine(which, g).wait()
        for m in range(1, row_count):
            remote(which, m, g).wait_recv()
        return dot(pick[...], jnp.concatenate([slots[which, m, g] for m in range(row_count)], axis=0))

    x = [take(0, step * pair + j) for j in range(pair)]
    for n in range(LAYERS):
        v = []
        for j in range(pair):
            xs[n, j] = x[j]
            u, _ = normal(x[j])
            u = (u * gain1[n : n + 1] + bias1[n : n + 1]).astype(BF16)
            xl, xsm = analyse(tl[...], ts[...], u)
            spec[n, j, : 2 * NL] = xl
            spec[n, j, 2 * NL :] = xsm
            lr, li = xl[:NL], xl[NL:]
            sr, si = xsm[: PER * NS], xsm[PER * NS :]
            gr, gi = filt_l[n, 0], filt_l[n, 1]
            yl = jnp.concatenate([lr * gr - li * gi, lr * gi + li * gr], axis=0).astype(BF16)
            gr, gi = thrice(filt_s[n, 0]), thrice(filt_s[n, 1])
            ys = jnp.concatenate([sr * gr - si * gi, sr * gi + si * gr], axis=0).astype(BF16)
            z = synthesise(tlb[...], tsb[...], yl, ys)
            zs[n, j] = z
            q, _ = normal(z)
            q = (q * gain2[n : n + 1] + bias2[n : n + 1]).astype(BF16)
            vs[n, j] = q
            v.append(q)
        v = jnp.concatenate(v, axis=0)
        total = jnp.concatenate(x, axis=0) + b2[n : n + 1]
        for c in range(0, FF, CH):
            h = dot(v, w1[n, :, c : c + CH]) + b1[n : n + 1, c : c + CH]
            g, slope = gelu_both(h)
            g = g.astype(BF16)
            slope = slope.astype(BF16)
            for j in range(pair):
                gs[n, j, :, c : c + CH] = g[j * T : (j + 1) * T]
                ps[n, j, :, c : c + CH] = slope[j * T : (j + 1) * T]
            total = total + dot(g, w2[n, c : c + CH, :])
        x = [total[j * T : (j + 1) * T] for j in range(pair)]
    for j in range(pair):
        spread = dot(place[...], (x[j] * live(step * pair + j)).astype(BF16)).astype(BF16)
        for m in range(row_count):
            outs[m, j] = spread[m * BAND : (m + 1) * BAND]

    @pl.when(step == last)
    def _():
        for g in range(groups):
            do[g] = (take(1, g) * live(g)).astype(BF16)
        for which in range(2):
            @pl.loop(0, groups)
            def _(g):
                for m in range(1, row_count):
                    remote(which, m, g).wait_send()


def forward(mesh, groups, pair, packed_in, packed_cot, counts, bounds, small):
    rows = mesh.shape["rows"]
    sizes = [(T, D, F32), (T, D, F32), (2 * NL + 2 * PER * NS, D, F32), (T, D, BF16), (T, FF, BF16), (T, FF, BF16)]
    extra = [((groups, T, D), BF16), ((rows * BAND, T), BF16), ((LAYERS, 2, NL, D), F32), ((LAYERS, 2, NS, D), F32), ((NS, NL), F32)]
    hbm = pl.BlockSpec(memory_space=pl.ANY)
    return pl.pallas_call(
        partial(forward_kernel, rows, groups, pair),
        grid=(groups // pair,),
        in_specs=[hbm, hbm, scalars(), scalars()] + [whole(a.shape) for a in small],
        out_specs=[pl.BlockSpec((rows, pair, BAND, D), lambda i: (0, i, 0, 0))]
        + [pl.BlockSpec((LAYERS, pair, a, b), lambda i: (0, i, 0, 0)) for a, b, _ in sizes]
        + [whole(a) for a, _ in extra],
        out_shape=[jax.ShapeDtypeStruct((rows, groups, BAND, D), BF16)]
        + [jax.ShapeDtypeStruct((LAYERS, groups, a, b), t) for a, b, t in sizes]
        + [jax.ShapeDtypeStruct(a, t) for a, t in extra],
        scratch_shapes=[pltpu.VMEM((T, rows * BAND), BF16), pltpu.VMEM((2, rows, groups, BAND, D), BF16), pltpu.SemaphoreType.DMA((2, groups)),
                        pltpu.SemaphoreType.DMA((2, rows - 1, groups)), pltpu.SemaphoreType.DMA((2, rows - 1, groups))],
        compiler_params=pltpu.CompilerParams(collective_id=1, has_side_effects=True, vmem_limit_bytes=VMEM_LIMIT),
        name="forward",
    )(packed_in, packed_cot, counts, bounds, *small)


SPREAD = True
LOW = 2


def add_rows(target, at_target, base, sources, count):
    step = next(s for s in (128, 96, 64, 48, 32, 16) if count % s == 0)

    @pl.loop(0, count // step)
    def _(i):
        at = pl.multiple_of(i * step, 16)
        rows = pl.ds(pl.multiple_of(base + at, 16), step)
        total = at_target[rows, :].astype(F32)
        for ref in sources:
            total = total + ref[pl.ds(at, step), :].astype(F32)
        target[rows, :] = total.astype(BF16)


class Sum:
    def __init__(self, mesh_rows, mesh_batch, acc, full, out, count, bufs, sems, save_sem):
        batch, row = lax.axis_index("batch"), lax.axis_index("rows")
        self.acc, self.full, self.out, self.count, self.bufs, self.sems, self.save_sem = acc, full, out, count, bufs, sems, save_sem
        self.size = kinds(mesh_rows, mesh_batch)
        self.levels = len(self.size)
        x_n = mesh_rows // 2
        core, x, z, y = lax.rem(row, 2), lax.div(row, 2), lax.div(batch, LOW), lax.rem(batch, LOW)
        self.me = [core, y, z * x_n + x] if SPREAD else [core, y, x, z]
        self.others, self.offsets, self.counts = [], [0], [count]
        for level, n in enumerate(self.size):
            count //= n
            self.counts.append(count)
            self.offsets.append(self.offsets[-1] + self.me[level] * count)
            found = []
            for step in range(1, n):
                at = lax.rem(self.me[level] + step, n)
                device = [(batch, x * 2 + at), (z * LOW + at, row)]
                device += [(lax.div(at, x_n) * LOW + y, lax.rem(at, x_n) * 2 + core)] if SPREAD else [
                    (batch, at * 2 + core), (at * LOW + y, row)]
                found.append((device[level], at))
            self.others.append(found)

    def region(self, part, level):
        return part * self.count + self.offsets[level], self.counts[level]

    def rows(self, base, count):
        return pl.ds(pl.multiple_of(base, 16), count)

    def down(self, part, level, step):
        base, count = self.region(part, level)
        device, at = self.others[level][step - 1]
        chunk = count // self.size[level]
        return pltpu.make_async_remote_copy(
            src_ref=self.acc.at[self.rows(base + at * chunk, chunk)], dst_ref=self.bufs[level].at[part, self.rows((step - 1) * chunk, chunk)],
            send_sem=self.sems[level].at[0, part], recv_sem=self.sems[level].at[1, part],
            device_id=device, device_id_type=MESH)

    def up(self, part, level, step):
        base, count = self.region(part, level + 1)
        rows = self.rows(base, count)
        return pltpu.make_async_remote_copy(
            src_ref=self.full.at[rows], dst_ref=self.full.at[rows],
            send_sem=self.sems[level].at[2, part], recv_sem=self.sems[level].at[3, part],
            device_id=self.others[level][step - 1][0], device_id_type=MESH)

    def arrived(self, part, level, sem):
        every = self.bufs[level].at[part]
        pltpu.make_async_copy(every, every, self.sems[level].at[sem, part]).wait()

    def save(self, part):
        rows = self.rows(part * self.count, self.count)
        return pltpu.make_async_copy(self.full.at[rows], self.out.at[rows], self.save_sem.at[part])

    def stage(self, part, k):
        top = self.levels
        if 1 <= k <= top:
            level = k - 1
            self.arrived(part, level, 0)
            self.arrived(part, level, 1)
            base, count = self.region(part, level + 1)
            add_rows(self.full if k == top else self.acc, self.acc, base,
                     [self.bufs[level].at[part, self.rows(s * count, count)] for s in range(self.size[level] - 1)], count)
        if k < top:
            for step in range(1, self.size[k]):
                self.down(part, k, step).start()
        if k > top:
            level = 2 * top - k
            self.arrived(part, level, 2)
            self.arrived(part, level, 3)
        if top <= k < 2 * top:
            for step in range(1, self.size[2 * top - 1 - k]):
                self.up(part, 2 * top - 1 - k, step).start()
        if k == 2 * top:
            self.save(part).start()


def kinds(mesh_rows, mesh_batch):
    x_n, z_n = mesh_rows // 2, mesh_batch // LOW
    return [2, LOW, x_n * z_n] if SPREAD else [2, LOW, x_n, z_n]


def columns(mesh_rows, mesh_batch):
    sizes = {w: w * padded(mesh_rows, mesh_batch, 2 * D * (CB // w)) for w in (256, 128)}
    return min(sizes, key=sizes.get)


def padded(mesh_rows, mesh_batch, count):
    unit = 16 * math.prod(kinds(mesh_rows, mesh_batch))
    return -(-count // unit) * unit


def sum_scratch(mesh_rows, mesh_batch, parts, count, width):
    size = kinds(mesh_rows, mesh_batch)
    shapes = [pltpu.VMEM((parts * count, width), BF16)] * 2
    for n in size:
        count //= n
        shapes.append(pltpu.VMEM((parts, (n - 1) * count, width), BF16))
    return shapes + [pltpu.SemaphoreType.DMA((4, parts)) for n in size] + [pltpu.SemaphoreType.DMA((parts,))]


def backward_kernel(row_count, batch_count, groups, pair, place, filt_l, filt_s, gain1, gain2, w1, w2, tl, ts, tlb, tsb,
                    mix, fold, outs, do_in, xs, zs, spec, vs, gs, ps,
                    out_land, grad_land, weights_out, small_out,
                    dx, dv, do, dot_, vt, dh, gslots, dvec, dhid, dfl, dfs, out_sem, grad_sem, own_sem, *sums):
    i = pl.program_id(0)
    batch, row = lax.axis_index("batch"), lax.axis_index("rows")
    chunks, pairs = FF // CB, groups // pair
    per = chunks + pairs
    compute_steps = LAYERS * per
    layer, q = LAYERS - 1 - i // per, i % per
    width = columns(row_count, batch_count)
    part_rows = padded(row_count, batch_count, 2 * D * (CB // width))
    small_rows = padded(row_count, batch_count, SMALL)
    sums_of = []
    for out, count in ((weights_out, part_rows), (small_out, small_rows)):
        n = len(kinds(row_count, batch_count))
        sums_of.append(Sum(row_count, batch_count, sums[0], sums[1], out, count, sums[2 : 2 + n], sums[2 + n : 2 + 2 * n], sums[2 + 2 * n]))
        sums = sums[3 + 2 * n :]
    weights, small = sums_of

    def send_out(m, g):
        return pltpu.make_async_remote_copy(
            src_ref=outs.at[m, g], dst_ref=out_land.at[m, g], send_sem=out_sem.at[0, m - 1, g], recv_sem=out_sem.at[1, m - 1, g],
            device_id=(batch, lax.rem(row + (row_count - m), row_count)), device_id_type=MESH)

    def send_grad(m, g):
        return pltpu.make_async_remote_copy(
            src_ref=gslots.at[m, g], dst_ref=grad_land.at[m, g], send_sem=grad_sem.at[0, m - 1, g], recv_sem=grad_sem.at[1, m - 1, g],
            device_id=(batch, lax.rem(row + (row_count - m), row_count)), device_id_type=MESH)

    def keep_out():
        return pltpu.make_async_copy(outs.at[0], out_land.at[0], own_sem.at[0])

    def keep_grad():
        return pltpu.make_async_copy(gslots.at[0], grad_land.at[0], own_sem.at[1])

    plan = {key: [a for a in PLAN[key] if a[0] != -2 or groups == 6] for key in PLAN}
    if groups != 6:
        plan[compute_steps - 1, 9] = [(-2, g) for g in range(groups)] + plan[compute_steps - 1, 9]
    left = set(plan)

    def do_now(part, k):
        if part >= 0:
            weights.stage(part, k)
        elif part == -1:
            small.stage(0, k)
        elif k < groups:
            for m in range(1, row_count):
                (send_grad if part == -2 else send_out)(m, k).start()

    def advance(place, steps):
        for at in steps:
            found = sorted(key for key in left if key[0] == at and (key[1] == place or place == 9))
            if found:
                @pl.when(i == at)
                def _():
                    for key in found:
                        left.discard(key)
                        for part, k in plan[key]:
                            do_now(part, k)

    first_steps = [at for at in range(compute_steps) if at % per < chunks]
    second_steps = [at for at in range(compute_steps) if at % per >= chunks]

    @pl.when(i == 0)
    def _():
        barrier = pltpu.get_barrier_semaphore()
        greeted = 0
        for m in range(1, row_count):
            pl.semaphore_signal(barrier, inc=1, device_id=(batch, lax.rem(row + m, row_count)), device_id_type=MESH)
            greeted += 1
        for level in range(1, weights.levels):
            for step in range(1, weights.size[level]):
                pl.semaphore_signal(barrier, inc=1, device_id=weights.others[level][step - 1][0], device_id_type=MESH)
                greeted += 1
        keep_out().start()
        if part_rows > 2 * D * (CB // width):
            weights.acc[...] = jnp.zeros_like(weights.acc)
        for g in range(groups):
            dx[g] = do_in[g].astype(F32)
        for ref in (dvec, dfl, dfs):
            ref[...] = jnp.zeros_like(ref)
        pl.semaphore_wait(barrier, greeted)

    @pl.when((i < compute_steps) & (q == 0))
    def _():
        for g in range(groups):
            rows = pl.ds(g * T, T)
            low = dx[g].astype(BF16)
            do[g] = low
            dvec[layer, 4:5] += jnp.sum(low.astype(F32), axis=0, keepdims=True)
        dot_[...] = do[...].reshape(groups * T, D).T
        vt[:D] = vs[0].reshape(groups * T, D).T
        vt[D:] = jnp.ones((16, groups * T), BF16)
        dv[...] = jnp.zeros_like(dv)

    @pl.when((i < compute_steps) & (q < chunks))
    def _():
        for g in range(0, groups, pair):
            rows = slice(g * T, (g + pair) * T)
            some = do[g : g + pair].reshape(pair * T, D)
            slope = ps[0, g : g + pair].reshape(pair * T, CB)
            part = (dot_nt(some, w2[0]) * slope.astype(F32)).astype(BF16)
            dh[rows] = part
            dv[g : g + pair] += dot_nt(part, w1[0]).reshape(pair, T, D)
            advance(g // pair, first_steps)
        part = (LAYERS - 1 - layer) * chunks + q
        base = part * part_rows
        one = dot(vt[...], dh[...])
        dhid[layer, :, pl.ds(pl.multiple_of(q * CB, CB), CB)] = one[D : D + 1]
        two = dot(dot_[...], gs[0].reshape(groups * T, CB))
        for c in range(CB // width):
            cols = slice(c * width, (c + 1) * width)
            weights.acc[weights.rows(base + c * D, D), :] = one[:D, cols].astype(BF16)
            weights.acc[weights.rows(base + (CB // width + c) * D, D), :] = two[:, cols].astype(BF16)

    @pl.when((i < compute_steps) & (q >= chunks))
    def _():
        for j in range(pair):
            if j:
                advance(2 * j - 1, second_steps)
            g = (q - chunks) * pair + j
            dvg = dv[g]
            u, scale = normal(zs[0, j])
            row_sum = lambda a: jnp.sum(a, axis=0, keepdims=True)
            dvec[layer, 2:3] += row_sum(dvg * u)
            dvec[layer, 3:4] += row_sum(dvg)
            dz = normal_back(dvg, gain2[pl.ds(layer, 1)], u, scale).astype(BF16)
            yl, ysm = analyse(tl[...], ts[...], dz)
            lr, li = yl[:NL], yl[NL:]
            sr, si = ysm[: PER * NS], ysm[PER * NS :]
            xr, xi = spec[0, j, :NL], spec[0, j, NL : 2 * NL]
            dfl[layer, :NL] += lr * xr + li * xi
            dfl[layer, NL:] += li * xr - lr * xi
            advance(2 * j, second_steps)
            gr, gi = filt_l[0, 0], filt_l[0, 1]
            dl = jnp.concatenate([lr * gr + li * gi, li * gr - lr * gi], axis=0).astype(BF16)
            xr, xi = spec[0, j, 2 * NL : 2 * NL + PER * NS], spec[0, j, 2 * NL + PER * NS :]
            once = lambda a: a[:NS] + a[NS : 2 * NS] + a[2 * NS :]
            dfs[layer, :NS] += once(sr * xr + si * xi)
            dfs[layer, NS:] += once(si * xr - sr * xi)
            gr, gi = thrice(filt_s[0, 0]), thrice(filt_s[0, 1])
            ds = jnp.concatenate([sr * gr + si * gi, si * gr - sr * gi], axis=0).astype(BF16)
            du = synthesise(tlb[...], tsb[...], dl, ds)
            u, scale = normal(xs[0, j])
            dvec[layer, 0:1] += row_sum(du * u)
            dvec[layer, 1:2] += row_sum(du)
            grad = dx[g] + normal_back(du, gain1[pl.ds(layer, 1)], u, scale)
            dx[g] = grad

            @pl.when(layer == 0)
            def _():
                spread = dot(place[...], grad.astype(BF16)).astype(BF16)
                for m in range(row_count):
                    gslots[m, g] = spread[m * BAND : (m + 1) * BAND]

    @pl.when(i == compute_steps - 1)
    def _():
        small.acc[...] = jnp.zeros_like(small.acc)
        exact = partial(jnp.dot, preferred_element_type=F32, precision=HIGHEST)
        mix_t = mix[...].T
        for n in range(LAYERS):
            for c in range(2):
                at = (n * 2 + c) * NL
                small.acc[at : at + NL, :] = (dfl[n, c * NL : (c + 1) * NL] * fold[...]
                                              + exact(mix_t, dfs[n, c * NS : (c + 1) * NS])).astype(BF16)
        at = LAYERS * 2 * NL
        rest = [dvec[n, k : k + 1] for n in range(LAYERS) for k in range(5)]
        rest += [dhid[n, :, c : c + D] for n in range(LAYERS) for c in range(0, FF, D)]
        rest.append(jnp.zeros((-len(rest) % 16, D), F32))
        rest = jnp.concatenate(rest, axis=0).astype(BF16)
        small.acc[at : at + rest.shape[0], :] = rest
        keep_grad().start()

    advance(9, range(compute_steps))

    @pl.when(i == pl.num_programs(0) - 1)
    def _():
        keep_out().wait()
        keep_grad().wait()
        for m in range(1, row_count):
            @pl.loop(0, groups)
            def _(g):
                send_out(m, g).wait()
                send_grad(m, g).wait()
        for part in range(LAYERS * chunks):
            weights.save(part).wait()
        small.save(0).wait()


def backward(mesh, groups, pair, small, tabs, mix, fold, outs, do, saved):
    rows, batch = mesh.shape["rows"], mesh.shape["batch"]
    place, filt_l, filt_s, gain1, gain2, w1, w2 = small
    chunks, pairs = FF // CB, groups // pair
    per, last = chunks + pairs, LAYERS - 1
    steps = LAYERS * per
    layer = lambda i: jnp.maximum(last - i // per, 0)
    when = lambda i: jnp.where(i < LAYERS * per, i % per, per - 1)
    chunk = lambda i: jnp.minimum(when(i), chunks - 1)
    place_of = lambda i: jnp.maximum(when(i) - chunks, 0)
    per_layer = lambda a: pl.BlockSpec((1,) + a.shape[1:], lambda i: (layer(i),) + (0,) * (a.ndim - 1))
    by_pair = lambda a: pl.BlockSpec((1, pair) + a.shape[2:], lambda i: (layer(i), place_of(i), 0, 0))
    by_chunk = lambda a: pl.BlockSpec((1, groups, T, CB), lambda i: (layer(i), 0, 0, chunk(i)))
    xs, zs, spec, vs, gs, ps = saved
    hbm = pl.BlockSpec(memory_space=pl.ANY)
    width = columns(rows, batch)
    part_rows, small_rows = padded(rows, batch, 2 * D * (CB // width)), padded(rows, batch, SMALL)
    dma = pltpu.SemaphoreType.DMA
    return pl.pallas_call(
        partial(backward_kernel, rows, batch, groups, pair),
        grid=(steps,),
        in_specs=[whole(place.shape), per_layer(filt_l), per_layer(filt_s), whole(gain1.shape), whole(gain2.shape)]
        + [pl.BlockSpec((1, D, CB), lambda i: (layer(i), 0, chunk(i))), pl.BlockSpec((1, CB, D), lambda i: (layer(i), chunk(i), 0))]
        + [whole(a.shape) for a in (*tabs, mix, fold)] + [hbm, whole(do.shape)]
        + [by_pair(xs), by_pair(zs), by_pair(spec), per_layer(vs), by_chunk(gs), by_chunk(ps)],
        out_specs=[hbm] * 4,
        out_shape=[jax.ShapeDtypeStruct((rows, groups, BAND, D), BF16)] * 2
        + [jax.ShapeDtypeStruct((LAYERS * chunks * part_rows, width), BF16), jax.ShapeDtypeStruct((small_rows, D), BF16)],
        scratch_shapes=[pltpu.VMEM((groups, T, D), F32), pltpu.VMEM((groups, T, D), F32), pltpu.VMEM((groups, T, D), BF16),
                        pltpu.VMEM((D, groups * T), BF16), pltpu.VMEM((D + 16, groups * T), BF16),
                        pltpu.VMEM((groups * T, CB), BF16), pltpu.VMEM((rows, groups, BAND, D), BF16),
                        pltpu.VMEM((LAYERS, 5, D), F32), pltpu.VMEM((LAYERS, 1, FF), F32),
                        pltpu.VMEM((LAYERS, 2 * NL, D), F32), pltpu.VMEM((LAYERS, 2 * NS, D), F32),
                        dma((2, rows - 1, groups)), dma((2, rows - 1, groups)), dma((2,))]
        + sum_scratch(rows, batch, LAYERS * chunks, part_rows, width) + sum_scratch(rows, batch, 1, small_rows, D),
        compiler_params=pltpu.CompilerParams(collective_id=2, has_side_effects=True, vmem_limit_bytes=VMEM_LIMIT),
        name="backward",
    )(place, filt_l, filt_s, gain1, gain2, w1, w2, *tabs, mix, fold, outs, do, xs, zs, spec, vs, gs, ps)


def unpack_kernel(order, outs, grads, weights, small, large_out, small_crops, large_grad, small_grad, dw1, dw2,
                  dfilter, dvec, dhid):
    i = pl.program_id(0)
    for given, large, little in ((outs, large_out, small_crops), (grads, large_grad, small_grad)):
        for g in range(given.shape[1]):
            block = given[0, g].astype(F32)
            for s in range(WL):
                large[g, 0, s] = block[s * BL : (s + 1) * BL]
            for p in range(PER):
                for s in range(WS):
                    at = BL * WL + (p * WS + s) * BS
                    little[g * PER + p, 0, s] = block[at : at + BS]
    width = weights.shape[1]
    parts = CB // width
    for c in range(parts):
        cols = slice(c * width, (c + 1) * width)
        dw1[0, :, cols] = weights[c * D : (c + 1) * D, :].astype(F32)
        dw2[0, cols, :] = weights[(parts + c) * D : (parts + c + 1) * D, :].astype(F32).T

    @pl.when(i == 0)
    def _():
        at = LAYERS * 2 * NL
        for n in range(LAYERS):
            for c in range(2):
                dfilter[n, c] = small[(n * 2 + c) * NL : (n * 2 + c + 1) * NL].astype(F32)
        rest = small[at : at + 32].astype(F32)
        for n in range(LAYERS):
            for k in range(5):
                dvec[k, n : n + 1] = rest[n * 5 + k : n * 5 + k + 1]
            for c in range(FF // D):
                r = LAYERS * 5 + n * (FF // D) + c
                dhid[n : n + 1, c * D : (c + 1) * D] = rest[r : r + 1]


def unpack(mesh, groups, outs, grads, weights, small):
    rows = mesh.shape["rows"]
    me = lax.axis_index("rows")
    crops = rows * groups
    chunks = FF // CB
    parts = LAYERS * chunks
    steps = max(rows, parts)
    order = (jnp.arange(rows, dtype=jnp.int32) - me) % rows
    dev = lambda i: jnp.minimum(i, rows - 1)
    part = lambda i: jnp.minimum(i, parts - 1)
    part_rows = weights.shape[0] // parts
    given = pl.BlockSpec((1, groups, BAND, D), lambda i, order: (order[dev(i)], 0, 0, 0))
    large = pl.BlockSpec((groups, 1, WL, BL, D), lambda i, order: (dev(i), 0, 0, 0, 0))
    little = pl.BlockSpec((groups * PER, 1, WS, BS, D), lambda i, order: (dev(i), 0, 0, 0, 0))
    every = lambda shape: pl.BlockSpec(shape, lambda i, order: (0,) * len(shape))
    large_shape = jax.ShapeDtypeStruct((crops, 1, WL, BL, D), F32)
    little_shape = jax.ShapeDtypeStruct((crops * PER, 1, WS, BS, D), F32)
    shapes = [(LAYERS, 2, NL, D), (5, LAYERS, D), (LAYERS, FF)]
    return pl.pallas_call(
        unpack_kernel,
        grid_spec=pltpu.PrefetchScalarGridSpec(
            num_scalar_prefetch=1, grid=(steps,),
            in_specs=[given, given, pl.BlockSpec((part_rows, weights.shape[1]), lambda i, order: (part(i), 0)), every(small.shape)],
            out_specs=[large, little, large, little,
                       pl.BlockSpec((1, D, CB), lambda i, order: (LAYERS - 1 - part(i) // chunks, 0, part(i) % chunks)),
                       pl.BlockSpec((1, CB, D), lambda i, order: (LAYERS - 1 - part(i) // chunks, part(i) % chunks, 0))]
            + [every(s) for s in shapes]),
        out_shape=[large_shape, little_shape, large_shape, little_shape,
                   jax.ShapeDtypeStruct((LAYERS, D, FF), F32), jax.ShapeDtypeStruct((LAYERS, FF, D), F32)]
        + [jax.ShapeDtypeStruct(s, F32) for s in shapes],
        compiler_params=pltpu.CompilerParams(vmem_limit_bytes=VMEM_LIMIT),
        name="unpack",
    )(order, outs, grads, weights, small)


def wanted_rows():
    t, c = np.arange(T), np.arange(BAND)
    small_t, small_c = t >= TL, c >= BL * WL
    at = np.where(small_t, (t - TL) % TS, t)
    wide = np.where(small_t, WS, WL)
    r, w, crop = at // wide, at % wide, np.where(small_t, (t - TL) // TS, 0)
    at_c = np.where(small_c, (c - BL * WL) % (BS * WS), c)
    slots = np.where(small_c, BS, BL)
    s_c, w_c, crop_c = at_c % slots, at_c // slots, np.where(small_c, (c - BL * WL) // (BS * WS), 0)
    same = (small_t[:, None] == small_c) & (w[:, None] == w_c) & (crop[:, None] == crop_c)
    return np.where(same, r[:, None] - s_c, -99).astype(np.int32), s_c[None].astype(np.int32)


def interp_tables():
    fold_l = np.where((np.arange(FL) == 0) | (2 * np.arange(FL) == WL), 1.0, 2.0)
    fold_s = np.where((np.arange(FS) == 0) | (2 * np.arange(FS) == WS), 1.0, 2.0)
    each = lambda n, times: np.repeat(np.eye(n), times, axis=0)
    again = lambda n, times: np.tile(np.eye(n), (times, 1))
    return [jnp.asarray(a, F32) for a in (each(HS, FS), each(HL, FL).T, again(FS, HS) * np.tile(fold_s, HS)[:, None],
                                          again(FL, HL).T, np.tile(fold_l, HL)[:, None])]


def local(mesh, large_in, small_in, large_cot, small_cot, crop_counts, band_bounds, row_interp, col_interp,
          norm1_gain, norm1_bias, filters, norm2_gain, norm2_bias, fc1_weight, fc1_bias, fc2_weight, fc2_bias):
    rows = mesh.shape["rows"]
    me = lax.axis_index("rows")
    crops = large_in.shape[0]
    groups = crops // rows
    pair = 2 if groups % 2 == 0 else 1
    tabs = tables()
    filters = filters.reshape(LAYERS, 2, NL, D)

    def pack(large, small):
        return jnp.concatenate([large.transpose(0, 1, 3, 2, 4).reshape(crops, BL * WL, D),
                                small.transpose(0, 1, 3, 2, 4).reshape(crops, PER * BS * WS, D),
                                jnp.zeros((crops, BAND - BL * WL - PER * BS * WS, D), large.dtype)], axis=1)

    need, slot = wanted_rows()
    extras = (jnp.asarray(need), jnp.asarray(slot), row_interp, col_interp, *interp_tables())
    outs, *saved, do, place, filt_l, filt_s, mix = forward(mesh, groups, pair, pack(large_in, small_in), pack(large_cot, small_cot), crop_counts, band_bounds,
                               (filters, norm1_gain, norm1_bias, norm2_gain, norm2_bias, fc1_weight, fc1_bias, fc2_weight, fc2_bias,
                                *tabs, *extras))
    outs, grads, weights, small = backward(
        mesh, groups, pair, (place, filt_l, filt_s, norm1_gain, norm2_gain, fc1_weight, fc2_weight), tabs,
        mix, extras[-1], outs, do, saved)
    large_out, small_out, large_grad, small_grad, dw1, dw2, dfilter, dvec, dhid = unpack(
        mesh, groups, outs, grads, weights, small)
    large_out, small_out, large_grad, small_grad = (
        a.transpose(0, 1, 3, 2, 4) for a in (large_out, small_out, large_grad, small_grad))
    return (large_out, small_out, large_grad, small_grad, dvec[0], dvec[1], dfilter.reshape(LAYERS, 2, HL, FL, D), dvec[2], dvec[3],
            dw1, dhid, dw2, dvec[4])


def solution(mesh):
    split = P("batch", "rows", None, None, None)
    return jax.shard_map(partial(local, mesh), mesh=mesh, in_specs=(split,) * 4 + (P("batch", None),) + (P(),) * 12,
                         out_specs=(split,) * 4 + (P(),) * 9, check_vma=False)
```

```python
import math
from functools import partial
import numpy as np
import jax
import jax.numpy as jnp
from jax import lax
from jax.experimental import pallas as pl
from jax.experimental.pallas import tpu as pltpu
from jax.sharding import PartitionSpec as P

D, FF = 384, 1536
HL, WL, FL = 14, 14, 8
HS, WS, FS = 6, 6, 4
BL, BS = 4, 2
LAYERS = 2
EPS = 1e-6
TL, TS = HL * WL, HS * WS
PER = 3
T = TL + PER * TS
CUT, END = 192, 208
NL, NS = HL * FL, HS * FS
BAND = 96
CH = 512
CB = 512
SMALL = 512
PLAN = {
    (0, 0): [(-3, 0)],
    (0, 9): [(0, 0), (-3, 1)],
    (1, 2): [(0, 1), (-3, 2)],
    (1, 9): [(1, 0)],
    (2, 0): [(-3, 3)],
    (2, 2): [(1, 1)],
    (2, 9): [(0, 2), (2, 0)],
    (3, 0): [(-3, 4)],
    (3, 2): [(2, 1)],
    (4, 0): [(-3, 5)],
    (4, 1): [(1, 2)],
    (5, 1): [(0, 3)],
    (5, 2): [(2, 2)],
    (6, 9): [(1, 3), (3, 0)],
    (7, 1): [(0, 4)],
    (7, 2): [(3, 1)],
    (7, 9): [(4, 0), (2, 3)],
    (8, 2): [(4, 1)],
    (8, 9): [(1, 4), (0, 5), (5, 0)],
    (9, 1): [(3, 2)],
    (9, 2): [(0, 6)],
    (9, 9): [(5, 1), (2, 4), (-2, 0)],
    (10, 1): [(4, 2)],
    (11, 0): [(-2, 1)],
    (11, 1): [(1, 5)],
    (11, 9): [(3, 3), (-1, 0), (1, 6), (5, 2), (-1, 1), (4, 3), (2, 5), (-1, 2), (2, 6), (3, 4), (-2, 2), (5, 3), (3, 5), (-2, 3), (4, 4), (3, 6), (-1, 3), (5, 4), (-2, 4), (4, 5), (-1, 4), (-2, 5), (4, 6), (5, 5), (-1, 5), (5, 6), (-1, 6)],
}
MESH = pl.DeviceIdType.MESH
VMEM_LIMIT = 60 * 2**20
F32, BF16 = jnp.float32, jnp.bfloat16
HIGHEST = lax.Precision.HIGHEST


def table(height, width, count):
    k = np.arange(height)[:, None, None, None]
    l = np.arange(count)[None, :, None, None]
    s = np.arange(height)[None, None, :, None]
    w = np.arange(width)[None, None, None, :]
    phase = (k * s * width + l * w * height) % (height * width)
    angle = phase.astype(np.float32) * np.float32(2.0 * math.pi / (height * width))
    scale = np.float32(1.0 / math.sqrt(height * width))
    both = np.stack([np.cos(angle) * scale, -np.sin(angle) * scale])
    return both.reshape(2, height * count, height * width).astype(jnp.bfloat16).astype(np.float32)


def tables():
    large = np.zeros((2 * NL, END), np.float32)
    large[:, :TL] = table(HL, WL, FL).reshape(2 * NL, TL)
    one = table(HS, WS, FS)
    small = np.zeros((2, PER, NS, T - CUT), np.float32)
    for at in range(PER):
        small[:, at, :, TL - CUT + at * TS : TL - CUT + (at + 1) * TS] = one
    small = small.reshape(2 * PER * NS, T - CUT)
    return [jnp.asarray(t, BF16) for t in (large, small, large.T, small.T)]


def normal(x):
    mean = jnp.mean(x, axis=-1, keepdims=True)
    centred = x - mean
    scale = lax.rsqrt(jnp.mean(centred * centred, axis=-1, keepdims=True) + EPS)
    return centred * scale, scale


def normal_back(grad, gain, unit, scale):
    inner = grad * gain
    first = jnp.mean(inner, axis=-1, keepdims=True)
    second = jnp.mean(inner * unit, axis=-1, keepdims=True)
    return (inner - first - unit * second) * scale


def dot(a, b):
    return jnp.dot(a, b, preferred_element_type=F32)


def dot_nt(a, b):
    return lax.dot_general(a, b, (((1,), (1,)), ((), ())), preferred_element_type=F32)


def dot_tn(a, b):
    return lax.dot_general(a, b, (((0,), (0,)), ((), ())), preferred_element_type=F32)


def analyse(large_table, small_table, values):
    return dot(large_table, values[:END]), dot(small_table, values[CUT:])


def synthesise(large_back, small_back, large, small):
    a, b = dot(large_back, large), dot(small_back, small)
    return jnp.concatenate([a[:CUT], a[CUT:] + b[: END - CUT], b[END - CUT :]], axis=0)


def thrice(x):
    return jnp.concatenate([x] * PER, axis=0)


def gelu_both(h):
    cdf = 0.5 + 0.5 * lax.erf(h * np.float32(math.sqrt(0.5)))
    dens = jnp.exp(h * h * np.float32(-0.5)) * np.float32(1 / math.sqrt(2 * math.pi))
    return h * cdf, cdf + h * dens


def live_rows(counts, group):
    t = lax.broadcasted_iota(jnp.int32, (T, 1), 0)
    place, limit = jnp.full((T, 1), group), jnp.where(t < TL, counts[0, 0], counts[0, 1])
    for at in range(PER):
        place = jnp.where(t >= TL + at * TS, group * PER + at, place)
    return jnp.where(place < limit, 1.0, 0.0)


def whole(shape):
    return pl.BlockSpec(shape, lambda *a: (0,) * len(shape))


def scalars():
    return pl.BlockSpec(memory_space=pltpu.SMEM)


def forward_kernel(row_count, groups, pair, large_in, small_in, large_cot, small_cot, counts, bounds, filters, gain1, bias1, gain2, bias2,
                   w1, b1, w2, b2, tl, ts, tlb, tsb, need, slot, row_interp, col_interp, row_s, row_l, col_s, col_l, fold,
                   outs, xs, zs, both_scales, spec, vs, gs, ps, do, place, filt_l, filt_s, mix,
                   pick, lined, large_slots, small_slots, own_sem, send_sem, recv_sem):
    step = pl.program_id(0)
    batch, row = lax.axis_index("batch"), lax.axis_index("rows")
    last = groups // pair - 1

    def ends(which, m, g, to):
        crop = to * groups + g
        return (((large_in, large_cot)[which].at[crop, 0], large_slots.at[which, m, g]),
                ((small_in, small_cot)[which].at[pl.ds(crop * PER, PER), 0], small_slots.at[which, m, g]))

    def remote(which, m, g):
        to = lax.rem(row + m, row_count)
        return [pltpu.make_async_remote_copy(
            src_ref=source, dst_ref=target,
            send_sem=send_sem.at[which, k, m - 1, g], recv_sem=recv_sem.at[which, k, m - 1, g],
            device_id=(batch, to), device_id_type=MESH) for k, (source, target) in enumerate(ends(which, m, g, to))]

    def mine(which, g):
        return [pltpu.make_async_copy(source, target, own_sem.at[which, k, g])
                for k, (source, target) in enumerate(ends(which, 0, g, row))]

    @pl.when(step == 0)
    def _():
        barrier = pltpu.get_barrier_semaphore()
        for m in range(1, row_count):
            pl.semaphore_signal(barrier, inc=1, device_id=(batch, lax.rem(row + m, row_count)), device_id_type=MESH)
        for which in range(2):
            @pl.loop(0, groups)
            def _(g):
                for copy in mine(which, g):
                    copy.start()
        pl.semaphore_wait(barrier, row_count - 1)
        for which in range(2):
            @pl.loop(0, groups)
            def _(g):
                for m in range(1, row_count):
                    for copy in remote(which, m, g):
                        copy.start()
        lined[...] = jnp.zeros_like(lined)
        for m in range(row_count):
            band = lax.rem(row + (row_count - m), row_count)
            large = lax.broadcasted_iota(jnp.int32, (T, BAND), 0) < TL
            first = jnp.where(large, bounds[0, band], bounds[1, band])
            size = jnp.where(large, bounds[0, band + 1], bounds[1, band + 1]) - first
            hit = (need[...] == first) & (slot[...] < size)
            hit = jnp.where(hit, 1.0, 0.0)
            pick[:, m * BAND : (m + 1) * BAND] = hit.astype(BF16)
            place[m * BAND : (m + 1) * BAND, :] = hit.T.astype(BF16)
        exact = partial(jnp.dot, preferred_element_type=F32, precision=HIGHEST)
        both = exact(exact(row_s[...], row_interp[...]), row_l[...]) * exact(exact(col_s[...], col_interp[...]), col_l[...])
        mix[...] = both
        for n in range(LAYERS):
            for c in range(2):
                filt_l[n, c] = filters[n, c] * fold[...]
                filt_s[n, c] = exact(both, filters[n, c])

    def live(g):
        return live_rows(counts, row * groups + g)

    def take(which, g):
        for copy in mine(which, g):
            copy.wait()
        for m in range(1, row_count):
            for copy in remote(which, m, g):
                copy.wait_recv()
        for m in range(row_count):
            at = m * BAND
            for w in range(WL):
                lined[at + w * BL : at + (w + 1) * BL, :] = large_slots[which, m, g, w].astype(F32)
            at += BL * WL
            for p in range(PER):
                for w in range(WS):
                    row_at = at + (p * WS + w) * BS
                    lined[row_at : row_at + BS, :] = small_slots[which, m, g, p, w].astype(F32)
        return dot(pick[...], lined[...].astype(BF16))

    side = lambda parts: jnp.concatenate(parts, axis=1)
    lanes = lambda a: [a[:, j * D : (j + 1) * D] for j in range(pair)]
    x = [take(0, step * pair + j) for j in range(pair)]
    for n in range(LAYERS):
        u, scales = [], []
        for j in range(pair):
            unit, scale = normal(x[j])
            xs[n, j] = unit.astype(BF16)
            scales.append(scale)
            u.append((unit * gain1[n : n + 1] + bias1[n : n + 1]).astype(BF16))
        xl, xsm = analyse(tl[...], ts[...], side(u))
        yl, ys = [], []
        for j, (a, b) in enumerate(zip(lanes(xl), lanes(xsm))):
            spec[n, j, : 2 * NL] = a.astype(BF16)
            spec[n, j, 2 * NL :] = b.astype(BF16)
            lr, li = a[:NL], a[NL:]
            sr, si = b[: PER * NS], b[PER * NS :]
            gr, gi = filt_l[n, 0], filt_l[n, 1]
            yl.append(jnp.concatenate([lr * gr - li * gi, lr * gi + li * gr], axis=0).astype(BF16))
            gr, gi = thrice(filt_s[n, 0]), thrice(filt_s[n, 1])
            ys.append(jnp.concatenate([sr * gr - si * gi, sr * gi + si * gr], axis=0).astype(BF16))
        v = []
        for j, z in enumerate(lanes(synthesise(tlb[...], tsb[...], side(yl), side(ys)))):
            unit, scale = normal(z)
            zs[n, j] = unit.astype(BF16)
            both_scales[n, j] = side([scales[j], scale])
            unit = (unit * gain2[n : n + 1] + bias2[n : n + 1]).astype(BF16)
            vs[n, j] = unit
            v.append(unit)
        v = jnp.concatenate(v, axis=0)
        total = jnp.concatenate(x, axis=0) + b2[n : n + 1]
        for c in range(0, FF, CH):
            h = dot(v, w1[n, :, c : c + CH]) + b1[n : n + 1, c : c + CH]
            g, slope = gelu_both(h)
            g = g.astype(BF16)
            slope = slope.astype(BF16)
            for j in range(pair):
                gs[n, j, :, c : c + CH] = g[j * T : (j + 1) * T]
                ps[n, j, :, c : c + CH] = slope[j * T : (j + 1) * T]
            total = total + dot(g, w2[n, c : c + CH, :])
        x = [total[j * T : (j + 1) * T] for j in range(pair)]
    for j in range(pair):
        spread = dot(place[...], (x[j] * live(step * pair + j)).astype(BF16)).astype(BF16)
        for m in range(row_count):
            outs[m, j] = spread[m * BAND : (m + 1) * BAND]

    @pl.when(step == last)
    def _():
        for g in range(groups):
            do[g] = (take(1, g) * live(g)).astype(BF16)
        for which in range(2):
            @pl.loop(0, groups)
            def _(g):
                for m in range(1, row_count):
                    for copy in remote(which, m, g):
                        copy.wait_send()


def forward(mesh, groups, pair, crops, counts, bounds, small):
    rows = mesh.shape["rows"]
    sizes = [(T, D, BF16), (T, D, BF16), (T, 2, F32), (2 * NL + 2 * PER * NS, D, BF16), (T, D, BF16), (T, FF, BF16), (T, FF, BF16)]
    extra = [((groups, T, D), BF16), ((rows * BAND, T), BF16), ((LAYERS, 2, NL, D), F32), ((LAYERS, 2, NS, D), F32), ((NS, NL), F32)]
    hbm = pl.BlockSpec(memory_space=pl.ANY)
    return pl.pallas_call(
        partial(forward_kernel, rows, groups, pair),
        grid=(groups // pair,),
        in_specs=[hbm] * 4 + [scalars(), scalars()] + [whole(a.shape) for a in small],
        out_specs=[pl.BlockSpec((rows, pair, BAND, D), lambda i: (0, i, 0, 0))]
        + [pl.BlockSpec((LAYERS, pair, a, b), lambda i: (0, i, 0, 0)) for a, b, _ in sizes]
        + [whole(a) for a, _ in extra],
        out_shape=[jax.ShapeDtypeStruct((rows, groups, BAND, D), BF16)]
        + [jax.ShapeDtypeStruct((LAYERS, groups, a, b), t) for a, b, t in sizes]
        + [jax.ShapeDtypeStruct(a, t) for a, t in extra],
        scratch_shapes=[pltpu.VMEM((T, rows * BAND), BF16), pltpu.VMEM((rows * BAND, D), F32),
                        pltpu.VMEM((2, rows, groups, WL, BL, D), BF16), pltpu.VMEM((2, rows, groups, PER, WS, BS, D), BF16),
                        pltpu.SemaphoreType.DMA((2, 2, groups)), pltpu.SemaphoreType.DMA((2, 2, rows - 1, groups)),
                        pltpu.SemaphoreType.DMA((2, 2, rows - 1, groups))],
        compiler_params=pltpu.CompilerParams(collective_id=1, has_side_effects=True, vmem_limit_bytes=VMEM_LIMIT),
        name="forward",
    )(*crops, counts, bounds, *small)


SPREAD = True
LOW = 2


def add_rows(target, at_target, base, sources, count):
    step = next(s for s in (128, 96, 64, 48, 32, 16) if count % s == 0)

    @pl.loop(0, count // step)
    def _(i):
        at = pl.multiple_of(i * step, 16)
        rows = pl.ds(pl.multiple_of(base + at, 16), step)
        total = at_target[rows, :].astype(F32)
        for ref in sources:
            total = total + ref[pl.ds(at, step), :].astype(F32)
        target[rows, :] = total.astype(BF16)


class Sum:
    def __init__(self, mesh_rows, mesh_batch, acc, full, out, count, bufs, sems, save_sem):
        batch, row = lax.axis_index("batch"), lax.axis_index("rows")
        self.acc, self.full, self.out, self.count, self.bufs, self.sems, self.save_sem = acc, full, out, count, bufs, sems, save_sem
        self.size = kinds(mesh_rows, mesh_batch)
        self.levels = len(self.size)
        x_n = mesh_rows // 2
        core, x, z, y = lax.rem(row, 2), lax.div(row, 2), lax.div(batch, LOW), lax.rem(batch, LOW)
        self.me = [core, y, z * x_n + x] if SPREAD else [core, y, x, z]
        self.others, self.offsets, self.counts = [], [0], [count]
        for level, n in enumerate(self.size):
            count //= n
            self.counts.append(count)
            self.offsets.append(self.offsets[-1] + self.me[level] * count)
            found = []
            for step in range(1, n):
                at = lax.rem(self.me[level] + step, n)
                device = [(batch, x * 2 + at), (z * LOW + at, row)]
                device += [(lax.div(at, x_n) * LOW + y, lax.rem(at, x_n) * 2 + core)] if SPREAD else [
                    (batch, at * 2 + core), (at * LOW + y, row)]
                found.append((device[level], at))
            self.others.append(found)

    def region(self, part, level):
        return part * self.count + self.offsets[level], self.counts[level]

    def rows(self, base, count):
        return pl.ds(pl.multiple_of(base, 16), count)

    def down(self, part, level, step):
        base, count = self.region(part, level)
        device, at = self.others[level][step - 1]
        chunk = count // self.size[level]
        return pltpu.make_async_remote_copy(
            src_ref=self.acc.at[self.rows(base + at * chunk, chunk)], dst_ref=self.bufs[level].at[part, self.rows((step - 1) * chunk, chunk)],
            send_sem=self.sems[level].at[0, part], recv_sem=self.sems[level].at[1, part],
            device_id=device, device_id_type=MESH)

    def up(self, part, level, step):
        base, count = self.region(part, level + 1)
        rows = self.rows(base, count)
        return pltpu.make_async_remote_copy(
            src_ref=self.full.at[rows], dst_ref=self.full.at[rows],
            send_sem=self.sems[level].at[2, part], recv_sem=self.sems[level].at[3, part],
            device_id=self.others[level][step - 1][0], device_id_type=MESH)

    def arrived(self, part, level, sem):
        every = self.bufs[level].at[part]
        pltpu.make_async_copy(every, every, self.sems[level].at[sem, part]).wait()

    def save(self, part):
        rows = self.rows(part * self.count, self.count)
        return pltpu.make_async_copy(self.full.at[rows], self.out.at[rows], self.save_sem.at[part])

    def stage(self, part, k):
        top = self.levels
        if 1 <= k <= top:
            level = k - 1
            self.arrived(part, level, 0)
            self.arrived(part, level, 1)
            base, count = self.region(part, level + 1)
            add_rows(self.full if k == top else self.acc, self.acc, base,
                     [self.bufs[level].at[part, self.rows(s * count, count)] for s in range(self.size[level] - 1)], count)
        if k < top:
            for step in range(1, self.size[k]):
                self.down(part, k, step).start()
        if k > top:
            level = 2 * top - k
            self.arrived(part, level, 2)
            self.arrived(part, level, 3)
        if top <= k < 2 * top:
            for step in range(1, self.size[2 * top - 1 - k]):
                self.up(part, 2 * top - 1 - k, step).start()
        if k == 2 * top:
            self.save(part).start()


def kinds(mesh_rows, mesh_batch):
    x_n, z_n = mesh_rows // 2, mesh_batch // LOW
    return [2, LOW, x_n * z_n] if SPREAD else [2, LOW, x_n, z_n]


def columns(mesh_rows, mesh_batch):
    sizes = {w: w * padded(mesh_rows, mesh_batch, 2 * D * (CB // w)) for w in (256, 128)}
    return min(sizes, key=sizes.get)


def padded(mesh_rows, mesh_batch, count):
    unit = 16 * math.prod(kinds(mesh_rows, mesh_batch))
    return -(-count // unit) * unit


def sum_scratch(mesh_rows, mesh_batch, parts, count, width):
    size = kinds(mesh_rows, mesh_batch)
    shapes = [pltpu.VMEM((parts * count, width), BF16)] * 2
    for n in size:
        count //= n
        shapes.append(pltpu.VMEM((parts, (n - 1) * count, width), BF16))
    return shapes + [pltpu.SemaphoreType.DMA((4, parts)) for n in size] + [pltpu.SemaphoreType.DMA((parts,))]


def backward_kernel(row_count, batch_count, groups, pair, place, filt_l, filt_s, gain1, gain2, w1, w2, tl, ts, tlb, tsb,
                    mix, fold, outs, do_in, xs, zs, both_scales, spec, vs, gs, ps,
                    out_land, grad_land, weights_out, small_out,
                    dx, dv, do, dot_, vt, dh, gslots, dvec, dhid, dfl, dfs, out_sem, grad_sem, own_sem, *sums):
    i = pl.program_id(0)
    batch, row = lax.axis_index("batch"), lax.axis_index("rows")
    chunks, pairs = FF // CB, groups // pair
    per = chunks + pairs
    compute_steps = LAYERS * per
    layer, q = LAYERS - 1 - i // per, i % per
    width = columns(row_count, batch_count)
    part_rows = padded(row_count, batch_count, 2 * D * (CB // width))
    small_rows = padded(row_count, batch_count, SMALL)
    sums_of = []
    for out, count in ((weights_out, part_rows), (small_out, small_rows)):
        n = len(kinds(row_count, batch_count))
        sums_of.append(Sum(row_count, batch_count, sums[0], sums[1], out, count, sums[2 : 2 + n], sums[2 + n : 2 + 2 * n], sums[2 + 2 * n]))
        sums = sums[3 + 2 * n :]
    weights, small = sums_of

    def send_out(m, g):
        return pltpu.make_async_remote_copy(
            src_ref=outs.at[m, g], dst_ref=out_land.at[m, g], send_sem=out_sem.at[0, m - 1, g], recv_sem=out_sem.at[1, m - 1, g],
            device_id=(batch, lax.rem(row + (row_count - m), row_count)), device_id_type=MESH)

    def send_grad(m, g):
        return pltpu.make_async_remote_copy(
            src_ref=gslots.at[m, g], dst_ref=grad_land.at[m, g], send_sem=grad_sem.at[0, m - 1, g], recv_sem=grad_sem.at[1, m - 1, g],
            device_id=(batch, lax.rem(row + (row_count - m), row_count)), device_id_type=MESH)

    def keep_out():
        return pltpu.make_async_copy(outs.at[0], out_land.at[0], own_sem.at[0])

    def keep_grad():
        return pltpu.make_async_copy(gslots.at[0], grad_land.at[0], own_sem.at[1])

    plan = {key: [a for a in PLAN[key] if a[0] != -2 or groups == 6] for key in PLAN}
    if groups != 6:
        plan[compute_steps - 1, 9] = [(-2, g) for g in range(groups)] + plan[compute_steps - 1, 9]
    left = set(plan)

    def do_now(part, k):
        if part >= 0:
            weights.stage(part, k)
        elif part == -1:
            small.stage(0, k)
        elif k < groups:
            for m in range(1, row_count):
                (send_grad if part == -2 else send_out)(m, k).start()

    def advance(place, steps):
        for at in steps:
            found = sorted(key for key in left if key[0] == at and (key[1] == place or place == 9))
            if found:
                @pl.when(i == at)
                def _():
                    for key in found:
                        left.discard(key)
                        for part, k in plan[key]:
                            do_now(part, k)

    first_steps = [at for at in range(compute_steps) if at % per < chunks]
    second_steps = [at for at in range(compute_steps) if at % per >= chunks]

    @pl.when(i == 0)
    def _():
        barrier = pltpu.get_barrier_semaphore()
        greeted = 0
        for m in range(1, row_count):
            pl.semaphore_signal(barrier, inc=1, device_id=(batch, lax.rem(row + m, row_count)), device_id_type=MESH)
            greeted += 1
        for level in range(1, weights.levels):
            for step in range(1, weights.size[level]):
                pl.semaphore_signal(barrier, inc=1, device_id=weights.others[level][step - 1][0], device_id_type=MESH)
                greeted += 1
        keep_out().start()
        if part_rows > 2 * D * (CB // width):
            weights.acc[...] = jnp.zeros_like(weights.acc)
        for g in range(groups):
            dx[g] = do_in[g].astype(F32)
        for ref in (dvec, dfl, dfs):
            ref[...] = jnp.zeros_like(ref)
        pl.semaphore_wait(barrier, greeted)

    @pl.when((i < compute_steps) & (q == 0))
    def _():
        for g in range(groups):
            rows = pl.ds(g * T, T)
            low = dx[g].astype(BF16)
            do[g] = low
            dvec[layer, 4:5] += jnp.sum(low.astype(F32), axis=0, keepdims=True)
        dot_[...] = do[...].reshape(groups * T, D).T
        vt[:D] = vs[0].reshape(groups * T, D).T
        vt[D:] = jnp.ones((16, groups * T), BF16)
        dv[...] = jnp.zeros_like(dv)

    @pl.when((i < compute_steps) & (q < chunks))
    def _():
        for g in range(0, groups, pair):
            rows = slice(g * T, (g + pair) * T)
            some = do[g : g + pair].reshape(pair * T, D)
            slope = ps[0, g : g + pair].reshape(pair * T, CB)
            part = (dot_nt(some, w2[0]) * slope.astype(F32)).astype(BF16)
            dh[rows] = part
            dv[g : g + pair] += dot_nt(part, w1[0]).reshape(pair, T, D)
            advance(g // pair, first_steps)
        part = (LAYERS - 1 - layer) * chunks + q
        base = part * part_rows
        one = dot(vt[...], dh[...])
        dhid[layer, :, pl.ds(pl.multiple_of(q * CB, CB), CB)] = one[D : D + 1]
        two = dot(dot_[...], gs[0].reshape(groups * T, CB))
        for c in range(CB // width):
            cols = slice(c * width, (c + 1) * width)
            weights.acc[weights.rows(base + c * D, D), :] = one[:D, cols].astype(BF16)
            weights.acc[weights.rows(base + (CB // width + c) * D, D), :] = two[:, cols].astype(BF16)

    @pl.when((i < compute_steps) & (q >= chunks))
    def _():
        side = lambda parts: jnp.concatenate(parts, axis=1)
        lanes = lambda a: [a[:, j * D : (j + 1) * D] for j in range(pair)]
        row_sum = lambda a: jnp.sum(a, axis=0, keepdims=True)
        first = (q - chunks) * pair
        dz = []
        for j in range(pair):
            dvg = dv[first + j]
            unit = zs[0, j].astype(F32)
            dvec[layer, 2:3] += row_sum(dvg * unit)
            dvec[layer, 3:4] += row_sum(dvg)
            dz.append(normal_back(dvg, gain2[pl.ds(layer, 1)], unit, both_scales[0, j, :, 1:2]).astype(BF16))
        advance(0, second_steps)
        yl, ysm = analyse(tl[...], ts[...], side(dz))
        dl, ds = [], []
        for j, (a, b) in enumerate(zip(lanes(yl), lanes(ysm))):
            lr, li = a[:NL], a[NL:]
            sr, si = b[: PER * NS], b[PER * NS :]
            xr, xi = spec[0, j, :NL].astype(F32), spec[0, j, NL : 2 * NL].astype(F32)
            dfl[layer, :NL] += lr * xr + li * xi
            dfl[layer, NL:] += li * xr - lr * xi
            gr, gi = filt_l[0, 0], filt_l[0, 1]
            dl.append(jnp.concatenate([lr * gr + li * gi, li * gr - lr * gi], axis=0).astype(BF16))
            small_spec = spec[0, j, 2 * NL :].astype(F32)
            xr, xi = small_spec[: PER * NS], small_spec[PER * NS :]
            once = lambda a: a[:NS] + a[NS : 2 * NS] + a[2 * NS :]
            dfs[layer, :NS] += once(sr * xr + si * xi)
            dfs[layer, NS:] += once(si * xr - sr * xi)
            gr, gi = thrice(filt_s[0, 0]), thrice(filt_s[0, 1])
            ds.append(jnp.concatenate([sr * gr + si * gi, si * gr - sr * gi], axis=0).astype(BF16))
        advance(1, second_steps)
        grads = []
        for j, du in enumerate(lanes(synthesise(tlb[...], tsb[...], side(dl), side(ds)))):
            unit = xs[0, j].astype(F32)
            dvec[layer, 0:1] += row_sum(du * unit)
            dvec[layer, 1:2] += row_sum(du)
            grad = dx[first + j] + normal_back(du, gain1[pl.ds(layer, 1)], unit, both_scales[0, j, :, 0:1])
            dx[first + j] = grad
            grads.append(grad.astype(BF16))
        advance(2, second_steps)

        @pl.when(layer == 0)
        def _():
            spread = dot(place[...], side(grads)).astype(BF16)
            for j in range(pair):
                for m in range(row_count):
                    gslots[m, first + j] = spread[m * BAND : (m + 1) * BAND, j * D : (j + 1) * D]

    @pl.when(i == compute_steps - 1)
    def _():
        small.acc[...] = jnp.zeros_like(small.acc)
        exact = partial(jnp.dot, preferred_element_type=F32, precision=HIGHEST)
        mix_t = mix[...].T
        for n in range(LAYERS):
            for c in range(2):
                at = (n * 2 + c) * NL
                small.acc[at : at + NL, :] = (dfl[n, c * NL : (c + 1) * NL] * fold[...]
                                              + exact(mix_t, dfs[n, c * NS : (c + 1) * NS])).astype(BF16)
        at = LAYERS * 2 * NL
        rest = [dvec[n, k : k + 1] for n in range(LAYERS) for k in range(5)]
        rest += [dhid[n, :, c : c + D] for n in range(LAYERS) for c in range(0, FF, D)]
        rest.append(jnp.zeros((-len(rest) % 16, D), F32))
        rest = jnp.concatenate(rest, axis=0).astype(BF16)
        small.acc[at : at + rest.shape[0], :] = rest
        keep_grad().start()

    advance(9, range(compute_steps))

    @pl.when(i == pl.num_programs(0) - 1)
    def _():
        keep_out().wait()
        keep_grad().wait()
        for m in range(1, row_count):
            @pl.loop(0, groups)
            def _(g):
                send_out(m, g).wait()
                send_grad(m, g).wait()
        for part in range(LAYERS * chunks):
            weights.save(part).wait()
        small.save(0).wait()


def backward(mesh, groups, pair, small, tabs, mix, fold, outs, do, saved):
    rows, batch = mesh.shape["rows"], mesh.shape["batch"]
    place, filt_l, filt_s, gain1, gain2, w1, w2 = small
    chunks, pairs = FF // CB, groups // pair
    per, last = chunks + pairs, LAYERS - 1
    steps = LAYERS * per
    layer = lambda i: jnp.maximum(last - i // per, 0)
    when = lambda i: jnp.where(i < LAYERS * per, i % per, per - 1)
    chunk = lambda i: jnp.minimum(when(i), chunks - 1)
    place_of = lambda i: jnp.maximum(when(i) - chunks, 0)
    per_layer = lambda a: pl.BlockSpec((1,) + a.shape[1:], lambda i: (layer(i),) + (0,) * (a.ndim - 1))
    by_pair = lambda a: pl.BlockSpec((1, pair) + a.shape[2:], lambda i: (layer(i), place_of(i), 0, 0))
    by_chunk = lambda a: pl.BlockSpec((1, groups, T, CB), lambda i: (layer(i), 0, 0, chunk(i)))
    xs, zs, scales, spec, vs, gs, ps = saved
    hbm = pl.BlockSpec(memory_space=pl.ANY)
    width = columns(rows, batch)
    part_rows, small_rows = padded(rows, batch, 2 * D * (CB // width)), padded(rows, batch, SMALL)
    dma = pltpu.SemaphoreType.DMA
    return pl.pallas_call(
        partial(backward_kernel, rows, batch, groups, pair),
        grid=(steps,),
        in_specs=[whole(place.shape), per_layer(filt_l), per_layer(filt_s), whole(gain1.shape), whole(gain2.shape)]
        + [pl.BlockSpec((1, D, CB), lambda i: (layer(i), 0, chunk(i))), pl.BlockSpec((1, CB, D), lambda i: (layer(i), chunk(i), 0))]
        + [whole(a.shape) for a in (*tabs, mix, fold)] + [hbm, whole(do.shape)]
        + [by_pair(xs), by_pair(zs), by_pair(scales), by_pair(spec), per_layer(vs), by_chunk(gs), by_chunk(ps)],
        out_specs=[hbm] * 4,
        out_shape=[jax.ShapeDtypeStruct((rows, groups, BAND, D), BF16)] * 2
        + [jax.ShapeDtypeStruct((LAYERS * chunks * part_rows, width), BF16), jax.ShapeDtypeStruct((small_rows, D), BF16)],
        scratch_shapes=[pltpu.VMEM((groups, T, D), F32), pltpu.VMEM((groups, T, D), F32), pltpu.VMEM((groups, T, D), BF16),
                        pltpu.VMEM((D, groups * T), BF16), pltpu.VMEM((D + 16, groups * T), BF16),
                        pltpu.VMEM((groups * T, CB), BF16), pltpu.VMEM((rows, groups, BAND, D), BF16),
                        pltpu.VMEM((LAYERS, 5, D), F32), pltpu.VMEM((LAYERS, 1, FF), F32),
                        pltpu.VMEM((LAYERS, 2 * NL, D), F32), pltpu.VMEM((LAYERS, 2 * NS, D), F32),
                        dma((2, rows - 1, groups)), dma((2, rows - 1, groups)), dma((2,))]
        + sum_scratch(rows, batch, LAYERS * chunks, part_rows, width) + sum_scratch(rows, batch, 1, small_rows, D),
        compiler_params=pltpu.CompilerParams(collective_id=2, has_side_effects=True, vmem_limit_bytes=VMEM_LIMIT),
        name="backward",
    )(place, filt_l, filt_s, gain1, gain2, w1, w2, *tabs, mix, fold, outs, do, xs, zs, scales, spec, vs, gs, ps)


def unpack_kernel(groups, order, outs, grads, weights, small, large_out, small_crops, large_grad, small_grad, dw1, dw2, dfilter, dhid,
                  *rest):
    dvec, rest = rest[:5], rest[5:]
    given, weight, large, little, one, two, in_sem, weight_sem, out_sem, done_sem = rest
    rows = outs.shape[0]
    parts, chunks, width = weight.shape[0], FF // CB, weight.shape[2]
    halves = CB // width

    def read(dev, kind):
        return pltpu.make_async_copy((outs, grads)[kind].at[order[dev]], given.at[kind, dev], in_sem.at[kind, dev])

    def read_weight(part):
        return pltpu.make_async_copy(weights.at[part], weight.at[part], weight_sem.at[part])

    def write(dev, kind):
        to_large, to_little = ((large_out, small_crops), (large_grad, small_grad))[kind]
        return (pltpu.make_async_copy(large.at[kind, dev], to_large.at[pl.ds(dev * groups, groups)], out_sem.at[kind, 0, dev]),
                pltpu.make_async_copy(little.at[kind, dev], to_little.at[pl.ds(dev * groups * PER, groups * PER)], out_sem.at[kind, 1, dev]))

    def write_weight(part):
        layer, at = LAYERS - 1 - part // chunks, part % chunks * CB
        return (pltpu.make_async_copy(one.at[part], dw1.at[layer, :, pl.ds(at, CB)], done_sem.at[0, part]),
                pltpu.make_async_copy(two.at[part], dw2.at[layer, pl.ds(at, CB)], done_sem.at[1, part]))

    for part in range(parts):
        read_weight(part).start()
    for dev in range(rows):
        for kind in range(2):
            read(dev, kind).start()
    for part in range(parts):
        read_weight(part).wait()
        for c in range(halves):
            cols = slice(c * width, (c + 1) * width)
            one[part, :, cols] = weight[part, c * D : (c + 1) * D].astype(F32)
            two[part, cols] = weight[part, (halves + c) * D : (halves + c + 1) * D].astype(F32).T
        for copy in write_weight(part):
            copy.start()
    for dev in range(rows):
        for kind in range(2):
            read(dev, kind).wait()

            @pl.loop(0, groups)
            def _(g):
                block = given[kind, dev, g].astype(F32)
                for w in range(WL):
                    large[kind, dev, g, 0, w] = block[w * BL : (w + 1) * BL]
                for p in range(PER):
                    for w in range(WS):
                        at = BL * WL + (p * WS + w) * BS
                        little[kind, dev, g * PER + p, 0, w] = block[at : at + BS]

            for copy in write(dev, kind):
                copy.start()
    at = LAYERS * 2 * NL
    for n in range(LAYERS):
        for c in range(2):
            dfilter[n, c] = small[(n * 2 + c) * NL : (n * 2 + c + 1) * NL].astype(F32)
    others = small[at : at + 32].astype(F32)
    for n in range(LAYERS):
        for k in range(5):
            dvec[k][n : n + 1] = others[n * 5 + k : n * 5 + k + 1]
        for c in range(FF // D):
            r = LAYERS * 5 + n * (FF // D) + c
            dhid[n : n + 1, c * D : (c + 1) * D] = others[r : r + 1]
    for part in range(parts):
        for copy in write_weight(part):
            copy.wait()
    for dev in range(rows):
        for kind in range(2):
            for copy in write(dev, kind):
                copy.wait()


def unpack(mesh, groups, pair, outs, grads, weights, small):
    rows = mesh.shape["rows"]
    me = lax.axis_index("rows")
    crops = rows * groups
    width = weights.shape[1]
    halves = CB // width
    parts = LAYERS * (FF // CB)
    weights = weights.reshape(parts, -1, width)[:, : 2 * D * halves]
    order = lax.rem(jnp.arange(rows, dtype=jnp.int32) + (rows - me), rows)
    large_shape, little_shape = (crops, 1, WL, BL, D), (crops * PER, 1, WS, BS, D)
    shapes = [(LAYERS, 2, NL, D), (LAYERS, FF)] + [(LAYERS, D)] * 5
    hbm, vmem, dma = pl.BlockSpec(memory_space=pl.ANY), pl.BlockSpec(memory_space=pltpu.VMEM), pltpu.SemaphoreType.DMA
    return pl.pallas_call(
        partial(unpack_kernel, groups),
        in_specs=[scalars()] + [hbm] * 3 + [vmem],
        out_specs=[hbm] * 6 + [vmem] * len(shapes),
        out_shape=[jax.ShapeDtypeStruct(s, F32) for s in [large_shape, little_shape] * 2 + [(LAYERS, D, FF), (LAYERS, FF, D)] + shapes],
        scratch_shapes=[pltpu.VMEM((2, rows, groups, BAND, D), BF16), pltpu.VMEM(weights.shape, BF16),
                        pltpu.VMEM((2, rows, groups, 1, WL, BL, D), F32), pltpu.VMEM((2, rows, groups * PER, 1, WS, BS, D), F32),
                        pltpu.VMEM((parts, D, CB), F32), pltpu.VMEM((parts, CB, D), F32),
                        dma((2, rows)), dma((parts,)), dma((2, 2, rows)), dma((2, parts))],
        compiler_params=pltpu.CompilerParams(vmem_limit_bytes=VMEM_LIMIT),
        name="unpack",
    )(order, outs, grads, weights, small)


def wanted_rows():
    t, c = np.arange(T), np.arange(BAND)
    small_t, small_c = t >= TL, c >= BL * WL
    at = np.where(small_t, (t - TL) % TS, t)
    wide = np.where(small_t, WS, WL)
    r, w, crop = at // wide, at % wide, np.where(small_t, (t - TL) // TS, 0)
    at_c = np.where(small_c, (c - BL * WL) % (BS * WS), c)
    slots = np.where(small_c, BS, BL)
    s_c, w_c, crop_c = at_c % slots, at_c // slots, np.where(small_c, (c - BL * WL) // (BS * WS), 0)
    same = (small_t[:, None] == small_c) & (w[:, None] == w_c) & (crop[:, None] == crop_c)
    return np.where(same, r[:, None] - s_c, -99).astype(np.int32), s_c[None].astype(np.int32)


def interp_tables():
    fold_l = np.where((np.arange(FL) == 0) | (2 * np.arange(FL) == WL), 1.0, 2.0)
    fold_s = np.where((np.arange(FS) == 0) | (2 * np.arange(FS) == WS), 1.0, 2.0)
    each = lambda n, times: np.repeat(np.eye(n), times, axis=0)
    again = lambda n, times: np.tile(np.eye(n), (times, 1))
    return [jnp.asarray(a, F32) for a in (each(HS, FS), each(HL, FL).T, again(FS, HS) * np.tile(fold_s, HS)[:, None],
                                          again(FL, HL).T, np.tile(fold_l, HL)[:, None])]


def local(mesh, large_in, small_in, large_cot, small_cot, crop_counts, band_bounds, row_interp, col_interp,
          norm1_gain, norm1_bias, filters, norm2_gain, norm2_bias, fc1_weight, fc1_bias, fc2_weight, fc2_bias):
    rows = mesh.shape["rows"]
    me = lax.axis_index("rows")
    crops = large_in.shape[0]
    groups = crops // rows
    pair = 2 if groups % 2 == 0 else 1
    tabs = tables()
    filters = filters.reshape(LAYERS, 2, NL, D)

    arrays = [a.transpose(0, 1, 3, 2, 4) for a in (large_in, small_in, large_cot, small_cot)]
    need, slot = wanted_rows()
    extras = (jnp.asarray(need), jnp.asarray(slot), row_interp, col_interp, *interp_tables())
    outs, *saved, do, place, filt_l, filt_s, mix = forward(mesh, groups, pair, arrays, crop_counts, band_bounds,
                               (filters, norm1_gain, norm1_bias, norm2_gain, norm2_bias, fc1_weight, fc1_bias, fc2_weight, fc2_bias,
                                *tabs, *extras))
    outs, grads, weights, small = backward(
        mesh, groups, pair, (place, filt_l, filt_s, norm1_gain, norm2_gain, fc1_weight, fc2_weight), tabs,
        mix, extras[-1], outs, do, saved)
    large_out, small_out, large_grad, small_grad, dw1, dw2, dfilter, dhid, *dvec = unpack(
        mesh, groups, pair, outs, grads, weights, small)
    large_out, small_out, large_grad, small_grad = (
        a.transpose(0, 1, 3, 2, 4) for a in (large_out, small_out, large_grad, small_grad))
    return (large_out, small_out, large_grad, small_grad, dvec[0], dvec[1], dfilter.reshape(LAYERS, 2, HL, FL, D), dvec[2], dvec[3],
            dw1, dhid, dw2, dvec[4])


def solution(mesh):
    split = P("batch", "rows", None, None, None)
    return jax.shard_map(partial(local, mesh), mesh=mesh, in_specs=(split,) * 4 + (P("batch", None),) + (P(),) * 12,
                         out_specs=(split,) * 4 + (P(),) * 9, check_vma=False)
```

```python
import math
from functools import partial
import numpy as np
import jax
import jax.numpy as jnp
from jax import lax
from jax.experimental import pallas as pl
from jax.experimental.pallas import tpu as pltpu
from jax.sharding import PartitionSpec as P

D, FF = 384, 1536
HL, WL, FL = 14, 14, 8
HS, WS, FS = 6, 6, 4
BL, BS = 4, 2
LAYERS = 2
EPS = 1e-6
TL, TS = HL * WL, HS * WS
PER = 3
T = TL + PER * TS
CUT, END = 192, 208
NL, NS = HL * FL, HS * FS
BAND = 96
CH = 512
CB = 512
SMALL = 512
PLAN = {
    (0, 0): [(-3, 0)],
    (0, 9): [(0, 0), (-3, 1)],
    (1, 2): [(0, 1), (-3, 2)],
    (1, 9): [(1, 0)],
    (2, 0): [(-3, 3)],
    (2, 2): [(1, 1)],
    (2, 9): [(2, 0), (-3, 4)],
    (3, 0): [(0, 2)],
    (3, 2): [(2, 1)],
    (4, 0): [(-3, 5)],
    (4, 2): [(1, 2)],
    (5, 9): [(2, 2)],
    (6, 0): [(0, 3)],
    (6, 9): [(3, 0)],
    (7, 0): [(1, 3)],
    (7, 1): [(3, 1)],
    (7, 9): [(2, 3), (4, 0)],
    (8, 2): [(4, 1)],
    (8, 9): [(0, 4), (3, 2), (5, 0)],
    (9, 2): [(5, 1), (1, 4)],
    (9, 9): [(-2, 0)],
    (10, 1): [(4, 2)],
    (10, 9): [(2, 4)],
    (11, 0): [(-2, 1)],
    (11, 1): [(0, 5)],
    (11, 9): [(-1, 0), (0, 6), (-2, 2), (3, 3), (5, 2), (-1, 1), (4, 3), (1, 5), (1, 6), (2, 5), (-1, 2), (-2, 3), (2, 6), (3, 4), (5, 3), (4, 4), (-2, 4), (3, 5), (3, 6), (-1, 3), (5, 4), (-2, 5), (4, 5), (4, 6), (-1, 4), (5, 5), (-1, 5), (5, 6), (-1, 6)],
}
MESH = pl.DeviceIdType.MESH
VMEM_LIMIT = 60 * 2**20
F32, BF16 = jnp.float32, jnp.bfloat16
HIGHEST = lax.Precision.HIGHEST


def table(height, width, count):
    k = np.arange(height)[:, None, None, None]
    l = np.arange(count)[None, :, None, None]
    s = np.arange(height)[None, None, :, None]
    w = np.arange(width)[None, None, None, :]
    phase = (k * s * width + l * w * height) % (height * width)
    angle = phase.astype(np.float32) * np.float32(2.0 * math.pi / (height * width))
    scale = np.float32(1.0 / math.sqrt(height * width))
    both = np.stack([np.cos(angle) * scale, -np.sin(angle) * scale])
    return both.reshape(2, height * count, height * width).astype(jnp.bfloat16).astype(np.float32)


def tables():
    large = np.zeros((2 * NL, END), np.float32)
    large[:, :TL] = table(HL, WL, FL).reshape(2 * NL, TL)
    one = table(HS, WS, FS)
    small = np.zeros((2, PER, NS, T - CUT), np.float32)
    for at in range(PER):
        small[:, at, :, TL - CUT + at * TS : TL - CUT + (at + 1) * TS] = one
    small = small.reshape(2 * PER * NS, T - CUT)
    return [jnp.asarray(t, BF16) for t in (large, small, large.T, small.T)]


def normal(x):
    mean = jnp.mean(x, axis=-1, keepdims=True)
    centred = x - mean
    scale = lax.rsqrt(jnp.mean(centred * centred, axis=-1, keepdims=True) + EPS)
    return centred * scale, scale


def normal_back(grad, gain, unit, scale):
    inner = grad * gain
    first = jnp.mean(inner, axis=-1, keepdims=True)
    second = jnp.mean(inner * unit, axis=-1, keepdims=True)
    return (inner - first - unit * second) * scale


def dot(a, b):
    return jnp.dot(a, b, preferred_element_type=F32)


def dot_nt(a, b):
    return lax.dot_general(a, b, (((1,), (1,)), ((), ())), preferred_element_type=F32)


def dot_tn(a, b):
    return lax.dot_general(a, b, (((0,), (0,)), ((), ())), preferred_element_type=F32)


def analyse(large_table, small_table, values):
    return dot(large_table, values[:END]), dot(small_table, values[CUT:])


def synthesise(large_back, small_back, large, small):
    a, b = dot(large_back, large), dot(small_back, small)
    return jnp.concatenate([a[:CUT], a[CUT:] + b[: END - CUT], b[END - CUT :]], axis=0)


def thrice(x):
    return jnp.concatenate([x] * PER, axis=0)


def gelu_both(h):
    cdf = 0.5 + 0.5 * lax.erf(h * np.float32(math.sqrt(0.5)))
    dens = jnp.exp(h * h * np.float32(-0.5)) * np.float32(1 / math.sqrt(2 * math.pi))
    return h * cdf, cdf + h * dens


def live_rows(counts, group):
    t = lax.broadcasted_iota(jnp.int32, (T, 1), 0)
    place, limit = jnp.full((T, 1), group), jnp.where(t < TL, counts[0, 0], counts[0, 1])
    for at in range(PER):
        place = jnp.where(t >= TL + at * TS, group * PER + at, place)
    return jnp.where(place < limit, 1.0, 0.0)


def whole(shape):
    return pl.BlockSpec(shape, lambda *a: (0,) * len(shape))


def scalars():
    return pl.BlockSpec(memory_space=pltpu.SMEM)


def forward_kernel(row_count, groups, pair, large_in, small_in, large_cot, small_cot, counts, bounds, filters, gain1, bias1, gain2, bias2,
                   w1_in, b1, w2_in, b2, tl, ts, tlb, tsb, need, slot, row_interp, col_interp, row_s, row_l, col_s, col_l, fold,
                   outs, xs, zs, both_scales, spec, vs, gs_out, ps_out, do, place, filt_l, filt_s, mix,
                   w1, w2, gs, ps, weight_sem, save_sem, pick, lined, large_slots, small_slots, own_sem, send_sem, recv_sem):
    step = pl.program_id(0)
    batch, row = lax.axis_index("batch"), lax.axis_index("rows")
    last = groups // pair - 1

    def ends(which, m, g, to):
        crop = to * groups + g
        return (((large_in, large_cot)[which].at[crop, 0], large_slots.at[which, m, g]),
                ((small_in, small_cot)[which].at[pl.ds(crop * PER, PER), 0], small_slots.at[which, m, g]))

    def remote(which, m, g):
        to = lax.rem(row + m, row_count)
        return [pltpu.make_async_remote_copy(
            src_ref=source, dst_ref=target,
            send_sem=send_sem.at[which, k, m - 1, g], recv_sem=recv_sem.at[which, k, m - 1, g],
            device_id=(batch, to), device_id_type=MESH) for k, (source, target) in enumerate(ends(which, m, g, to))]

    def mine(which, g):
        return [pltpu.make_async_copy(source, target, own_sem.at[which, k, g])
                for k, (source, target) in enumerate(ends(which, 0, g, row))]

    def weights(n):
        return [pltpu.make_async_copy(w1_in.at[n], w1.at[n], weight_sem.at[0, n]),
                pltpu.make_async_copy(w2_in.at[n], w2.at[n], weight_sem.at[1, n])]

    def keep(n, c, at):
        cols = pl.ds(c, CH)
        return [pltpu.make_async_copy(ref.at[n, :, :, cols], out.at[n, pl.ds(at * pair, pair), :, cols], save_sem.at[k, n, c // CH])
                for k, (ref, out) in enumerate(((gs, gs_out), (ps, ps_out)))]

    @pl.when(step == 0)
    def _():
        barrier = pltpu.get_barrier_semaphore()
        for m in range(1, row_count):
            pl.semaphore_signal(barrier, inc=1, device_id=(batch, lax.rem(row + m, row_count)), device_id_type=MESH)
        for which in range(2):
            @pl.loop(0, groups)
            def _(g):
                for copy in mine(which, g):
                    copy.start()
        pl.semaphore_wait(barrier, row_count - 1)
        for which in range(2):
            @pl.loop(0, groups)
            def _(g):
                for m in range(1, row_count):
                    for copy in remote(which, m, g):
                        copy.start()
        for n in range(LAYERS):
            for copy in weights(n):
                copy.start()
        lined[...] = jnp.zeros_like(lined)
        for m in range(row_count):
            band = lax.rem(row + (row_count - m), row_count)
            large = lax.broadcasted_iota(jnp.int32, (T, BAND), 0) < TL
            first = jnp.where(large, bounds[0, band], bounds[1, band])
            size = jnp.where(large, bounds[0, band + 1], bounds[1, band + 1]) - first
            hit = (need[...] == first) & (slot[...] < size)
            hit = jnp.where(hit, 1.0, 0.0)
            pick[:, m * BAND : (m + 1) * BAND] = hit.astype(BF16)
            place[m * BAND : (m + 1) * BAND, :] = hit.T.astype(BF16)
        exact = partial(jnp.dot, preferred_element_type=F32, precision=HIGHEST)
        both = exact(exact(row_s[...], row_interp[...]), row_l[...]) * exact(exact(col_s[...], col_interp[...]), col_l[...])
        mix[...] = both
        for n in range(LAYERS):
            for c in range(2):
                filt_l[n, c] = filters[n, c] * fold[...]
                filt_s[n, c] = exact(both, filters[n, c])

    def live(g):
        return live_rows(counts, row * groups + g)

    def take(which, g):
        for copy in mine(which, g):
            copy.wait()
        for m in range(1, row_count):
            for copy in remote(which, m, g):
                copy.wait_recv()
        for m in range(row_count):
            at = m * BAND
            for w in range(WL):
                lined[at + w * BL : at + (w + 1) * BL, :] = large_slots[which, m, g, w].astype(F32)
            at += BL * WL
            for p in range(PER):
                for w in range(WS):
                    row_at = at + (p * WS + w) * BS
                    lined[row_at : row_at + BS, :] = small_slots[which, m, g, p, w].astype(F32)
        return dot(pick[...], lined[...].astype(BF16))

    side = lambda parts: jnp.concatenate(parts, axis=1)
    lanes = lambda a: [a[:, j * D : (j + 1) * D] for j in range(pair)]
    x = [take(0, step * pair + j) for j in range(pair)]
    for n in range(LAYERS):
        u, scales = [], []
        for j in range(pair):
            unit, scale = normal(x[j])
            xs[n, j] = unit.astype(BF16)
            scales.append(scale)
            u.append((unit * gain1[n : n + 1] + bias1[n : n + 1]).astype(BF16))
        xl, xsm = analyse(tl[...], ts[...], side(u))
        yl, ys = [], []
        for j, (a, b) in enumerate(zip(lanes(xl), lanes(xsm))):
            spec[n, j, : 2 * NL] = a.astype(BF16)
            spec[n, j, 2 * NL :] = b.astype(BF16)
            lr, li = a[:NL], a[NL:]
            sr, si = b[: PER * NS], b[PER * NS :]
            gr, gi = filt_l[n, 0], filt_l[n, 1]
            yl.append(jnp.concatenate([lr * gr - li * gi, lr * gi + li * gr], axis=0).astype(BF16))
            gr, gi = thrice(filt_s[n, 0]), thrice(filt_s[n, 1])
            ys.append(jnp.concatenate([sr * gr - si * gi, sr * gi + si * gr], axis=0).astype(BF16))
        v = []
        for j, z in enumerate(lanes(synthesise(tlb[...], tsb[...], side(yl), side(ys)))):
            unit, scale = normal(z)
            zs[n, j] = unit.astype(BF16)
            both_scales[n, j] = side([scales[j], scale])
            unit = (unit * gain2[n : n + 1] + bias2[n : n + 1]).astype(BF16)
            vs[n, j] = unit
            v.append(unit)
        v = jnp.concatenate(v, axis=0)
        total = jnp.concatenate(x, axis=0) + b2[n : n + 1]
        @pl.when(step == 0)
        def _():
            for copy in weights(n):
                copy.wait()

        @pl.when(step > 0)
        def _():
            for c in range(0, FF, CH):
                for copy in keep(n, c, step - 1):
                    copy.wait()

        for c in range(0, FF, CH):
            h = dot(v, w1[n, :, c : c + CH]) + b1[n : n + 1, c : c + CH]
            g, slope = gelu_both(h)
            g = g.astype(BF16)
            slope = slope.astype(BF16)
            for j in range(pair):
                gs[n, j, :, c : c + CH] = g[j * T : (j + 1) * T]
                ps[n, j, :, c : c + CH] = slope[j * T : (j + 1) * T]
            for copy in keep(n, c, step):
                copy.start()
            total = total + dot(g, w2[n, c : c + CH, :])
        x = [total[j * T : (j + 1) * T] for j in range(pair)]
    for j in range(pair):
        spread = dot(place[...], (x[j] * live(step * pair + j)).astype(BF16)).astype(BF16)
        for m in range(row_count):
            outs[m, j] = spread[m * BAND : (m + 1) * BAND]

    @pl.when(step == last)
    def _():
        for g in range(groups):
            do[g] = (take(1, g) * live(g)).astype(BF16)
        for which in range(2):
            @pl.loop(0, groups)
            def _(g):
                for m in range(1, row_count):
                    for copy in remote(which, m, g):
                        copy.wait_send()
        for n in range(LAYERS):
            for c in range(0, FF, CH):
                for copy in keep(n, c, last):
                    copy.wait()


def forward(mesh, groups, pair, crops, counts, bounds, small):
    rows = mesh.shape["rows"]
    sizes = [(T, D, BF16), (T, D, BF16), (T, 2, F32), (2 * NL + 2 * PER * NS, D, BF16), (T, D, BF16), (T, FF, BF16), (T, FF, BF16)]
    extra = [((groups, T, D), BF16), ((rows * BAND, T), BF16), ((LAYERS, 2, NL, D), F32), ((LAYERS, 2, NS, D), F32), ((NS, NL), F32)]
    hbm = pl.BlockSpec(memory_space=pl.ANY)
    return pl.pallas_call(
        partial(forward_kernel, rows, groups, pair),
        grid=(groups // pair,),
        in_specs=[hbm] * 4 + [scalars(), scalars()] + [hbm if a.shape[1:] in ((D, FF), (FF, D)) else whole(a.shape) for a in small],
        out_specs=[pl.BlockSpec((rows, pair, BAND, D), lambda i: (0, i, 0, 0))]
        + [pl.BlockSpec((LAYERS, pair, a, b), lambda i: (0, i, 0, 0)) if b != FF else hbm for a, b, _ in sizes]
        + [whole(a) for a, _ in extra],
        out_shape=[jax.ShapeDtypeStruct((rows, groups, BAND, D), BF16)]
        + [jax.ShapeDtypeStruct((LAYERS, groups, a, b), t) for a, b, t in sizes]
        + [jax.ShapeDtypeStruct(a, t) for a, t in extra],
        scratch_shapes=[pltpu.VMEM((LAYERS, D, FF), BF16), pltpu.VMEM((LAYERS, FF, D), BF16)]
        + [pltpu.VMEM((LAYERS, pair, T, FF), BF16)] * 2
        + [pltpu.SemaphoreType.DMA((2, LAYERS)), pltpu.SemaphoreType.DMA((2, LAYERS, FF // CH)),
                        pltpu.VMEM((T, rows * BAND), BF16), pltpu.VMEM((rows * BAND, D), F32),
                        pltpu.VMEM((2, rows, groups, WL, BL, D), BF16), pltpu.VMEM((2, rows, groups, PER, WS, BS, D), BF16),
                        pltpu.SemaphoreType.DMA((2, 2, groups)), pltpu.SemaphoreType.DMA((2, 2, rows - 1, groups)),
                        pltpu.SemaphoreType.DMA((2, 2, rows - 1, groups))],
        compiler_params=pltpu.CompilerParams(collective_id=1, has_side_effects=True, vmem_limit_bytes=VMEM_LIMIT),
        name="forward",
    )(*crops, counts, bounds, *small)


SPREAD = True
LOW = 2


def add_rows(target, at_target, base, sources, count):
    step = next(s for s in (128, 96, 64, 48, 32, 16) if count % s == 0)

    @pl.loop(0, count // step)
    def _(i):
        at = pl.multiple_of(i * step, 16)
        rows = pl.ds(pl.multiple_of(base + at, 16), step)
        total = at_target[rows, :].astype(F32)
        for ref in sources:
            total = total + ref[pl.ds(at, step), :].astype(F32)
        target[rows, :] = total.astype(BF16)


class Sum:
    def __init__(self, mesh_rows, mesh_batch, acc, full, out, count, bufs, sems, save_sem):
        batch, row = lax.axis_index("batch"), lax.axis_index("rows")
        self.acc, self.full, self.out, self.count, self.bufs, self.sems, self.save_sem = acc, full, out, count, bufs, sems, save_sem
        self.size = kinds(mesh_rows, mesh_batch)
        self.levels = len(self.size)
        x_n = mesh_rows // 2
        core, x, z, y = lax.rem(row, 2), lax.div(row, 2), lax.div(batch, LOW), lax.rem(batch, LOW)
        self.me = [core, y, z * x_n + x] if SPREAD else [core, y, x, z]
        self.others, self.offsets, self.counts = [], [0], [count]
        for level, n in enumerate(self.size):
            count //= n
            self.counts.append(count)
            self.offsets.append(self.offsets[-1] + self.me[level] * count)
            found = []
            for step in range(1, n):
                at = lax.rem(self.me[level] + step, n)
                device = [(batch, x * 2 + at), (z * LOW + at, row)]
                device += [(lax.div(at, x_n) * LOW + y, lax.rem(at, x_n) * 2 + core)] if SPREAD else [
                    (batch, at * 2 + core), (at * LOW + y, row)]
                found.append((device[level], at))
            self.others.append(found)

    def region(self, part, level):
        return part * self.count + self.offsets[level], self.counts[level]

    def rows(self, base, count):
        return pl.ds(pl.multiple_of(base, 16), count)

    def down(self, part, level, step):
        base, count = self.region(part, level)
        device, at = self.others[level][step - 1]
        chunk = count // self.size[level]
        return pltpu.make_async_remote_copy(
            src_ref=self.acc.at[self.rows(base + at * chunk, chunk)], dst_ref=self.bufs[level].at[part, self.rows((step - 1) * chunk, chunk)],
            send_sem=self.sems[level].at[0, part], recv_sem=self.sems[level].at[1, part],
            device_id=device, device_id_type=MESH)

    def up(self, part, level, step):
        base, count = self.region(part, level + 1)
        rows = self.rows(base, count)
        return pltpu.make_async_remote_copy(
            src_ref=self.full.at[rows], dst_ref=self.full.at[rows],
            send_sem=self.sems[level].at[2, part], recv_sem=self.sems[level].at[3, part],
            device_id=self.others[level][step - 1][0], device_id_type=MESH)

    def arrived(self, part, level, sem):
        every = self.bufs[level].at[part]
        pltpu.make_async_copy(every, every, self.sems[level].at[sem, part]).wait()

    def save(self, part):
        rows = self.rows(part * self.count, self.count)
        return pltpu.make_async_copy(self.full.at[rows], self.out.at[rows], self.save_sem.at[part])

    def stage(self, part, k):
        top = self.levels
        if 1 <= k <= top:
            level = k - 1
            self.arrived(part, level, 0)
            self.arrived(part, level, 1)
            base, count = self.region(part, level + 1)
            add_rows(self.full if k == top else self.acc, self.acc, base,
                     [self.bufs[level].at[part, self.rows(s * count, count)] for s in range(self.size[level] - 1)], count)
        if k < top:
            for step in range(1, self.size[k]):
                self.down(part, k, step).start()
        if k > top:
            level = 2 * top - k
            self.arrived(part, level, 2)
            self.arrived(part, level, 3)
        if top <= k < 2 * top:
            for step in range(1, self.size[2 * top - 1 - k]):
                self.up(part, 2 * top - 1 - k, step).start()
        if k == 2 * top:
            self.save(part).start()


def kinds(mesh_rows, mesh_batch):
    x_n, z_n = mesh_rows // 2, mesh_batch // LOW
    return [2, LOW, x_n * z_n] if SPREAD else [2, LOW, x_n, z_n]


def columns(mesh_rows, mesh_batch):
    sizes = {w: w * padded(mesh_rows, mesh_batch, 2 * D * (CB // w)) for w in (256, 128)}
    return min(sizes, key=sizes.get)


def padded(mesh_rows, mesh_batch, count):
    unit = 16 * math.prod(kinds(mesh_rows, mesh_batch))
    return -(-count // unit) * unit


def sum_scratch(mesh_rows, mesh_batch, parts, count, width):
    size = kinds(mesh_rows, mesh_batch)
    shapes = [pltpu.VMEM((parts * count, width), BF16)] * 2
    for n in size:
        count //= n
        shapes.append(pltpu.VMEM((parts, (n - 1) * count, width), BF16))
    return shapes + [pltpu.SemaphoreType.DMA((4, parts)) for n in size] + [pltpu.SemaphoreType.DMA((parts,))]


def backward_kernel(row_count, batch_count, groups, pair, place, filt_l, filt_s, gain1, gain2, w1, w2, tl, ts, tlb, tsb,
                    mix, fold, outs, do_in, xs, zs, both_scales, spec, vs, gs, ps,
                    out_land, grad_land, weights_out, small_out,
                    dx, dv, do, dot_, vt, dh, gslots, dvec, dhid, dfl, dfs, out_sem, grad_sem, own_sem, *sums):
    i = pl.program_id(0)
    batch, row = lax.axis_index("batch"), lax.axis_index("rows")
    chunks, pairs = FF // CB, groups // pair
    per = chunks + pairs
    compute_steps = LAYERS * per
    layer, q = LAYERS - 1 - i // per, i % per
    width = columns(row_count, batch_count)
    part_rows = padded(row_count, batch_count, 2 * D * (CB // width))
    small_rows = padded(row_count, batch_count, SMALL)
    sums_of = []
    for out, count in ((weights_out, part_rows), (small_out, small_rows)):
        n = len(kinds(row_count, batch_count))
        sums_of.append(Sum(row_count, batch_count, sums[0], sums[1], out, count, sums[2 : 2 + n], sums[2 + n : 2 + 2 * n], sums[2 + 2 * n]))
        sums = sums[3 + 2 * n :]
    weights, small = sums_of

    def send_out(m, g):
        return pltpu.make_async_remote_copy(
            src_ref=outs.at[m, g], dst_ref=out_land.at[m, g], send_sem=out_sem.at[0, m - 1, g], recv_sem=out_sem.at[1, m - 1, g],
            device_id=(batch, lax.rem(row + (row_count - m), row_count)), device_id_type=MESH)

    def send_grad(m, g):
        return pltpu.make_async_remote_copy(
            src_ref=gslots.at[m, g], dst_ref=grad_land.at[m, g], send_sem=grad_sem.at[0, m - 1, g], recv_sem=grad_sem.at[1, m - 1, g],
            device_id=(batch, lax.rem(row + (row_count - m), row_count)), device_id_type=MESH)

    def keep_out():
        return pltpu.make_async_copy(outs.at[0], out_land.at[0], own_sem.at[0])

    def keep_grad():
        return pltpu.make_async_copy(gslots.at[0], grad_land.at[0], own_sem.at[1])

    plan = {key: [a for a in PLAN[key] if a[0] != -2 or groups == 6] for key in PLAN}
    if groups != 6:
        plan[compute_steps - 1, 9] = [(-2, g) for g in range(groups)] + plan[compute_steps - 1, 9]
    left = set(plan)

    def do_now(part, k):
        if part >= 0:
            weights.stage(part, k)
        elif part == -1:
            small.stage(0, k)
        elif k < groups:
            for m in range(1, row_count):
                (send_grad if part == -2 else send_out)(m, k).start()

    def advance(place, steps):
        for at in steps:
            found = sorted(key for key in left if key[0] == at and (key[1] == place or place == 9))
            if found:
                @pl.when(i == at)
                def _():
                    for key in found:
                        left.discard(key)
                        for part, k in plan[key]:
                            do_now(part, k)

    first_steps = [at for at in range(compute_steps) if at % per < chunks]
    second_steps = [at for at in range(compute_steps) if at % per >= chunks]

    @pl.when(i == 0)
    def _():
        barrier = pltpu.get_barrier_semaphore()
        greeted = 0
        for m in range(1, row_count):
            pl.semaphore_signal(barrier, inc=1, device_id=(batch, lax.rem(row + m, row_count)), device_id_type=MESH)
            greeted += 1
        for level in range(1, weights.levels):
            for step in range(1, weights.size[level]):
                pl.semaphore_signal(barrier, inc=1, device_id=weights.others[level][step - 1][0], device_id_type=MESH)
                greeted += 1
        keep_out().start()
        if part_rows > 2 * D * (CB // width):
            weights.acc[...] = jnp.zeros_like(weights.acc)
        for g in range(groups):
            dx[g] = do_in[g].astype(F32)
        for ref in (dvec, dfl, dfs):
            ref[...] = jnp.zeros_like(ref)
        pl.semaphore_wait(barrier, greeted)

    @pl.when((i < compute_steps) & (q == 0))
    def _():
        for g in range(groups):
            rows = pl.ds(g * T, T)
            low = dx[g].astype(BF16)
            do[g] = low
            dvec[layer, 4:5] += jnp.sum(low.astype(F32), axis=0, keepdims=True)
        dot_[...] = do[...].reshape(groups * T, D).T
        vt[:D] = vs[0].reshape(groups * T, D).T
        vt[D:] = jnp.ones((16, groups * T), BF16)
        dv[...] = jnp.zeros_like(dv)

    @pl.when((i < compute_steps) & (q < chunks))
    def _():
        for g in range(0, groups, pair):
            rows = slice(g * T, (g + pair) * T)
            some = do[g : g + pair].reshape(pair * T, D)
            slope = ps[0, g : g + pair].reshape(pair * T, CB)
            part = (dot_nt(some, w2[0]) * slope.astype(F32)).astype(BF16)
            dh[rows] = part
            dv[g : g + pair] += dot_nt(part, w1[0]).reshape(pair, T, D)
            advance(g // pair, first_steps)
        part = (LAYERS - 1 - layer) * chunks + q
        base = part * part_rows
        one = dot(vt[...], dh[...])
        dhid[layer, :, pl.ds(pl.multiple_of(q * CB, CB), CB)] = one[D : D + 1]
        two = dot(dot_[...], gs[0].reshape(groups * T, CB))
        for c in range(CB // width):
            cols = slice(c * width, (c + 1) * width)
            weights.acc[weights.rows(base + c * D, D), :] = one[:D, cols].astype(BF16)
            weights.acc[weights.rows(base + (CB // width + c) * D, D), :] = two[:, cols].astype(BF16)

    @pl.when((i < compute_steps) & (q >= chunks))
    def _():
        side = lambda parts: jnp.concatenate(parts, axis=1)
        lanes = lambda a: [a[:, j * D : (j + 1) * D] for j in range(pair)]
        row_sum = lambda a: jnp.sum(a, axis=0, keepdims=True)
        first = (q - chunks) * pair
        dz = []
        for j in range(pair):
            dvg = dv[first + j]
            unit = zs[0, j].astype(F32)
            dvec[layer, 2:3] += row_sum(dvg * unit)
            dvec[layer, 3:4] += row_sum(dvg)
            dz.append(normal_back(dvg, gain2[pl.ds(layer, 1)], unit, both_scales[0, j, :, 1:2]).astype(BF16))
        advance(0, second_steps)
        yl, ysm = analyse(tl[...], ts[...], side(dz))
        dl, ds = [], []
        for j, (a, b) in enumerate(zip(lanes(yl), lanes(ysm))):
            lr, li = a[:NL], a[NL:]
            sr, si = b[: PER * NS], b[PER * NS :]
            xr, xi = spec[0, j, :NL].astype(F32), spec[0, j, NL : 2 * NL].astype(F32)
            dfl[layer, :NL] += lr * xr + li * xi
            dfl[layer, NL:] += li * xr - lr * xi
            gr, gi = filt_l[0, 0], filt_l[0, 1]
            dl.append(jnp.concatenate([lr * gr + li * gi, li * gr - lr * gi], axis=0).astype(BF16))
            small_spec = spec[0, j, 2 * NL :].astype(F32)
            xr, xi = small_spec[: PER * NS], small_spec[PER * NS :]
            once = lambda a: a[:NS] + a[NS : 2 * NS] + a[2 * NS :]
            dfs[layer, :NS] += once(sr * xr + si * xi)
            dfs[layer, NS:] += once(si * xr - sr * xi)
            gr, gi = thrice(filt_s[0, 0]), thrice(filt_s[0, 1])
            ds.append(jnp.concatenate([sr * gr + si * gi, si * gr - sr * gi], axis=0).astype(BF16))
        advance(1, second_steps)
        grads = []
        for j, du in enumerate(lanes(synthesise(tlb[...], tsb[...], side(dl), side(ds)))):
            unit = xs[0, j].astype(F32)
            dvec[layer, 0:1] += row_sum(du * unit)
            dvec[layer, 1:2] += row_sum(du)
            grad = dx[first + j] + normal_back(du, gain1[pl.ds(layer, 1)], unit, both_scales[0, j, :, 0:1])
            dx[first + j] = grad
            grads.append(grad.astype(BF16))
        advance(2, second_steps)

        @pl.when(layer == 0)
        def _():
            spread = dot(place[...], side(grads)).astype(BF16)
            for j in range(pair):
                for m in range(row_count):
                    gslots[m, first + j] = spread[m * BAND : (m + 1) * BAND, j * D : (j + 1) * D]

    @pl.when(i == compute_steps - 1)
    def _():
        small.acc[...] = jnp.zeros_like(small.acc)
        exact = partial(jnp.dot, preferred_element_type=F32, precision=HIGHEST)
        mix_t = mix[...].T
        for n in range(LAYERS):
            for c in range(2):
                at = (n * 2 + c) * NL
                small.acc[at : at + NL, :] = (dfl[n, c * NL : (c + 1) * NL] * fold[...]
                                              + exact(mix_t, dfs[n, c * NS : (c + 1) * NS])).astype(BF16)
        at = LAYERS * 2 * NL
        rest = [dvec[n, k : k + 1] for n in range(LAYERS) for k in range(5)]
        rest += [dhid[n, :, c : c + D] for n in range(LAYERS) for c in range(0, FF, D)]
        rest.append(jnp.zeros((-len(rest) % 16, D), F32))
        rest = jnp.concatenate(rest, axis=0).astype(BF16)
        small.acc[at : at + rest.shape[0], :] = rest
        keep_grad().start()

    advance(9, range(compute_steps))

    @pl.when(i == pl.num_programs(0) - 1)
    def _():
        keep_out().wait()
        keep_grad().wait()
        for m in range(1, row_count):
            @pl.loop(0, groups)
            def _(g):
                send_out(m, g).wait()
                send_grad(m, g).wait()
        for part in range(LAYERS * chunks):
            weights.save(part).wait()
        small.save(0).wait()


def backward(mesh, groups, pair, small, tabs, mix, fold, outs, do, saved):
    rows, batch = mesh.shape["rows"], mesh.shape["batch"]
    place, filt_l, filt_s, gain1, gain2, w1, w2 = small
    chunks, pairs = FF // CB, groups // pair
    per, last = chunks + pairs, LAYERS - 1
    steps = LAYERS * per
    layer = lambda i: jnp.maximum(last - i // per, 0)
    when = lambda i: jnp.where(i < LAYERS * per, i % per, per - 1)
    chunk = lambda i: jnp.minimum(when(i), chunks - 1)
    place_of = lambda i: jnp.maximum(when(i) - chunks, 0)
    per_layer = lambda a: pl.BlockSpec((1,) + a.shape[1:], lambda i: (layer(i),) + (0,) * (a.ndim - 1))
    by_pair = lambda a: pl.BlockSpec((1, pair) + a.shape[2:], lambda i: (layer(i), place_of(i), 0, 0))
    by_chunk = lambda a: pl.BlockSpec((1, groups, T, CB), lambda i: (layer(i), 0, 0, chunk(i)))
    xs, zs, scales, spec, vs, gs, ps = saved
    hbm = pl.BlockSpec(memory_space=pl.ANY)
    width = columns(rows, batch)
    part_rows, small_rows = padded(rows, batch, 2 * D * (CB // width)), padded(rows, batch, SMALL)
    dma = pltpu.SemaphoreType.DMA
    return pl.pallas_call(
        partial(backward_kernel, rows, batch, groups, pair),
        grid=(steps,),
        in_specs=[whole(place.shape), per_layer(filt_l), per_layer(filt_s), whole(gain1.shape), whole(gain2.shape)]
        + [pl.BlockSpec((1, D, CB), lambda i: (layer(i), 0, chunk(i))), pl.BlockSpec((1, CB, D), lambda i: (layer(i), chunk(i), 0))]
        + [whole(a.shape) for a in (*tabs, mix, fold)] + [hbm, whole(do.shape)]
        + [by_pair(xs), by_pair(zs), by_pair(scales), by_pair(spec), per_layer(vs), by_chunk(gs), by_chunk(ps)],
        out_specs=[hbm] * 4,
        out_shape=[jax.ShapeDtypeStruct((rows, groups, BAND, D), BF16)] * 2
        + [jax.ShapeDtypeStruct((LAYERS * chunks * part_rows, width), BF16), jax.ShapeDtypeStruct((small_rows, D), BF16)],
        scratch_shapes=[pltpu.VMEM((groups, T, D), F32), pltpu.VMEM((groups, T, D), F32), pltpu.VMEM((groups, T, D), BF16),
                        pltpu.VMEM((D, groups * T), BF16), pltpu.VMEM((D + 16, groups * T), BF16),
                        pltpu.VMEM((groups * T, CB), BF16), pltpu.VMEM((rows, groups, BAND, D), BF16),
                        pltpu.VMEM((LAYERS, 5, D), F32), pltpu.VMEM((LAYERS, 1, FF), F32),
                        pltpu.VMEM((LAYERS, 2 * NL, D), F32), pltpu.VMEM((LAYERS, 2 * NS, D), F32),
                        dma((2, rows - 1, groups)), dma((2, rows - 1, groups)), dma((2,))]
        + sum_scratch(rows, batch, LAYERS * chunks, part_rows, width) + sum_scratch(rows, batch, 1, small_rows, D),
        compiler_params=pltpu.CompilerParams(collective_id=2, has_side_effects=True, vmem_limit_bytes=VMEM_LIMIT),
        name="backward",
    )(place, filt_l, filt_s, gain1, gain2, w1, w2, *tabs, mix, fold, outs, do, xs, zs, scales, spec, vs, gs, ps)


def unpack_kernel(groups, order, outs, grads, weights, small, large_out, small_crops, large_grad, small_grad, dw1, dw2, dfilter, dhid,
                  *rest):
    dvec, rest = rest[:5], rest[5:]
    given, weight, large, little, one, two, in_sem, weight_sem, out_sem, done_sem = rest
    rows = outs.shape[0]
    parts, chunks, width = weight.shape[0], FF // CB, weight.shape[2]
    halves = CB // width

    def read(dev, kind):
        return pltpu.make_async_copy((outs, grads)[kind].at[order[dev]], given.at[kind, dev], in_sem.at[kind, dev])

    def read_weight(part):
        return pltpu.make_async_copy(weights.at[part], weight.at[part], weight_sem.at[part])

    def write(dev, kind):
        to_large, to_little = ((large_out, small_crops), (large_grad, small_grad))[kind]
        return (pltpu.make_async_copy(large.at[kind, dev], to_large.at[pl.ds(dev * groups, groups)], out_sem.at[kind, 0, dev]),
                pltpu.make_async_copy(little.at[kind, dev], to_little.at[pl.ds(dev * groups * PER, groups * PER)], out_sem.at[kind, 1, dev]))

    def write_weight(part):
        layer, at = LAYERS - 1 - part // chunks, part % chunks * CB
        return (pltpu.make_async_copy(one.at[part], dw1.at[layer, :, pl.ds(at, CB)], done_sem.at[0, part]),
                pltpu.make_async_copy(two.at[part], dw2.at[layer, pl.ds(at, CB)], done_sem.at[1, part]))

    for part in range(parts):
        read_weight(part).start()
    for dev in range(rows):
        for kind in range(2):
            read(dev, kind).start()
    for part in range(parts):
        read_weight(part).wait()
        for c in range(halves):
            cols = slice(c * width, (c + 1) * width)
            one[part, :, cols] = weight[part, c * D : (c + 1) * D].astype(F32)
            two[part, cols] = weight[part, (halves + c) * D : (halves + c + 1) * D].astype(F32).T
        for copy in write_weight(part):
            copy.start()
    for dev in range(rows):
        for kind in range(2):
            read(dev, kind).wait()

            @pl.loop(0, groups)
            def _(g):
                block = given[kind, dev, g].astype(F32)
                for w in range(WL):
                    large[kind, dev, g, 0, w] = block[w * BL : (w + 1) * BL]
                for p in range(PER):
                    for w in range(WS):
                        at = BL * WL + (p * WS + w) * BS
                        little[kind, dev, g * PER + p, 0, w] = block[at : at + BS]

            for copy in write(dev, kind):
                copy.start()
    at = LAYERS * 2 * NL
    for n in range(LAYERS):
        for c in range(2):
            dfilter[n, c] = small[(n * 2 + c) * NL : (n * 2 + c + 1) * NL].astype(F32)
    others = small[at : at + 32].astype(F32)
    for n in range(LAYERS):
        for k in range(5):
            dvec[k][n : n + 1] = others[n * 5 + k : n * 5 + k + 1]
        for c in range(FF // D):
            r = LAYERS * 5 + n * (FF // D) + c
            dhid[n : n + 1, c * D : (c + 1) * D] = others[r : r + 1]
    for part in range(parts):
        for copy in write_weight(part):
            copy.wait()
    for dev in range(rows):
        for kind in range(2):
            for copy in write(dev, kind):
                copy.wait()


def unpack(mesh, groups, pair, outs, grads, weights, small):
    rows = mesh.shape["rows"]
    me = lax.axis_index("rows")
    crops = rows * groups
    width = weights.shape[1]
    halves = CB // width
    parts = LAYERS * (FF // CB)
    weights = weights.reshape(parts, -1, width)[:, : 2 * D * halves]
    order = lax.rem(jnp.arange(rows, dtype=jnp.int32) + (rows - me), rows)
    large_shape, little_shape = (crops, 1, WL, BL, D), (crops * PER, 1, WS, BS, D)
    shapes = [(LAYERS, 2, NL, D), (LAYERS, FF)] + [(LAYERS, D)] * 5
    hbm, vmem, dma = pl.BlockSpec(memory_space=pl.ANY), pl.BlockSpec(memory_space=pltpu.VMEM), pltpu.SemaphoreType.DMA
    return pl.pallas_call(
        partial(unpack_kernel, groups),
        in_specs=[scalars()] + [hbm] * 3 + [vmem],
        out_specs=[hbm] * 6 + [vmem] * len(shapes),
        out_shape=[jax.ShapeDtypeStruct(s, F32) for s in [large_shape, little_shape] * 2 + [(LAYERS, D, FF), (LAYERS, FF, D)] + shapes],
        scratch_shapes=[pltpu.VMEM((2, rows, groups, BAND, D), BF16), pltpu.VMEM(weights.shape, BF16),
                        pltpu.VMEM((2, rows, groups, 1, WL, BL, D), F32), pltpu.VMEM((2, rows, groups * PER, 1, WS, BS, D), F32),
                        pltpu.VMEM((parts, D, CB), F32), pltpu.VMEM((parts, CB, D), F32),
                        dma((2, rows)), dma((parts,)), dma((2, 2, rows)), dma((2, parts))],
        compiler_params=pltpu.CompilerParams(vmem_limit_bytes=VMEM_LIMIT),
        name="unpack",
    )(order, outs, grads, weights, small)


def wanted_rows():
    t, c = np.arange(T), np.arange(BAND)
    small_t, small_c = t >= TL, c >= BL * WL
    at = np.where(small_t, (t - TL) % TS, t)
    wide = np.where(small_t, WS, WL)
    r, w, crop = at // wide, at % wide, np.where(small_t, (t - TL) // TS, 0)
    at_c = np.where(small_c, (c - BL * WL) % (BS * WS), c)
    slots = np.where(small_c, BS, BL)
    s_c, w_c, crop_c = at_c % slots, at_c // slots, np.where(small_c, (c - BL * WL) // (BS * WS), 0)
    same = (small_t[:, None] == small_c) & (w[:, None] == w_c) & (crop[:, None] == crop_c)
    return np.where(same, r[:, None] - s_c, -99).astype(np.int32), s_c[None].astype(np.int32)


def interp_tables():
    fold_l = np.where((np.arange(FL) == 0) | (2 * np.arange(FL) == WL), 1.0, 2.0)
    fold_s = np.where((np.arange(FS) == 0) | (2 * np.arange(FS) == WS), 1.0, 2.0)
    each = lambda n, times: np.repeat(np.eye(n), times, axis=0)
    again = lambda n, times: np.tile(np.eye(n), (times, 1))
    return [jnp.asarray(a, F32) for a in (each(HS, FS), each(HL, FL).T, again(FS, HS) * np.tile(fold_s, HS)[:, None],
                                          again(FL, HL).T, np.tile(fold_l, HL)[:, None])]


def local(mesh, large_in, small_in, large_cot, small_cot, crop_counts, band_bounds, row_interp, col_interp,
          norm1_gain, norm1_bias, filters, norm2_gain, norm2_bias, fc1_weight, fc1_bias, fc2_weight, fc2_bias):
    rows = mesh.shape["rows"]
    me = lax.axis_index("rows")
    crops = large_in.shape[0]
    groups = crops // rows
    pair = 2 if groups % 2 == 0 else 1
    tabs = tables()
    filters = filters.reshape(LAYERS, 2, NL, D)

    arrays = [a.transpose(0, 1, 3, 2, 4) for a in (large_in, small_in, large_cot, small_cot)]
    need, slot = wanted_rows()
    extras = (jnp.asarray(need), jnp.asarray(slot), row_interp, col_interp, *interp_tables())
    outs, *saved, do, place, filt_l, filt_s, mix = forward(mesh, groups, pair, arrays, crop_counts, band_bounds,
                               (filters, norm1_gain, norm1_bias, norm2_gain, norm2_bias, fc1_weight, fc1_bias, fc2_weight, fc2_bias,
                                *tabs, *extras))
    outs, grads, weights, small = backward(
        mesh, groups, pair, (place, filt_l, filt_s, norm1_gain, norm2_gain, fc1_weight, fc2_weight), tabs,
        mix, extras[-1], outs, do, saved)
    large_out, small_out, large_grad, small_grad, dw1, dw2, dfilter, dhid, *dvec = unpack(
        mesh, groups, pair, outs, grads, weights, small)
    large_out, small_out, large_grad, small_grad = (
        a.transpose(0, 1, 3, 2, 4) for a in (large_out, small_out, large_grad, small_grad))
    return (large_out, small_out, large_grad, small_grad, dvec[0], dvec[1], dfilter.reshape(LAYERS, 2, HL, FL, D), dvec[2], dvec[3],
            dw1, dhid, dw2, dvec[4])


def solution(mesh):
    split = P("batch", "rows", None, None, None)
    return jax.shard_map(partial(local, mesh), mesh=mesh, in_specs=(split,) * 4 + (P("batch", None),) + (P(),) * 12,
                         out_specs=(split,) * 4 + (P(),) * 9, check_vma=False)
```

```python
import math
from functools import partial
import numpy as np
import jax
import jax.numpy as jnp
from jax import lax
from jax.experimental import pallas as pl
from jax.experimental.pallas import tpu as pltpu
from jax.sharding import PartitionSpec as P

D, FF = 384, 1536
HL, WL, FL = 14, 14, 8
HS, WS, FS = 6, 6, 4
BL, BS = 4, 2
LAYERS = 2
EPS = 1e-6
TL, TS = HL * WL, HS * WS
PER = 3
T = TL + PER * TS
CUT, END = 192, 208
NL, NS = HL * FL, HS * FS
BAND = 96
CH = 512
CB = 512
SMALL = 512
PLAN = {
    (0, 0): [(-3, 0)],
    (0, 3): [(0, 0), (-3, 1)],
    (1, 1): [(0, 1), (-3, 2)],
    (1, 3): [(1, 0)],
    (1, 9): [(-3, 3)],
    (2, 1): [(1, 1)],
    (2, 3): [(0, 2), (2, 0)],
    (2, 9): [(-3, 4)],
    (3, 1): [(2, 1)],
    (3, 9): [(-3, 5)],
    (4, 0): [(1, 2)],
    (5, 2): [(0, 3), (2, 2)],
    (6, 3): [(3, 0)],
    (6, 9): [(1, 3)],
    (7, 1): [(3, 1)],
    (7, 3): [(0, 4), (4, 0)],
    (8, 1): [(4, 1)],
    (8, 3): [(2, 3), (3, 2), (5, 0)],
    (9, 1): [(5, 1)],
    (9, 2): [(1, 4), (0, 5)],
    (9, 9): [(-2, 0)],
    (10, 1): [(0, 6), (4, 2)],
    (11, 0): [(-2, 1)],
    (11, 1): [(2, 4)],
    (11, 2): [(5, 2)],
    (11, 9): [(-1, 0), (1, 5), (-1, 1), (3, 3), (1, 6), (2, 5), (-2, 2), (4, 3), (-1, 2), (2, 6), (5, 3), (3, 4), (-2, 3), (4, 4), (-2, 4), (-1, 3), (3, 5), (3, 6), (-2, 5), (5, 4), (4, 5), (4, 6), (-1, 4), (5, 5), (-1, 5), (5, 6), (-1, 6)],
}
MESH = pl.DeviceIdType.MESH
VMEM_LIMIT = 60 * 2**20
F32, BF16 = jnp.float32, jnp.bfloat16
HIGHEST = lax.Precision.HIGHEST


def table(height, width, count):
    k = np.arange(height)[:, None, None, None]
    l = np.arange(count)[None, :, None, None]
    s = np.arange(height)[None, None, :, None]
    w = np.arange(width)[None, None, None, :]
    phase = (k * s * width + l * w * height) % (height * width)
    angle = phase.astype(np.float32) * np.float32(2.0 * math.pi / (height * width))
    scale = np.float32(1.0 / math.sqrt(height * width))
    both = np.stack([np.cos(angle) * scale, -np.sin(angle) * scale])
    return both.reshape(2, height * count, height * width).astype(jnp.bfloat16).astype(np.float32)


def tables():
    large = np.zeros((2 * NL, END), np.float32)
    large[:, :TL] = table(HL, WL, FL).reshape(2 * NL, TL)
    one = table(HS, WS, FS)
    small = np.zeros((2, PER, NS, T - CUT), np.float32)
    for at in range(PER):
        small[:, at, :, TL - CUT + at * TS : TL - CUT + (at + 1) * TS] = one
    small = small.reshape(2 * PER * NS, T - CUT)
    return [jnp.asarray(t, BF16) for t in (large, small, large.T, small.T)]


def normal(x):
    mean = jnp.mean(x, axis=-1, keepdims=True)
    centred = x - mean
    scale = lax.rsqrt(jnp.mean(centred * centred, axis=-1, keepdims=True) + EPS)
    return centred * scale, scale


def normal_back(grad, gain, unit, scale):
    inner = grad * gain
    first = jnp.mean(inner, axis=-1, keepdims=True)
    second = jnp.mean(inner * unit, axis=-1, keepdims=True)
    return (inner - first - unit * second) * scale


def dot(a, b):
    return jnp.dot(a, b, preferred_element_type=F32)


def dot_nt(a, b):
    return lax.dot_general(a, b, (((1,), (1,)), ((), ())), preferred_element_type=F32)


def dot_tn(a, b):
    return lax.dot_general(a, b, (((0,), (0,)), ((), ())), preferred_element_type=F32)


def analyse(large_table, small_table, values):
    return dot(large_table, values[:END]), dot(small_table, values[CUT:])


def synthesise(large_back, small_back, large, small):
    a, b = dot(large_back, large), dot(small_back, small)
    return jnp.concatenate([a[:CUT], a[CUT:] + b[: END - CUT], b[END - CUT :]], axis=0)


def thrice(x):
    return jnp.concatenate([x] * PER, axis=0)


def gelu_both(h):
    cdf = 0.5 + 0.5 * lax.erf(h * np.float32(math.sqrt(0.5)))
    dens = jnp.exp(h * h * np.float32(-0.5)) * np.float32(1 / math.sqrt(2 * math.pi))
    return h * cdf, cdf + h * dens


def live_rows(counts, group):
    t = lax.broadcasted_iota(jnp.int32, (T, 1), 0)
    place, limit = jnp.full((T, 1), group), jnp.where(t < TL, counts[0, 0], counts[0, 1])
    for at in range(PER):
        place = jnp.where(t >= TL + at * TS, group * PER + at, place)
    return jnp.where(place < limit, 1.0, 0.0)


def whole(shape):
    return pl.BlockSpec(shape, lambda *a: (0,) * len(shape))


def scalars():
    return pl.BlockSpec(memory_space=pltpu.SMEM)


def forward_kernel(row_count, groups, pair, large_in, small_in, large_cot, small_cot, counts, bounds, filters, gain1, bias1, gain2, bias2,
                   w1_in, b1, w2_in, b2, tl, ts, tlb, tsb, need, slot, row_interp, col_interp, row_s, row_l, col_s, col_l, fold,
                   outs, xs, zs, both_scales, spec, vs, gs_out, ps_out, do, place, filt_l, filt_s, mix,
                   w1, w2, gs, ps, weight_sem, save_sem, pick, lined, large_slots, small_slots, own_sem, send_sem, recv_sem):
    step = pl.program_id(0)
    batch, row = lax.axis_index("batch"), lax.axis_index("rows")
    last = groups // pair - 1

    def ends(which, m, g, to):
        crop = to * groups + g
        return (((large_in, large_cot)[which].at[crop, 0], large_slots.at[which, m, g]),
                ((small_in, small_cot)[which].at[pl.ds(crop * PER, PER), 0], small_slots.at[which, m, g]))

    def remote(which, m, g):
        to = lax.rem(row + m, row_count)
        return [pltpu.make_async_remote_copy(
            src_ref=source, dst_ref=target,
            send_sem=send_sem.at[which, k, m - 1, g], recv_sem=recv_sem.at[which, k, m - 1, g],
            device_id=(batch, to), device_id_type=MESH) for k, (source, target) in enumerate(ends(which, m, g, to))]

    def mine(which, g):
        return [pltpu.make_async_copy(source, target, own_sem.at[which, k, g])
                for k, (source, target) in enumerate(ends(which, 0, g, row))]

    def weights(n):
        return [pltpu.make_async_copy(w1_in.at[n], w1.at[n], weight_sem.at[0, n]),
                pltpu.make_async_copy(w2_in.at[n], w2.at[n], weight_sem.at[1, n])]

    def keep(n, c, at):
        cols = pl.ds(c, CH)
        return [pltpu.make_async_copy(ref.at[n, :, :, cols], out.at[n, pl.ds(at * pair, pair), :, cols], save_sem.at[k, n, c // CH])
                for k, (ref, out) in enumerate(((gs, gs_out), (ps, ps_out)))]

    @pl.when(step == 0)
    def _():
        barrier = pltpu.get_barrier_semaphore()
        for m in range(1, row_count):
            pl.semaphore_signal(barrier, inc=1, device_id=(batch, lax.rem(row + m, row_count)), device_id_type=MESH)
        for which in range(2):
            @pl.loop(0, groups)
            def _(g):
                for copy in mine(which, g):
                    copy.start()
        pl.semaphore_wait(barrier, row_count - 1)
        for which in range(2):
            @pl.loop(0, groups)
            def _(g):
                for m in range(1, row_count):
                    for copy in remote(which, m, g):
                        copy.start()
        for n in range(LAYERS):
            for copy in weights(n):
                copy.start()
        lined[...] = jnp.zeros_like(lined)
        for m in range(row_count):
            band = lax.rem(row + (row_count - m), row_count)
            large = lax.broadcasted_iota(jnp.int32, (T, BAND), 0) < TL
            first = jnp.where(large, bounds[0, band], bounds[1, band])
            size = jnp.where(large, bounds[0, band + 1], bounds[1, band + 1]) - first
            hit = (need[...] == first) & (slot[...] < size)
            hit = jnp.where(hit, 1.0, 0.0)
            pick[:, m * BAND : (m + 1) * BAND] = hit.astype(BF16)
            place[m * BAND : (m + 1) * BAND, :] = hit.T.astype(BF16)
        exact = partial(jnp.dot, preferred_element_type=F32, precision=HIGHEST)
        both = exact(exact(row_s[...], row_interp[...]), row_l[...]) * exact(exact(col_s[...], col_interp[...]), col_l[...])
        mix[...] = both
        for n in range(LAYERS):
            for c in range(2):
                filt_l[n, c] = filters[n, c] * fold[...]
                filt_s[n, c] = exact(both, filters[n, c])

    def live(g):
        return live_rows(counts, row * groups + g)

    def take(which, g):
        for copy in mine(which, g):
            copy.wait()
        for m in range(1, row_count):
            for copy in remote(which, m, g):
                copy.wait_recv()
        for m in range(row_count):
            at = m * BAND
            for w in range(WL):
                lined[at + w * BL : at + (w + 1) * BL, :] = large_slots[which, m, g, w].astype(F32)
            at += BL * WL
            for p in range(PER):
                for w in range(WS):
                    row_at = at + (p * WS + w) * BS
                    lined[row_at : row_at + BS, :] = small_slots[which, m, g, p, w].astype(F32)
        return dot(pick[...], lined[...].astype(BF16))

    side = lambda parts: jnp.concatenate(parts, axis=1)
    lanes = lambda a: [a[:, j * D : (j + 1) * D] for j in range(pair)]
    x = [take(0, step * pair + j) for j in range(pair)]
    for n in range(LAYERS):
        u, scales = [], []
        for j in range(pair):
            unit, scale = normal(x[j])
            xs[n, j] = unit.astype(BF16)
            scales.append(scale)
            u.append((unit * gain1[n : n + 1] + bias1[n : n + 1]).astype(BF16))
        xl, xsm = analyse(tl[...], ts[...], side(u))
        yl, ys = [], []
        for j, (a, b) in enumerate(zip(lanes(xl), lanes(xsm))):
            spec[n, j, : 2 * NL] = a.astype(BF16)
            spec[n, j, 2 * NL :] = b.astype(BF16)
            lr, li = a[:NL], a[NL:]
            sr, si = b[: PER * NS], b[PER * NS :]
            gr, gi = filt_l[n, 0], filt_l[n, 1]
            yl.append(jnp.concatenate([lr * gr - li * gi, lr * gi + li * gr], axis=0).astype(BF16))
            gr, gi = thrice(filt_s[n, 0]), thrice(filt_s[n, 1])
            ys.append(jnp.concatenate([sr * gr - si * gi, sr * gi + si * gr], axis=0).astype(BF16))
        v = []
        for j, z in enumerate(lanes(synthesise(tlb[...], tsb[...], side(yl), side(ys)))):
            unit, scale = normal(z)
            zs[n, j] = unit.astype(BF16)
            both_scales[n, j] = side([scales[j], scale])
            unit = (unit * gain2[n : n + 1] + bias2[n : n + 1]).astype(BF16)
            vs[n, j] = unit
            v.append(unit)
        v = jnp.concatenate(v, axis=0)
        total = jnp.concatenate(x, axis=0) + b2[n : n + 1]
        @pl.when(step == 0)
        def _():
            for copy in weights(n):
                copy.wait()

        @pl.when(step > 0)
        def _():
            for c in range(0, FF, CH):
                for copy in keep(n, c, step - 1):
                    copy.wait()

        for c in range(0, FF, CH):
            h = dot(v, w1[n, :, c : c + CH]) + b1[n : n + 1, c : c + CH]
            g, slope = gelu_both(h)
            g = g.astype(BF16)
            slope = slope.astype(BF16)
            for j in range(pair):
                gs[n, j, :, c : c + CH] = g[j * T : (j + 1) * T]
                ps[n, j, :, c : c + CH] = slope[j * T : (j + 1) * T]
            for copy in keep(n, c, step):
                copy.start()
            total = total + dot(g, w2[n, c : c + CH, :])
        x = [total[j * T : (j + 1) * T] for j in range(pair)]
    for j in range(pair):
        spread = dot(place[...], (x[j] * live(step * pair + j)).astype(BF16)).astype(BF16)
        for m in range(row_count):
            outs[m, j] = spread[m * BAND : (m + 1) * BAND]

    @pl.when(step == last)
    def _():
        for g in range(groups):
            do[g] = (take(1, g) * live(g)).astype(BF16)
        for which in range(2):
            @pl.loop(0, groups)
            def _(g):
                for m in range(1, row_count):
                    for copy in remote(which, m, g):
                        copy.wait_send()
        for n in range(LAYERS):
            for c in range(0, FF, CH):
                for copy in keep(n, c, last):
                    copy.wait()


def forward(mesh, groups, pair, crops, counts, bounds, small):
    rows = mesh.shape["rows"]
    sizes = [(T, D, BF16), (T, D, BF16), (T, 2, F32), (2 * NL + 2 * PER * NS, D, BF16), (T, D, BF16), (T, FF, BF16), (T, FF, BF16)]
    extra = [((groups, T, D), BF16), ((rows * BAND, T), BF16), ((LAYERS, 2, NL, D), F32), ((LAYERS, 2, NS, D), F32), ((NS, NL), F32)]
    hbm = pl.BlockSpec(memory_space=pl.ANY)
    return pl.pallas_call(
        partial(forward_kernel, rows, groups, pair),
        grid=(groups // pair,),
        in_specs=[hbm] * 4 + [scalars(), scalars()] + [hbm if a.shape[1:] in ((D, FF), (FF, D)) else whole(a.shape) for a in small],
        out_specs=[pl.BlockSpec((rows, pair, BAND, D), lambda i: (0, i, 0, 0))]
        + [pl.BlockSpec((LAYERS, pair, a, b), lambda i: (0, i, 0, 0)) if b != FF else hbm for a, b, _ in sizes]
        + [whole(a) for a, _ in extra],
        out_shape=[jax.ShapeDtypeStruct((rows, groups, BAND, D), BF16)]
        + [jax.ShapeDtypeStruct((LAYERS, groups, a, b), t) for a, b, t in sizes]
        + [jax.ShapeDtypeStruct(a, t) for a, t in extra],
        scratch_shapes=[pltpu.VMEM((LAYERS, D, FF), BF16), pltpu.VMEM((LAYERS, FF, D), BF16)]
        + [pltpu.VMEM((LAYERS, pair, T, FF), BF16)] * 2
        + [pltpu.SemaphoreType.DMA((2, LAYERS)), pltpu.SemaphoreType.DMA((2, LAYERS, FF // CH)),
                        pltpu.VMEM((T, rows * BAND), BF16), pltpu.VMEM((rows * BAND, D), F32),
                        pltpu.VMEM((2, rows, groups, WL, BL, D), BF16), pltpu.VMEM((2, rows, groups, PER, WS, BS, D), BF16),
                        pltpu.SemaphoreType.DMA((2, 2, groups)), pltpu.SemaphoreType.DMA((2, 2, rows - 1, groups)),
                        pltpu.SemaphoreType.DMA((2, 2, rows - 1, groups))],
        compiler_params=pltpu.CompilerParams(collective_id=1, has_side_effects=True, vmem_limit_bytes=VMEM_LIMIT),
        name="forward",
    )(*crops, counts, bounds, *small)


SPREAD = True
LOW = 2


def add_rows(target, at_target, base, sources, count):
    step = next(s for s in (128, 96, 64, 48, 32, 16) if count % s == 0)

    @pl.loop(0, count // step)
    def _(i):
        at = pl.multiple_of(i * step, 16)
        rows = pl.ds(pl.multiple_of(base + at, 16), step)
        total = at_target[rows, :].astype(F32)
        for ref in sources:
            total = total + ref[pl.ds(at, step), :].astype(F32)
        target[rows, :] = total.astype(BF16)


class Sum:
    def __init__(self, mesh_rows, mesh_batch, acc, full, out, count, bufs, sems, save_sem):
        batch, row = lax.axis_index("batch"), lax.axis_index("rows")
        self.acc, self.full, self.out, self.count, self.bufs, self.sems, self.save_sem = acc, full, out, count, bufs, sems, save_sem
        self.size = kinds(mesh_rows, mesh_batch)
        self.levels = len(self.size)
        x_n = mesh_rows // 2
        core, x, z, y = lax.rem(row, 2), lax.div(row, 2), lax.div(batch, LOW), lax.rem(batch, LOW)
        self.me = [core, y, z * x_n + x] if SPREAD else [core, y, x, z]
        self.others, self.offsets, self.counts = [], [0], [count]
        for level, n in enumerate(self.size):
            count //= n
            self.counts.append(count)
            self.offsets.append(self.offsets[-1] + self.me[level] * count)
            found = []
            for step in range(1, n):
                at = lax.rem(self.me[level] + step, n)
                device = [(batch, x * 2 + at), (z * LOW + at, row)]
                device += [(lax.div(at, x_n) * LOW + y, lax.rem(at, x_n) * 2 + core)] if SPREAD else [
                    (batch, at * 2 + core), (at * LOW + y, row)]
                found.append((device[level], at))
            self.others.append(found)

    def region(self, part, level):
        return part * self.count + self.offsets[level], self.counts[level]

    def rows(self, base, count):
        return pl.ds(pl.multiple_of(base, 16), count)

    def down(self, part, level, step):
        base, count = self.region(part, level)
        device, at = self.others[level][step - 1]
        chunk = count // self.size[level]
        return pltpu.make_async_remote_copy(
            src_ref=self.acc.at[self.rows(base + at * chunk, chunk)], dst_ref=self.bufs[level].at[part, self.rows((step - 1) * chunk, chunk)],
            send_sem=self.sems[level].at[0, part], recv_sem=self.sems[level].at[1, part],
            device_id=device, device_id_type=MESH)

    def up(self, part, level, step):
        base, count = self.region(part, level + 1)
        rows = self.rows(base, count)
        return pltpu.make_async_remote_copy(
            src_ref=self.full.at[rows], dst_ref=(self.full if level else self.out).at[rows],
            send_sem=self.sems[level].at[2, part], recv_sem=self.sems[level].at[3, part],
            device_id=self.others[level][step - 1][0], device_id_type=MESH)

    def arrived(self, part, level, sem):
        every = self.bufs[level].at[part]
        pltpu.make_async_copy(every, every, self.sems[level].at[sem, part]).wait()

    def save(self, part):
        rows = self.rows(*self.region(part, 1))
        return pltpu.make_async_copy(self.full.at[rows], self.out.at[rows], self.save_sem.at[part])

    def stage(self, part, k):
        top = self.levels
        if 1 <= k <= top:
            level = k - 1
            self.arrived(part, level, 0)
            self.arrived(part, level, 1)
            base, count = self.region(part, level + 1)
            add_rows(self.full if k == top else self.acc, self.acc, base,
                     [self.bufs[level].at[part, self.rows(s * count, count)] for s in range(self.size[level] - 1)], count)
        if k < top:
            for step in range(1, self.size[k]):
                self.down(part, k, step).start()
        if k > top:
            level = 2 * top - k
            self.arrived(part, level, 2)
            self.arrived(part, level, 3)
        if top <= k < 2 * top:
            for step in range(1, self.size[2 * top - 1 - k]):
                self.up(part, 2 * top - 1 - k, step).start()
        if k == 2 * top - 1:
            self.save(part).start()


def kinds(mesh_rows, mesh_batch):
    x_n, z_n = mesh_rows // 2, mesh_batch // LOW
    return [2, LOW, x_n * z_n] if SPREAD else [2, LOW, x_n, z_n]


def columns(mesh_rows, mesh_batch):
    sizes = {w: w * padded(mesh_rows, mesh_batch, 2 * D * (CB // w)) for w in (256, 128)}
    return min(sizes, key=sizes.get)


def padded(mesh_rows, mesh_batch, count):
    unit = 16 * math.prod(kinds(mesh_rows, mesh_batch))
    return -(-count // unit) * unit


def sum_scratch(mesh_rows, mesh_batch, parts, count, width):
    size = kinds(mesh_rows, mesh_batch)
    shapes = [pltpu.VMEM((parts * count, width), BF16)] * 2
    for n in size:
        count //= n
        shapes.append(pltpu.VMEM((parts, (n - 1) * count, width), BF16))
    return shapes + [pltpu.SemaphoreType.DMA((4, parts)) for n in size] + [pltpu.SemaphoreType.DMA((parts,))]


def backward_kernel(row_count, batch_count, groups, pair, place, filt_l, filt_s, gain1, gain2, w1, w2, tl, ts, tlb, tsb,
                    mix, fold, outs, do_in, xs, zs, both_scales, spec, vs, gs, ps,
                    out_land, grad_land, weights_out, small_out,
                    dx, dv, do, dh, gslots, dvec, dhid, dfl, dfs, out_sem, grad_sem, own_sem, *sums):
    i = pl.program_id(0)
    batch, row = lax.axis_index("batch"), lax.axis_index("rows")
    chunks, pairs = FF // CB, groups // pair
    per = chunks + pairs
    compute_steps = LAYERS * per
    layer, q = LAYERS - 1 - i // per, i % per
    width = columns(row_count, batch_count)
    part_rows = padded(row_count, batch_count, 2 * D * (CB // width))
    small_rows = padded(row_count, batch_count, SMALL)
    sums_of = []
    for out, count in ((weights_out, part_rows), (small_out, small_rows)):
        n = len(kinds(row_count, batch_count))
        sums_of.append(Sum(row_count, batch_count, sums[0], sums[1], out, count, sums[2 : 2 + n], sums[2 + n : 2 + 2 * n], sums[2 + 2 * n]))
        sums = sums[3 + 2 * n :]
    weights, small = sums_of

    def send_out(m, g):
        return pltpu.make_async_remote_copy(
            src_ref=outs.at[m, g], dst_ref=out_land.at[m, g], send_sem=out_sem.at[0, m - 1, g], recv_sem=out_sem.at[1, m - 1, g],
            device_id=(batch, lax.rem(row + (row_count - m), row_count)), device_id_type=MESH)

    def send_grad(m, g):
        return pltpu.make_async_remote_copy(
            src_ref=gslots.at[m, g], dst_ref=grad_land.at[m, g], send_sem=grad_sem.at[0, m - 1, g], recv_sem=grad_sem.at[1, m - 1, g],
            device_id=(batch, lax.rem(row + (row_count - m), row_count)), device_id_type=MESH)

    def keep_out():
        return pltpu.make_async_copy(outs.at[0], out_land.at[0], own_sem.at[0])

    def keep_grad():
        return pltpu.make_async_copy(gslots.at[0], grad_land.at[0], own_sem.at[1])

    plan = {key: [a for a in PLAN[key] if a[0] != -2 or groups == 6] for key in PLAN}
    if groups != 6:
        plan[compute_steps - 1, 9] = [(-2, g) for g in range(groups)] + plan[compute_steps - 1, 9]
    left = set(plan)

    def do_now(part, k):
        if part >= 0:
            weights.stage(part, k)
        elif part == -1:
            small.stage(0, k)
        elif k < groups:
            for m in range(1, row_count):
                (send_grad if part == -2 else send_out)(m, k).start()

    def advance(place, steps):
        for at in steps:
            found = sorted(key for key in left if key[0] == at and (key[1] == place or place == 9))
            if found:
                @pl.when(i == at)
                def _():
                    for key in found:
                        left.discard(key)
                        for part, k in plan[key]:
                            do_now(part, k)

    first_steps = [at for at in range(compute_steps) if at % per < chunks]
    second_steps = [at for at in range(compute_steps) if at % per >= chunks]

    @pl.when(i == 0)
    def _():
        barrier = pltpu.get_barrier_semaphore()
        greeted = 0
        for m in range(1, row_count):
            pl.semaphore_signal(barrier, inc=1, device_id=(batch, lax.rem(row + m, row_count)), device_id_type=MESH)
            greeted += 1
        for level in range(1, weights.levels):
            for step in range(1, weights.size[level]):
                pl.semaphore_signal(barrier, inc=1, device_id=weights.others[level][step - 1][0], device_id_type=MESH)
                greeted += 1
        keep_out().start()
        if part_rows > 2 * D * (CB // width):
            weights.acc[...] = jnp.zeros_like(weights.acc)
        for g in range(groups):
            dx[g] = do_in[g].astype(F32)
        for ref in (dvec, dfl, dfs):
            ref[...] = jnp.zeros_like(ref)
        pl.semaphore_wait(barrier, greeted)

    @pl.when((i < compute_steps) & (q == 0))
    def _():
        for g in range(groups):
            rows = pl.ds(g * T, T)
            low = dx[g].astype(BF16)
            do[g] = low
            dvec[layer, 4:5] += jnp.sum(low.astype(F32), axis=0, keepdims=True)
        dv[...] = jnp.zeros_like(dv)

    @pl.when((i < compute_steps) & (q < chunks))
    def _():
        sums = jnp.zeros((1, CB), F32)
        for g in range(0, groups, pair):
            rows = slice(g * T, (g + pair) * T)
            some = do[g : g + pair].reshape(pair * T, D)
            slope = ps[0, g : g + pair].reshape(pair * T, CB)
            part = (dot_nt(some, w2[0]) * slope.astype(F32)).astype(BF16)
            dh[rows] = part
            sums = sums + jnp.sum(part.astype(F32), axis=0, keepdims=True)
            advance(g // pair, first_steps)
        part = (LAYERS - 1 - layer) * chunks + q
        base = part * part_rows
        dhid[layer, :, pl.ds(pl.multiple_of(q * CB, CB), CB)] = sums
        one = dot_tn(vs[0].reshape(groups * T, D), dh[...])
        two = dot_tn(do[...].reshape(groups * T, D), gs[0].reshape(groups * T, CB))
        for c in range(CB // width):
            cols = slice(c * width, (c + 1) * width)
            weights.acc[weights.rows(base + c * D, D), :] = one[:D, cols].astype(BF16)
            weights.acc[weights.rows(base + (CB // width + c) * D, D), :] = two[:, cols].astype(BF16)
        advance(3, first_steps)
        for g in range(0, groups, pair):
            dv[g : g + pair] += dot_nt(dh[g * T : (g + pair) * T], w1[0]).reshape(pair, T, D)

    @pl.when((i < compute_steps) & (q >= chunks))
    def _():
        side = lambda parts: jnp.concatenate(parts, axis=1)
        lanes = lambda a: [a[:, j * D : (j + 1) * D] for j in range(pair)]
        row_sum = lambda a: jnp.sum(a, axis=0, keepdims=True)
        first = (q - chunks) * pair
        dz = []
        for j in range(pair):
            dvg = dv[first + j]
            unit = zs[0, j].astype(F32)
            dvec[layer, 2:3] += row_sum(dvg * unit)
            dvec[layer, 3:4] += row_sum(dvg)
            dz.append(normal_back(dvg, gain2[pl.ds(layer, 1)], unit, both_scales[0, j, :, 1:2]).astype(BF16))
        advance(0, second_steps)
        yl, ysm = analyse(tl[...], ts[...], side(dz))
        dl, ds = [], []
        for j, (a, b) in enumerate(zip(lanes(yl), lanes(ysm))):
            lr, li = a[:NL], a[NL:]
            sr, si = b[: PER * NS], b[PER * NS :]
            xr, xi = spec[0, j, :NL].astype(F32), spec[0, j, NL : 2 * NL].astype(F32)
            dfl[layer, :NL] += lr * xr + li * xi
            dfl[layer, NL:] += li * xr - lr * xi
            gr, gi = filt_l[0, 0], filt_l[0, 1]
            dl.append(jnp.concatenate([lr * gr + li * gi, li * gr - lr * gi], axis=0).astype(BF16))
            small_spec = spec[0, j, 2 * NL :].astype(F32)
            xr, xi = small_spec[: PER * NS], small_spec[PER * NS :]
            once = lambda a: a[:NS] + a[NS : 2 * NS] + a[2 * NS :]
            dfs[layer, :NS] += once(sr * xr + si * xi)
            dfs[layer, NS:] += once(si * xr - sr * xi)
            gr, gi = thrice(filt_s[0, 0]), thrice(filt_s[0, 1])
            ds.append(jnp.concatenate([sr * gr + si * gi, si * gr - sr * gi], axis=0).astype(BF16))
        advance(1, second_steps)
        grads = []
        for j, du in enumerate(lanes(synthesise(tlb[...], tsb[...], side(dl), side(ds)))):
            unit = xs[0, j].astype(F32)
            dvec[layer, 0:1] += row_sum(du * unit)
            dvec[layer, 1:2] += row_sum(du)
            grad = dx[first + j] + normal_back(du, gain1[pl.ds(layer, 1)], unit, both_scales[0, j, :, 0:1])
            dx[first + j] = grad
            grads.append(grad.astype(BF16))
        advance(2, second_steps)

        @pl.when(layer == 0)
        def _():
            spread = dot(place[...], side(grads)).astype(BF16)
            for j in range(pair):
                for m in range(row_count):
                    gslots[m, first + j] = spread[m * BAND : (m + 1) * BAND, j * D : (j + 1) * D]

    def lay_out(layers):
        exact = partial(jnp.dot, preferred_element_type=F32, precision=HIGHEST)
        mix_t = mix[...].T
        for n in layers:
            for c in range(2):
                at = (n * 2 + c) * NL
                small.acc[at : at + NL, :] = (dfl[n, c * NL : (c + 1) * NL] * fold[...]
                                              + exact(mix_t, dfs[n, c * NS : (c + 1) * NS])).astype(BF16)

    @pl.when(i == compute_steps - pairs - 1)
    def _():
        small.acc[...] = jnp.zeros_like(small.acc)
        lay_out(range(1, LAYERS))

    @pl.when(i == compute_steps - 1)
    def _():
        lay_out([0])
        at = LAYERS * 2 * NL
        rest = [dvec[n, k : k + 1] for n in range(LAYERS) for k in range(5)]
        rest += [dhid[n, :, c : c + D] for n in range(LAYERS) for c in range(0, FF, D)]
        rest.append(jnp.zeros((-len(rest) % 16, D), F32))
        rest = jnp.concatenate(rest, axis=0).astype(BF16)
        small.acc[at : at + rest.shape[0], :] = rest
        keep_grad().start()

    advance(9, range(compute_steps))

    @pl.when(i == pl.num_programs(0) - 1)
    def _():
        keep_out().wait()
        keep_grad().wait()
        for m in range(1, row_count):
            @pl.loop(0, groups)
            def _(g):
                send_out(m, g).wait()
                send_grad(m, g).wait()
        for part in range(LAYERS * chunks):
            weights.save(part).wait()
        small.save(0).wait()


def backward(mesh, groups, pair, small, tabs, mix, fold, outs, do, saved):
    rows, batch = mesh.shape["rows"], mesh.shape["batch"]
    place, filt_l, filt_s, gain1, gain2, w1, w2 = small
    chunks, pairs = FF // CB, groups // pair
    per, last = chunks + pairs, LAYERS - 1
    steps = LAYERS * per
    layer = lambda i: jnp.maximum(last - i // per, 0)
    when = lambda i: jnp.where(i < LAYERS * per, i % per, per - 1)
    chunk = lambda i: jnp.minimum(when(i), chunks - 1)
    place_of = lambda i: jnp.maximum(when(i) - chunks, 0)
    per_layer = lambda a: pl.BlockSpec((1,) + a.shape[1:], lambda i: (layer(i),) + (0,) * (a.ndim - 1))
    by_pair = lambda a: pl.BlockSpec((1, pair) + a.shape[2:], lambda i: (layer(i), place_of(i), 0, 0))
    by_chunk = lambda a: pl.BlockSpec((1, groups, T, CB), lambda i: (layer(i), 0, 0, chunk(i)))
    xs, zs, scales, spec, vs, gs, ps = saved
    hbm = pl.BlockSpec(memory_space=pl.ANY)
    width = columns(rows, batch)
    part_rows, small_rows = padded(rows, batch, 2 * D * (CB // width)), padded(rows, batch, SMALL)
    dma = pltpu.SemaphoreType.DMA
    return pl.pallas_call(
        partial(backward_kernel, rows, batch, groups, pair),
        grid=(steps,),
        in_specs=[whole(place.shape), per_layer(filt_l), per_layer(filt_s), whole(gain1.shape), whole(gain2.shape)]
        + [pl.BlockSpec((1, D, CB), lambda i: (layer(i), 0, chunk(i))), pl.BlockSpec((1, CB, D), lambda i: (layer(i), chunk(i), 0))]
        + [whole(a.shape) for a in (*tabs, mix, fold)] + [hbm, whole(do.shape)]
        + [by_pair(xs), by_pair(zs), by_pair(scales), by_pair(spec), per_layer(vs), by_chunk(gs), by_chunk(ps)],
        out_specs=[hbm] * 4,
        out_shape=[jax.ShapeDtypeStruct((rows, groups, BAND, D), BF16)] * 2
        + [jax.ShapeDtypeStruct((LAYERS * chunks * part_rows, width), BF16), jax.ShapeDtypeStruct((small_rows, D), BF16)],
        scratch_shapes=[pltpu.VMEM((groups, T, D), F32), pltpu.VMEM((groups, T, D), F32), pltpu.VMEM((groups, T, D), BF16),
                        pltpu.VMEM((groups * T, CB), BF16), pltpu.VMEM((rows, groups, BAND, D), BF16),
                        pltpu.VMEM((LAYERS, 5, D), F32), pltpu.VMEM((LAYERS, 1, FF), F32),
                        pltpu.VMEM((LAYERS, 2 * NL, D), F32), pltpu.VMEM((LAYERS, 2 * NS, D), F32),
                        dma((2, rows - 1, groups)), dma((2, rows - 1, groups)), dma((2,))]
        + sum_scratch(rows, batch, LAYERS * chunks, part_rows, width) + sum_scratch(rows, batch, 1, small_rows, D),
        compiler_params=pltpu.CompilerParams(collective_id=2, has_side_effects=True, vmem_limit_bytes=VMEM_LIMIT),
        name="backward",
    )(place, filt_l, filt_s, gain1, gain2, w1, w2, *tabs, mix, fold, outs, do, xs, zs, scales, spec, vs, gs, ps)


def unpack_kernel(groups, order, outs, grads, weights, small, large_out, small_crops, large_grad, small_grad, dw1, dw2, dfilter, dhid,
                  *rest):
    dvec, rest = rest[:5], rest[5:]
    given, weight, large, little, one, two, in_sem, weight_sem, out_sem, done_sem = rest
    rows = outs.shape[0]
    parts, chunks, width = weight.shape[0], FF // CB, weight.shape[2]
    halves = CB // width

    def read(dev, kind):
        return pltpu.make_async_copy((outs, grads)[kind].at[order[dev]], given.at[kind, dev], in_sem.at[kind, dev])

    def read_weight(part):
        return pltpu.make_async_copy(weights.at[part], weight.at[part], weight_sem.at[part])

    def write(dev, kind):
        to_large, to_little = ((large_out, small_crops), (large_grad, small_grad))[kind]
        return (pltpu.make_async_copy(large.at[kind, dev], to_large.at[pl.ds(dev * groups, groups)], out_sem.at[kind, 0, dev]),
                pltpu.make_async_copy(little.at[kind, dev], to_little.at[pl.ds(dev * groups * PER, groups * PER)], out_sem.at[kind, 1, dev]))

    def write_weight(part):
        layer, at = LAYERS - 1 - part // chunks, part % chunks * CB
        return (pltpu.make_async_copy(one.at[part], dw1.at[layer, :, pl.ds(at, CB)], done_sem.at[0, part]),
                pltpu.make_async_copy(two.at[part], dw2.at[layer, pl.ds(at, CB)], done_sem.at[1, part]))

    for part in range(parts):
        read_weight(part).start()
    for dev in range(rows):
        for kind in range(2):
            read(dev, kind).start()
    for part in range(parts):
        read_weight(part).wait()
        for c in range(halves):
            cols = slice(c * width, (c + 1) * width)
            one[part, :, cols] = weight[part, c * D : (c + 1) * D].astype(F32)
            two[part, cols] = weight[part, (halves + c) * D : (halves + c + 1) * D].astype(F32).T
        for copy in write_weight(part):
            copy.start()
    for dev in range(rows):
        for kind in range(2):
            read(dev, kind).wait()

            @pl.loop(0, groups)
            def _(g):
                block = given[kind, dev, g].astype(F32)
                for w in range(WL):
                    large[kind, dev, g, 0, w] = block[w * BL : (w + 1) * BL]
                for p in range(PER):
                    for w in range(WS):
                        at = BL * WL + (p * WS + w) * BS
                        little[kind, dev, g * PER + p, 0, w] = block[at : at + BS]

            for copy in write(dev, kind):
                copy.start()
    at = LAYERS * 2 * NL
    for n in range(LAYERS):
        for c in range(2):
            dfilter[n, c] = small[(n * 2 + c) * NL : (n * 2 + c + 1) * NL].astype(F32)
    others = small[at : at + 32].astype(F32)
    for n in range(LAYERS):
        for k in range(5):
            dvec[k][n : n + 1] = others[n * 5 + k : n * 5 + k + 1]
        for c in range(FF // D):
            r = LAYERS * 5 + n * (FF // D) + c
            dhid[n : n + 1, c * D : (c + 1) * D] = others[r : r + 1]
    for part in range(parts):
        for copy in write_weight(part):
            copy.wait()
    for dev in range(rows):
        for kind in range(2):
            for copy in write(dev, kind):
                copy.wait()


def unpack(mesh, groups, pair, outs, grads, weights, small):
    rows = mesh.shape["rows"]
    me = lax.axis_index("rows")
    crops = rows * groups
    width = weights.shape[1]
    halves = CB // width
    parts = LAYERS * (FF // CB)
    weights = weights.reshape(parts, -1, width)[:, : 2 * D * halves]
    order = lax.rem(jnp.arange(rows, dtype=jnp.int32) + (rows - me), rows)
    large_shape, little_shape = (crops, 1, WL, BL, D), (crops * PER, 1, WS, BS, D)
    shapes = [(LAYERS, 2, NL, D), (LAYERS, FF)] + [(LAYERS, D)] * 5
    hbm, vmem, dma = pl.BlockSpec(memory_space=pl.ANY), pl.BlockSpec(memory_space=pltpu.VMEM), pltpu.SemaphoreType.DMA
    return pl.pallas_call(
        partial(unpack_kernel, groups),
        in_specs=[scalars()] + [hbm] * 3 + [vmem],
        out_specs=[hbm] * 6 + [vmem] * len(shapes),
        out_shape=[jax.ShapeDtypeStruct(s, F32) for s in [large_shape, little_shape] * 2 + [(LAYERS, D, FF), (LAYERS, FF, D)] + shapes],
        scratch_shapes=[pltpu.VMEM((2, rows, groups, BAND, D), BF16), pltpu.VMEM(weights.shape, BF16),
                        pltpu.VMEM((2, rows, groups, 1, WL, BL, D), F32), pltpu.VMEM((2, rows, groups * PER, 1, WS, BS, D), F32),
                        pltpu.VMEM((parts, D, CB), F32), pltpu.VMEM((parts, CB, D), F32),
                        dma((2, rows)), dma((parts,)), dma((2, 2, rows)), dma((2, parts))],
        compiler_params=pltpu.CompilerParams(vmem_limit_bytes=VMEM_LIMIT),
        name="unpack",
    )(order, outs, grads, weights, small)


def wanted_rows():
    t, c = np.arange(T), np.arange(BAND)
    small_t, small_c = t >= TL, c >= BL * WL
    at = np.where(small_t, (t - TL) % TS, t)
    wide = np.where(small_t, WS, WL)
    r, w, crop = at // wide, at % wide, np.where(small_t, (t - TL) // TS, 0)
    at_c = np.where(small_c, (c - BL * WL) % (BS * WS), c)
    slots = np.where(small_c, BS, BL)
    s_c, w_c, crop_c = at_c % slots, at_c // slots, np.where(small_c, (c - BL * WL) // (BS * WS), 0)
    same = (small_t[:, None] == small_c) & (w[:, None] == w_c) & (crop[:, None] == crop_c)
    return np.where(same, r[:, None] - s_c, -99).astype(np.int32), s_c[None].astype(np.int32)


def interp_tables():
    fold_l = np.where((np.arange(FL) == 0) | (2 * np.arange(FL) == WL), 1.0, 2.0)
    fold_s = np.where((np.arange(FS) == 0) | (2 * np.arange(FS) == WS), 1.0, 2.0)
    each = lambda n, times: np.repeat(np.eye(n), times, axis=0)
    again = lambda n, times: np.tile(np.eye(n), (times, 1))
    return [jnp.asarray(a, F32) for a in (each(HS, FS), each(HL, FL).T, again(FS, HS) * np.tile(fold_s, HS)[:, None],
                                          again(FL, HL).T, np.tile(fold_l, HL)[:, None])]


def local(mesh, large_in, small_in, large_cot, small_cot, crop_counts, band_bounds, row_interp, col_interp,
          norm1_gain, norm1_bias, filters, norm2_gain, norm2_bias, fc1_weight, fc1_bias, fc2_weight, fc2_bias):
    rows = mesh.shape["rows"]
    me = lax.axis_index("rows")
    crops = large_in.shape[0]
    groups = crops // rows
    pair = 2 if groups % 2 == 0 else 1
    tabs = tables()
    filters = filters.reshape(LAYERS, 2, NL, D)

    arrays = [a.transpose(0, 1, 3, 2, 4) for a in (large_in, small_in, large_cot, small_cot)]
    need, slot = wanted_rows()
    extras = (jnp.asarray(need), jnp.asarray(slot), row_interp, col_interp, *interp_tables())
    outs, *saved, do, place, filt_l, filt_s, mix = forward(mesh, groups, pair, arrays, crop_counts, band_bounds,
                               (filters, norm1_gain, norm1_bias, norm2_gain, norm2_bias, fc1_weight, fc1_bias, fc2_weight, fc2_bias,
                                *tabs, *extras))
    outs, grads, weights, small = backward(
        mesh, groups, pair, (place, filt_l, filt_s, norm1_gain, norm2_gain, fc1_weight, fc2_weight), tabs,
        mix, extras[-1], outs, do, saved)
    large_out, small_out, large_grad, small_grad, dw1, dw2, dfilter, dhid, *dvec = unpack(
        mesh, groups, pair, outs, grads, weights, small)
    large_out, small_out, large_grad, small_grad = (
        a.transpose(0, 1, 3, 2, 4) for a in (large_out, small_out, large_grad, small_grad))
    return (large_out, small_out, large_grad, small_grad, dvec[0], dvec[1], dfilter.reshape(LAYERS, 2, HL, FL, D), dvec[2], dvec[3],
            dw1, dhid, dw2, dvec[4])


def solution(mesh):
    split = P("batch", "rows", None, None, None)
    return jax.shard_map(partial(local, mesh), mesh=mesh, in_specs=(split,) * 4 + (P("batch", None),) + (P(),) * 12,
                         out_specs=(split,) * 4 + (P(),) * 9, check_vma=False)
```

```python
import math
from functools import partial
import numpy as np
import jax
import jax.numpy as jnp
from jax import lax
from jax.experimental import pallas as pl
from jax.experimental.pallas import tpu as pltpu
from jax.sharding import PartitionSpec as P

D, FF = 384, 1536
HL, WL, FL = 14, 14, 8
HS, WS, FS = 6, 6, 4
BL, BS = 4, 2
LAYERS = 2
EPS = 1e-6
TL, TS = HL * WL, HS * WS
PER = 3
T = TL + PER * TS
CUT, END = 192, 208
NL, NS = HL * FL, HS * FS
BAND = 96
CH = 512
CB = 512
SMALL = 512
PLAN = {
    (0, 0): [(-3, 0)],
    (0, 3): [(0, 0), (-3, 1)],
    (1, 1): [(0, 1), (-3, 2)],
    (1, 3): [(1, 0)],
    (1, 9): [(-3, 3)],
    (2, 1): [(1, 1)],
    (2, 3): [(0, 2), (2, 0)],
    (2, 9): [(-3, 4)],
    (3, 1): [(2, 1)],
    (3, 9): [(-3, 5)],
    (4, 0): [(1, 2)],
    (5, 2): [(0, 3), (2, 2)],
    (6, 3): [(3, 0)],
    (6, 9): [(1, 3)],
    (7, 1): [(3, 1)],
    (7, 3): [(0, 4), (4, 0)],
    (8, 1): [(4, 1)],
    (8, 3): [(2, 3), (3, 2), (5, 0)],
    (9, 1): [(5, 1)],
    (9, 2): [(1, 4), (0, 5)],
    (9, 9): [(-2, 0)],
    (10, 1): [(0, 6), (4, 2)],
    (11, 0): [(-2, 1)],
    (11, 1): [(2, 4)],
    (11, 2): [(5, 2)],
    (11, 9): [(-1, 0), (1, 5), (-1, 1), (3, 3), (1, 6), (2, 5), (4, 3), (-1, 2), (2, 6), (5, 3), (-2, 2), (3, 4), (4, 4), (-2, 3), (-1, 3), (-2, 4), (3, 5), (3, 6), (5, 4), (-2, 5), (4, 5), (4, 6), (-1, 4), (5, 5), (-1, 5), (5, 6), (-1, 6)],
}
MESH = pl.DeviceIdType.MESH
VMEM_LIMIT = 60 * 2**20
F32, BF16 = jnp.float32, jnp.bfloat16
HIGHEST = lax.Precision.HIGHEST


def table(height, width, count):
    k = np.arange(height)[:, None, None, None]
    l = np.arange(count)[None, :, None, None]
    s = np.arange(height)[None, None, :, None]
    w = np.arange(width)[None, None, None, :]
    phase = (k * s * width + l * w * height) % (height * width)
    angle = phase.astype(np.float32) * np.float32(2.0 * math.pi / (height * width))
    scale = np.float32(1.0 / math.sqrt(height * width))
    both = np.stack([np.cos(angle) * scale, -np.sin(angle) * scale])
    return both.reshape(2, height * count, height * width).astype(jnp.bfloat16).astype(np.float32)


def tables():
    large = np.zeros((2 * NL, END), np.float32)
    large[:, :TL] = table(HL, WL, FL).reshape(2 * NL, TL)
    one = table(HS, WS, FS)
    small = np.zeros((2, PER, NS, T - CUT), np.float32)
    for at in range(PER):
        small[:, at, :, TL - CUT + at * TS : TL - CUT + (at + 1) * TS] = one
    small = small.reshape(2 * PER * NS, T - CUT)
    return [jnp.asarray(t, BF16) for t in (large, small, large.T, small.T)]


def normal(x):
    mean = jnp.mean(x, axis=-1, keepdims=True)
    centred = x - mean
    scale = lax.rsqrt(jnp.mean(centred * centred, axis=-1, keepdims=True) + EPS)
    return centred * scale, scale


def normal_back(grad, gain, unit, scale):
    inner = grad * gain
    first = jnp.mean(inner, axis=-1, keepdims=True)
    second = jnp.mean(inner * unit, axis=-1, keepdims=True)
    return (inner - first - unit * second) * scale


def dot(a, b):
    return jnp.dot(a, b, preferred_element_type=F32)


def dot_nt(a, b):
    return lax.dot_general(a, b, (((1,), (1,)), ((), ())), preferred_element_type=F32)


def dot_tn(a, b):
    return lax.dot_general(a, b, (((0,), (0,)), ((), ())), preferred_element_type=F32)


def analyse(large_table, small_table, values):
    return dot(large_table, values[:END]), dot(small_table, values[CUT:])


def synthesise(large_back, small_back, large, small):
    a, b = dot(large_back, large), dot(small_back, small)
    return jnp.concatenate([a[:CUT], a[CUT:] + b[: END - CUT], b[END - CUT :]], axis=0)


def thrice(x):
    return jnp.concatenate([x] * PER, axis=0)


def gelu_both(h):
    cdf = 0.5 + 0.5 * lax.erf(h * np.float32(math.sqrt(0.5)))
    dens = jnp.exp(h * h * np.float32(-0.5)) * np.float32(1 / math.sqrt(2 * math.pi))
    return h * cdf, cdf + h * dens


def live_rows(counts, group):
    t = lax.broadcasted_iota(jnp.int32, (T, 1), 0)
    place, limit = jnp.full((T, 1), group), jnp.where(t < TL, counts[0, 0], counts[0, 1])
    for at in range(PER):
        place = jnp.where(t >= TL + at * TS, group * PER + at, place)
    return jnp.where(place < limit, 1.0, 0.0)


def whole(shape):
    return pl.BlockSpec(shape, lambda *a: (0,) * len(shape))


def scalars():
    return pl.BlockSpec(memory_space=pltpu.SMEM)


def forward_kernel(row_count, groups, pair, large_in, small_in, large_cot, small_cot, counts, bounds, filters, gain1, bias1, gain2, bias2,
                   w1_in, b1, w2_in, b2, tl, ts, tlb, tsb, need, slot, row_interp, col_interp, row_s, row_l, col_s, col_l, fold,
                   outs, xs, zs, both_scales, spec, vs, gs_out, ps_out, do, place, filt_l, filt_s, mix,
                   w1, w2, gs, ps, weight_sem, save_sem, pick, lined, large_slots, small_slots, own_sem, send_sem, recv_sem):
    step = pl.program_id(0)
    batch, row = lax.axis_index("batch"), lax.axis_index("rows")
    last = groups // pair - 1

    def ends(which, m, g, to):
        crop = to * groups + g
        return (((large_in, large_cot)[which].at[crop, 0], large_slots.at[which, m, g]),
                ((small_in, small_cot)[which].at[pl.ds(crop * PER, PER), 0], small_slots.at[which, m, g]))

    def remote(which, m, g):
        to = lax.rem(row + m, row_count)
        return [pltpu.make_async_remote_copy(
            src_ref=source, dst_ref=target,
            send_sem=send_sem.at[which, k, m - 1, g], recv_sem=recv_sem.at[which, k, m - 1, g],
            device_id=(batch, to), device_id_type=MESH) for k, (source, target) in enumerate(ends(which, m, g, to))]

    def mine(which, g):
        return [pltpu.make_async_copy(source, target, own_sem.at[which, k, g])
                for k, (source, target) in enumerate(ends(which, 0, g, row))]

    def weights(n):
        return [pltpu.make_async_copy(w1_in.at[n], w1.at[n], weight_sem.at[0, n]),
                pltpu.make_async_copy(w2_in.at[n], w2.at[n], weight_sem.at[1, n])]

    def keep(n, c, at):
        cols = pl.ds(c, CH)
        return [pltpu.make_async_copy(ref.at[n, :, :, cols], out.at[n, pl.ds(at * pair, pair), :, cols], save_sem.at[k, n, c // CH])
                for k, (ref, out) in enumerate(((gs, gs_out), (ps, ps_out)))]

    @pl.when(step == 0)
    def _():
        barrier = pltpu.get_barrier_semaphore()
        for m in range(1, row_count):
            pl.semaphore_signal(barrier, inc=1, device_id=(batch, lax.rem(row + m, row_count)), device_id_type=MESH)
        for which in range(2):
            @pl.loop(0, groups)
            def _(g):
                for copy in mine(which, g):
                    copy.start()
        pl.semaphore_wait(barrier, row_count - 1)
        for which in range(2):
            @pl.loop(0, groups)
            def _(g):
                for m in range(1, row_count):
                    for copy in remote(which, m, g):
                        copy.start()
        for n in range(LAYERS):
            for copy in weights(n):
                copy.start()
        lined[...] = jnp.zeros_like(lined)
        for m in range(row_count):
            band = lax.rem(row + (row_count - m), row_count)
            large = lax.broadcasted_iota(jnp.int32, (T, BAND), 0) < TL
            first = jnp.where(large, bounds[0, band], bounds[1, band])
            size = jnp.where(large, bounds[0, band + 1], bounds[1, band + 1]) - first
            hit = (need[...] == first) & (slot[...] < size)
            hit = jnp.where(hit, 1.0, 0.0)
            pick[:, m * BAND : (m + 1) * BAND] = hit.astype(BF16)
            place[m * BAND : (m + 1) * BAND, :] = hit.T.astype(BF16)
        exact = partial(jnp.dot, preferred_element_type=F32, precision=HIGHEST)
        both = exact(exact(row_s[...], row_interp[...]), row_l[...]) * exact(exact(col_s[...], col_interp[...]), col_l[...])
        mix[...] = both
        for n in range(LAYERS):
            for c in range(2):
                filt_l[n, c] = filters[n, c] * fold[...]
                filt_s[n, c] = exact(both, filters[n, c])

    def live(g):
        return live_rows(counts, row * groups + g)

    def take(which, g):
        for copy in mine(which, g):
            copy.wait()
        for m in range(1, row_count):
            for copy in remote(which, m, g):
                copy.wait_recv()
        for m in range(row_count):
            at = m * BAND
            for w in range(WL):
                lined[at + w * BL : at + (w + 1) * BL, :] = large_slots[which, m, g, w].astype(F32)
            at += BL * WL
            for p in range(PER):
                for w in range(WS):
                    row_at = at + (p * WS + w) * BS
                    lined[row_at : row_at + BS, :] = small_slots[which, m, g, p, w].astype(F32)
        return dot(pick[...], lined[...].astype(BF16))

    side = lambda parts: jnp.concatenate(parts, axis=1)
    lanes = lambda a: [a[:, j * D : (j + 1) * D] for j in range(pair)]
    x = [take(0, step * pair + j) for j in range(pair)]
    for n in range(LAYERS):
        u, scales = [], []
        for j in range(pair):
            unit, scale = normal(x[j])
            xs[n, j] = unit.astype(BF16)
            scales.append(scale)
            u.append((unit * gain1[n : n + 1] + bias1[n : n + 1]).astype(BF16))
        xl, xsm = analyse(tl[...], ts[...], side(u))
        yl, ys = [], []
        for j, (a, b) in enumerate(zip(lanes(xl), lanes(xsm))):
            spec[n, j, : 2 * NL] = a.astype(BF16)
            spec[n, j, 2 * NL :] = b.astype(BF16)
            lr, li = a[:NL], a[NL:]
            sr, si = b[: PER * NS], b[PER * NS :]
            gr, gi = filt_l[n, 0], filt_l[n, 1]
            yl.append(jnp.concatenate([lr * gr - li * gi, lr * gi + li * gr], axis=0).astype(BF16))
            gr, gi = thrice(filt_s[n, 0]), thrice(filt_s[n, 1])
            ys.append(jnp.concatenate([sr * gr - si * gi, sr * gi + si * gr], axis=0).astype(BF16))
        v = []
        for j, z in enumerate(lanes(synthesise(tlb[...], tsb[...], side(yl), side(ys)))):
            unit, scale = normal(z)
            zs[n, j] = unit.astype(BF16)
            both_scales[n, j] = side([scales[j], scale])
            unit = (unit * gain2[n : n + 1] + bias2[n : n + 1]).astype(BF16)
            vs[n, j] = unit
            v.append(unit)
        v = jnp.concatenate(v, axis=0)
        total = jnp.concatenate(x, axis=0) + b2[n : n + 1]
        @pl.when(step == 0)
        def _():
            for copy in weights(n):
                copy.wait()

        @pl.when(step > 0)
        def _():
            for c in range(0, FF, CH):
                for copy in keep(n, c, step - 1):
                    copy.wait()

        for c in range(0, FF, CH):
            h = dot(v, w1[n, :, c : c + CH]) + b1[n : n + 1, c : c + CH]
            g, slope = gelu_both(h)
            g = g.astype(BF16)
            slope = slope.astype(BF16)
            for j in range(pair):
                gs[n, j, :, c : c + CH] = g[j * T : (j + 1) * T]
                ps[n, j, :, c : c + CH] = slope[j * T : (j + 1) * T]
            for copy in keep(n, c, step):
                copy.start()
            total = total + dot(g, w2[n, c : c + CH, :])
        x = [total[j * T : (j + 1) * T] for j in range(pair)]
    for j in range(pair):
        spread = dot(place[...], (x[j] * live(step * pair + j)).astype(BF16)).astype(BF16)
        for m in range(row_count):
            outs[m, j] = spread[m * BAND : (m + 1) * BAND]

    @pl.when(step == last)
    def _():
        for g in range(groups):
            do[g] = (take(1, g) * live(g)).astype(BF16)
        for which in range(2):
            @pl.loop(0, groups)
            def _(g):
                for m in range(1, row_count):
                    for copy in remote(which, m, g):
                        copy.wait_send()
        for n in range(LAYERS):
            for c in range(0, FF, CH):
                for copy in keep(n, c, last):
                    copy.wait()


def forward(mesh, groups, pair, crops, counts, bounds, small):
    rows = mesh.shape["rows"]
    sizes = [(T, D, BF16), (T, D, BF16), (T, 2, F32), (2 * NL + 2 * PER * NS, D, BF16), (T, D, BF16), (T, FF, BF16), (T, FF, BF16)]
    extra = [((groups, T, D), BF16), ((rows * BAND, T), BF16), ((LAYERS, 2, NL, D), F32), ((LAYERS, 2, NS, D), F32), ((NS, NL), F32)]
    hbm = pl.BlockSpec(memory_space=pl.ANY)
    return pl.pallas_call(
        partial(forward_kernel, rows, groups, pair),
        grid=(groups // pair,),
        in_specs=[hbm] * 4 + [scalars(), scalars()] + [hbm if a.shape[1:] in ((D, FF), (FF, D)) else whole(a.shape) for a in small],
        out_specs=[pl.BlockSpec((rows, pair, BAND, D), lambda i: (0, i, 0, 0))]
        + [pl.BlockSpec((LAYERS, pair, a, b), lambda i: (0, i, 0, 0)) if b != FF else hbm for a, b, _ in sizes]
        + [whole(a) for a, _ in extra],
        out_shape=[jax.ShapeDtypeStruct((rows, groups, BAND, D), BF16)]
        + [jax.ShapeDtypeStruct((LAYERS, groups, a, b), t) for a, b, t in sizes]
        + [jax.ShapeDtypeStruct(a, t) for a, t in extra],
        scratch_shapes=[pltpu.VMEM((LAYERS, D, FF), BF16), pltpu.VMEM((LAYERS, FF, D), BF16)]
        + [pltpu.VMEM((LAYERS, pair, T, FF), BF16)] * 2
        + [pltpu.SemaphoreType.DMA((2, LAYERS)), pltpu.SemaphoreType.DMA((2, LAYERS, FF // CH)),
                        pltpu.VMEM((T, rows * BAND), BF16), pltpu.VMEM((rows * BAND, D), F32),
                        pltpu.VMEM((2, rows, groups, WL, BL, D), BF16), pltpu.VMEM((2, rows, groups, PER, WS, BS, D), BF16),
                        pltpu.SemaphoreType.DMA((2, 2, groups)), pltpu.SemaphoreType.DMA((2, 2, rows - 1, groups)),
                        pltpu.SemaphoreType.DMA((2, 2, rows - 1, groups))],
        compiler_params=pltpu.CompilerParams(collective_id=1, has_side_effects=True, vmem_limit_bytes=VMEM_LIMIT),
        name="forward",
    )(*crops, counts, bounds, *small)


SPREAD = True
LOW = 2


def add_rows(target, at_target, base, sources, count):
    step = next(s for s in (128, 96, 64, 48, 32, 16) if count % s == 0)

    @pl.loop(0, count // step)
    def _(i):
        at = pl.multiple_of(i * step, 16)
        rows = pl.ds(pl.multiple_of(base + at, 16), step)
        total = at_target[rows, :].astype(F32)
        for ref in sources:
            total = total + ref[pl.ds(at, step), :].astype(F32)
        target[rows, :] = total.astype(BF16)


class Sum:
    def __init__(self, mesh_rows, mesh_batch, acc, full, out, count, bufs, sems, save_sem):
        batch, row = lax.axis_index("batch"), lax.axis_index("rows")
        self.acc, self.full, self.out, self.count, self.bufs, self.sems, self.save_sem = acc, full, out, count, bufs, sems, save_sem
        self.size = kinds(mesh_rows, mesh_batch)
        self.levels = len(self.size)
        x_n = mesh_rows // 2
        core, x, z, y = lax.rem(row, 2), lax.div(row, 2), lax.div(batch, LOW), lax.rem(batch, LOW)
        self.me = [core, y, z * x_n + x] if SPREAD else [core, y, x, z]
        self.others, self.offsets, self.counts = [], [0], [count]
        for level, n in enumerate(self.size):
            count //= n
            self.counts.append(count)
            self.offsets.append(self.offsets[-1] + self.me[level] * count)
            found = []
            for step in range(1, n):
                at = lax.rem(self.me[level] + step, n)
                device = [(batch, x * 2 + at), (z * LOW + at, row)]
                device += [(lax.div(at, x_n) * LOW + y, lax.rem(at, x_n) * 2 + core)] if SPREAD else [
                    (batch, at * 2 + core), (at * LOW + y, row)]
                found.append((device[level], at))
            self.others.append(found)

    def region(self, part, level):
        return part * self.count + self.offsets[level], self.counts[level]

    def rows(self, base, count):
        return pl.ds(pl.multiple_of(base, 16), count)

    def down(self, part, level, step):
        base, count = self.region(part, level)
        device, at = self.others[level][step - 1]
        chunk = count // self.size[level]
        return pltpu.make_async_remote_copy(
            src_ref=self.acc.at[self.rows(base + at * chunk, chunk)], dst_ref=self.bufs[level].at[part, self.rows((step - 1) * chunk, chunk)],
            send_sem=self.sems[level].at[0, part], recv_sem=self.sems[level].at[1, part],
            device_id=device, device_id_type=MESH)

    def up(self, part, level, step):
        base, count = self.region(part, level + 1)
        rows = self.rows(base, count)
        return pltpu.make_async_remote_copy(
            src_ref=self.full.at[rows], dst_ref=(self.full if level else self.out).at[rows],
            send_sem=self.sems[level].at[2, part], recv_sem=self.sems[level].at[3, part],
            device_id=self.others[level][step - 1][0], device_id_type=MESH)

    def arrived(self, part, level, sem):
        every = self.bufs[level].at[part]
        pltpu.make_async_copy(every, every, self.sems[level].at[sem, part]).wait()

    def save(self, part):
        rows = self.rows(*self.region(part, 1))
        return pltpu.make_async_copy(self.full.at[rows], self.out.at[rows], self.save_sem.at[part])

    def stage(self, part, k):
        top = self.levels
        if 1 <= k <= top:
            level = k - 1
            self.arrived(part, level, 0)
            self.arrived(part, level, 1)
            base, count = self.region(part, level + 1)
            add_rows(self.full if k == top else self.acc, self.acc, base,
                     [self.bufs[level].at[part, self.rows(s * count, count)] for s in range(self.size[level] - 1)], count)
        if k < top:
            for step in range(1, self.size[k]):
                self.down(part, k, step).start()
        if k > top:
            level = 2 * top - k
            self.arrived(part, level, 2)
            self.arrived(part, level, 3)
        if top <= k < 2 * top:
            for step in range(1, self.size[2 * top - 1 - k]):
                self.up(part, 2 * top - 1 - k, step).start()
        if k == 2 * top - 1:
            self.save(part).start()


def kinds(mesh_rows, mesh_batch):
    x_n, z_n = mesh_rows // 2, mesh_batch // LOW
    return [2, LOW, x_n * z_n] if SPREAD else [2, LOW, x_n, z_n]


def columns(mesh_rows, mesh_batch):
    sizes = {w: w * padded(mesh_rows, mesh_batch, 2 * D * (CB // w)) for w in (256, 128)}
    return min(sizes, key=sizes.get)


def padded(mesh_rows, mesh_batch, count):
    unit = 16 * math.prod(kinds(mesh_rows, mesh_batch))
    return -(-count // unit) * unit


def sum_scratch(mesh_rows, mesh_batch, parts, count, width):
    size = kinds(mesh_rows, mesh_batch)
    shapes = [pltpu.VMEM((parts * count, width), BF16)] * 2
    for n in size:
        count //= n
        shapes.append(pltpu.VMEM((parts, (n - 1) * count, width), BF16))
    return shapes + [pltpu.SemaphoreType.DMA((4, parts)) for n in size] + [pltpu.SemaphoreType.DMA((parts,))]


def backward_kernel(row_count, batch_count, groups, pair, place, filt_l, filt_s, gain1, gain2, w1, w2, tl, ts, tlb, tsb,
                    mix, fold, outs, do_in, xs, zs, both_scales, spec, vs, gs, ps,
                    out_land, grad_land, weights_out, small_out,
                    dx, dv, do, dh, gslots, dvec, dhid, dfl, dfs, out_sem, grad_sem, own_sem, *sums):
    i = pl.program_id(0)
    batch, row = lax.axis_index("batch"), lax.axis_index("rows")
    chunks, pairs = FF // CB, groups // pair
    per = chunks + pairs
    compute_steps = LAYERS * per
    layer, q = LAYERS - 1 - i // per, i % per
    width = columns(row_count, batch_count)
    part_rows = padded(row_count, batch_count, 2 * D * (CB // width))
    small_rows = padded(row_count, batch_count, SMALL)
    sums_of = []
    for out, count in ((weights_out, part_rows), (small_out, small_rows)):
        n = len(kinds(row_count, batch_count))
        sums_of.append(Sum(row_count, batch_count, sums[0], sums[1], out, count, sums[2 : 2 + n], sums[2 + n : 2 + 2 * n], sums[2 + 2 * n]))
        sums = sums[3 + 2 * n :]
    weights, small = sums_of

    def send_out(m, g):
        return pltpu.make_async_remote_copy(
            src_ref=outs.at[m, g], dst_ref=out_land.at[m, g], send_sem=out_sem.at[0, m - 1, g], recv_sem=out_sem.at[1, m - 1, g],
            device_id=(batch, lax.rem(row + (row_count - m), row_count)), device_id_type=MESH)

    def send_grad(m, g):
        return pltpu.make_async_remote_copy(
            src_ref=gslots.at[m, g], dst_ref=grad_land.at[m, g], send_sem=grad_sem.at[0, m - 1, g], recv_sem=grad_sem.at[1, m - 1, g],
            device_id=(batch, lax.rem(row + (row_count - m), row_count)), device_id_type=MESH)

    def keep_out():
        return pltpu.make_async_copy(outs.at[0], out_land.at[0], own_sem.at[0])

    def keep_grad():
        return pltpu.make_async_copy(gslots.at[0], grad_land.at[0], own_sem.at[1])

    plan = {key: [a for a in PLAN[key] if a[0] != -2 or groups == 6] for key in PLAN}
    if groups != 6:
        plan[compute_steps - 1, 9] = [(-2, g) for g in range(groups)] + plan[compute_steps - 1, 9]
    left = set(plan)

    def do_now(part, k):
        if part >= 0:
            weights.stage(part, k)
        elif part == -1:
            small.stage(0, k)
        elif k < groups:
            for m in range(1, row_count):
                (send_grad if part == -2 else send_out)(m, k).start()

    def advance(place, steps):
        for at in steps:
            found = sorted(key for key in left if key[0] == at and (key[1] == place or place == 9))
            if found:
                @pl.when(i == at)
                def _():
                    for key in found:
                        left.discard(key)
                        for part, k in plan[key]:
                            do_now(part, k)

    first_steps = [at for at in range(compute_steps) if at % per < chunks]
    second_steps = [at for at in range(compute_steps) if at % per >= chunks]

    @pl.when(i == 0)
    def _():
        barrier = pltpu.get_barrier_semaphore()
        greeted = 0
        for m in range(1, row_count):
            pl.semaphore_signal(barrier, inc=1, device_id=(batch, lax.rem(row + m, row_count)), device_id_type=MESH)
            greeted += 1
        for level in range(1, weights.levels):
            for step in range(1, weights.size[level]):
                pl.semaphore_signal(barrier, inc=1, device_id=weights.others[level][step - 1][0], device_id_type=MESH)
                greeted += 1
        keep_out().start()
        if part_rows > 2 * D * (CB // width):
            weights.acc[...] = jnp.zeros_like(weights.acc)
        for g in range(groups):
            dx[g] = do_in[g].astype(F32)
        for ref in (dvec, dfl, dfs):
            ref[...] = jnp.zeros_like(ref)
        pl.semaphore_wait(barrier, greeted)

    @pl.when((i < compute_steps) & (q == 0))
    def _():
        for g in range(groups):
            rows = pl.ds(g * T, T)
            low = dx[g].astype(BF16)
            do[g] = low
            dvec[layer, 4:5] += jnp.sum(low.astype(F32), axis=0, keepdims=True)
        dv[...] = jnp.zeros_like(dv)

    @pl.when((i < compute_steps) & (q < chunks))
    def _():
        sums = jnp.zeros((1, CB), F32)
        for g in range(0, groups, pair):
            rows = slice(g * T, (g + pair) * T)
            some = do[g : g + pair].reshape(pair * T, D)
            slope = ps[0, g : g + pair].reshape(pair * T, CB)
            part = (dot_nt(some, w2[0]) * slope.astype(F32)).astype(BF16)
            dh[rows] = part
            sums = sums + jnp.sum(part.astype(F32), axis=0, keepdims=True)
            advance(g // pair, first_steps)
        part = (LAYERS - 1 - layer) * chunks + q
        base = part * part_rows
        dhid[layer, :, pl.ds(pl.multiple_of(q * CB, CB), CB)] = sums
        one = dot_tn(vs[0].reshape(groups * T, D), dh[...])
        two = dot_tn(do[...].reshape(groups * T, D), gs[0].reshape(groups * T, CB))
        for c in range(CB // width):
            cols = slice(c * width, (c + 1) * width)
            weights.acc[weights.rows(base + c * D, D), :] = one[:D, cols].astype(BF16)
            weights.acc[weights.rows(base + (CB // width + c) * D, D), :] = two[:, cols].astype(BF16)
        advance(3, first_steps)
        for g in range(0, groups, pair):
            dv[g : g + pair] += dot_nt(dh[g * T : (g + pair) * T], w1[0]).reshape(pair, T, D)

    @pl.when((i < compute_steps) & (q >= chunks))
    def _():
        side = lambda parts: jnp.concatenate(parts, axis=1)
        lanes = lambda a: [a[:, j * D : (j + 1) * D] for j in range(pair)]
        row_sum = lambda a: jnp.sum(a, axis=0, keepdims=True)
        first = (q - chunks) * pair
        dz = []
        for j in range(pair):
            dvg = dv[first + j]
            unit = zs[0, j].astype(F32)
            dvec[layer, 2:3] += row_sum(dvg * unit)
            dvec[layer, 3:4] += row_sum(dvg)
            dz.append(normal_back(dvg, gain2[pl.ds(layer, 1)], unit, both_scales[0, j, :, 1:2]).astype(BF16))
        advance(0, second_steps)
        yl, ysm = analyse(tl[...], ts[...], side(dz))
        dl, ds = [], []
        for j, (a, b) in enumerate(zip(lanes(yl), lanes(ysm))):
            lr, li = a[:NL], a[NL:]
            sr, si = b[: PER * NS], b[PER * NS :]
            xr, xi = spec[0, j, :NL].astype(F32), spec[0, j, NL : 2 * NL].astype(F32)
            dfl[layer, :NL] += lr * xr + li * xi
            dfl[layer, NL:] += li * xr - lr * xi
            gr, gi = filt_l[0, 0], filt_l[0, 1]
            dl.append(jnp.concatenate([lr * gr + li * gi, li * gr - lr * gi], axis=0).astype(BF16))
            small_spec = spec[0, j, 2 * NL :].astype(F32)
            xr, xi = small_spec[: PER * NS], small_spec[PER * NS :]
            once = lambda a: a[:NS] + a[NS : 2 * NS] + a[2 * NS :]
            dfs[layer, :NS] += once(sr * xr + si * xi)
            dfs[layer, NS:] += once(si * xr - sr * xi)
            gr, gi = thrice(filt_s[0, 0]), thrice(filt_s[0, 1])
            ds.append(jnp.concatenate([sr * gr + si * gi, si * gr - sr * gi], axis=0).astype(BF16))
        advance(1, second_steps)
        grads = []
        for j, du in enumerate(lanes(synthesise(tlb[...], tsb[...], side(dl), side(ds)))):
            unit = xs[0, j].astype(F32)
            dvec[layer, 0:1] += row_sum(du * unit)
            dvec[layer, 1:2] += row_sum(du)
            grad = dx[first + j] + normal_back(du, gain1[pl.ds(layer, 1)], unit, both_scales[0, j, :, 0:1])
            dx[first + j] = grad
            grads.append(grad.astype(BF16))
        advance(2, second_steps)

        @pl.when(layer == 0)
        def _():
            spread = dot(place[...], side(grads)).astype(BF16)
            for j in range(pair):
                for m in range(row_count):
                    gslots[m, first + j] = spread[m * BAND : (m + 1) * BAND, j * D : (j + 1) * D]

    def lay_out(layers):
        exact = partial(jnp.dot, preferred_element_type=F32, precision=HIGHEST)
        mix_t = mix[...].T
        for n in layers:
            for c in range(2):
                at = (n * 2 + c) * NL
                small.acc[at : at + NL, :] = (dfl[n, c * NL : (c + 1) * NL] * fold[...]
                                              + exact(mix_t, dfs[n, c * NS : (c + 1) * NS])).astype(BF16)

    @pl.when(i == compute_steps - pairs - 1)
    def _():
        small.acc[...] = jnp.zeros_like(small.acc)
        lay_out(range(1, LAYERS))

    @pl.when(i == compute_steps - 1)
    def _():
        lay_out([0])
        at = LAYERS * 2 * NL
        rest = [dvec[n, k : k + 1] for n in range(LAYERS) for k in range(5)]
        rest += [dhid[n, :, c : c + D] for n in range(LAYERS) for c in range(0, FF, D)]
        rest.append(jnp.zeros((-len(rest) % 16, D), F32))
        rest = jnp.concatenate(rest, axis=0).astype(BF16)
        small.acc[at : at + rest.shape[0], :] = rest
        keep_grad().start()

    advance(9, range(compute_steps))

    @pl.when(i == pl.num_programs(0) - 1)
    def _():
        keep_out().wait()
        keep_grad().wait()
        for m in range(1, row_count):
            @pl.loop(0, groups)
            def _(g):
                send_out(m, g).wait()
                send_grad(m, g).wait()
        for part in range(LAYERS * chunks):
            weights.save(part).wait()
        small.save(0).wait()


def backward(mesh, groups, pair, small, tabs, mix, fold, outs, do, saved):
    rows, batch = mesh.shape["rows"], mesh.shape["batch"]
    place, filt_l, filt_s, gain1, gain2, w1, w2 = small
    chunks, pairs = FF // CB, groups // pair
    per, last = chunks + pairs, LAYERS - 1
    steps = LAYERS * per
    layer = lambda i: jnp.maximum(last - i // per, 0)
    when = lambda i: jnp.where(i < LAYERS * per, i % per, per - 1)
    chunk = lambda i: jnp.minimum(when(i), chunks - 1)
    place_of = lambda i: jnp.maximum(when(i) - chunks, 0)
    per_layer = lambda a: pl.BlockSpec((1,) + a.shape[1:], lambda i: (layer(i),) + (0,) * (a.ndim - 1))
    by_pair = lambda a: pl.BlockSpec((1, pair) + a.shape[2:], lambda i: (layer(i), place_of(i), 0, 0))
    by_chunk = lambda a: pl.BlockSpec((1, groups, T, CB), lambda i: (layer(i), 0, 0, chunk(i)))
    xs, zs, scales, spec, vs, gs, ps = saved
    hbm = pl.BlockSpec(memory_space=pl.ANY)
    width = columns(rows, batch)
    part_rows, small_rows = padded(rows, batch, 2 * D * (CB // width)), padded(rows, batch, SMALL)
    dma = pltpu.SemaphoreType.DMA
    return pl.pallas_call(
        partial(backward_kernel, rows, batch, groups, pair),
        grid=(steps,),
        in_specs=[whole(place.shape), per_layer(filt_l), per_layer(filt_s), whole(gain1.shape), whole(gain2.shape)]
        + [pl.BlockSpec((1, D, CB), lambda i: (layer(i), 0, chunk(i))), pl.BlockSpec((1, CB, D), lambda i: (layer(i), chunk(i), 0))]
        + [whole(a.shape) for a in (*tabs, mix, fold)] + [hbm, whole(do.shape)]
        + [by_pair(xs), by_pair(zs), by_pair(scales), by_pair(spec), per_layer(vs), by_chunk(gs), by_chunk(ps)],
        out_specs=[hbm] * 4,
        out_shape=[jax.ShapeDtypeStruct((rows, groups, BAND, D), BF16)] * 2
        + [jax.ShapeDtypeStruct((LAYERS * chunks * part_rows, width), BF16), jax.ShapeDtypeStruct((small_rows, D), BF16)],
        scratch_shapes=[pltpu.VMEM((groups, T, D), F32), pltpu.VMEM((groups, T, D), F32), pltpu.VMEM((groups, T, D), BF16),
                        pltpu.VMEM((groups * T, CB), BF16), pltpu.VMEM((rows, groups, BAND, D), BF16),
                        pltpu.VMEM((LAYERS, 5, D), F32), pltpu.VMEM((LAYERS, 1, FF), F32),
                        pltpu.VMEM((LAYERS, 2 * NL, D), F32), pltpu.VMEM((LAYERS, 2 * NS, D), F32),
                        dma((2, rows - 1, groups)), dma((2, rows - 1, groups)), dma((2,))]
        + sum_scratch(rows, batch, LAYERS * chunks, part_rows, width) + sum_scratch(rows, batch, 1, small_rows, D),
        compiler_params=pltpu.CompilerParams(collective_id=2, has_side_effects=True, vmem_limit_bytes=VMEM_LIMIT),
        name="backward",
    )(place, filt_l, filt_s, gain1, gain2, w1, w2, *tabs, mix, fold, outs, do, xs, zs, scales, spec, vs, gs, ps)


def unpack_kernel(groups, order, outs, grads, weights, small, large_out, small_crops, large_grad, small_grad, dw1, dw2, dfilter, dhid,
                  *rest):
    dvec, rest = rest[:5], rest[5:]
    given, weight, large, little, one, two, in_sem, weight_sem, out_sem, done_sem = rest
    rows = outs.shape[0]
    parts, chunks, width = weight.shape[0], FF // CB, weight.shape[2]
    halves = CB // width

    def read(dev, kind):
        return pltpu.make_async_copy((outs, grads)[kind].at[order[dev]], given.at[kind, dev], in_sem.at[kind, dev])

    def read_weight(part):
        return pltpu.make_async_copy(weights.at[part], weight.at[part], weight_sem.at[part])

    def write(dev, kind):
        to_large, to_little = ((large_out, small_crops), (large_grad, small_grad))[kind]
        return (pltpu.make_async_copy(large.at[kind, dev], to_large.at[pl.ds(dev * groups, groups)], out_sem.at[kind, 0, dev]),
                pltpu.make_async_copy(little.at[kind, dev], to_little.at[pl.ds(dev * groups * PER, groups * PER)], out_sem.at[kind, 1, dev]))

    def write_weight(part):
        layer, at = LAYERS - 1 - part // chunks, part % chunks * CB
        return (pltpu.make_async_copy(one.at[part], dw1.at[layer, :, pl.ds(at, CB)], done_sem.at[0, part]),
                pltpu.make_async_copy(two.at[part], dw2.at[layer, pl.ds(at, CB)], done_sem.at[1, part]))

    for part in range(parts):
        read_weight(part).start()
    for dev in range(rows):
        for kind in range(2):
            read(dev, kind).start()
    for part in range(parts):
        read_weight(part).wait()
        for c in range(halves):
            cols = slice(c * width, (c + 1) * width)
            one[part, :, cols] = weight[part, c * D : (c + 1) * D].astype(F32)
            two[part, cols] = weight[part, (halves + c) * D : (halves + c + 1) * D].astype(F32).T
        for copy in write_weight(part):
            copy.start()
    for dev in range(rows):
        for kind in range(2):
            read(dev, kind).wait()

            @pl.loop(0, groups)
            def _(g):
                block = given[kind, dev, g].astype(F32)
                for w in range(WL):
                    large[kind, dev, g, 0, w] = block[w * BL : (w + 1) * BL]
                for p in range(PER):
                    for w in range(WS):
                        at = BL * WL + (p * WS + w) * BS
                        little[kind, dev, g * PER + p, 0, w] = block[at : at + BS]

            for copy in write(dev, kind):
                copy.start()
    at = LAYERS * 2 * NL
    for n in range(LAYERS):
        for c in range(2):
            dfilter[n, c] = small[(n * 2 + c) * NL : (n * 2 + c + 1) * NL].astype(F32)
    others = small[at : at + 32].astype(F32)
    for n in range(LAYERS):
        for k in range(5):
            dvec[k][n : n + 1] = others[n * 5 + k : n * 5 + k + 1]
        for c in range(FF // D):
            r = LAYERS * 5 + n * (FF // D) + c
            dhid[n : n + 1, c * D : (c + 1) * D] = others[r : r + 1]
    for part in range(parts):
        for copy in write_weight(part):
            copy.wait()
    for dev in range(rows):
        for kind in range(2):
            for copy in write(dev, kind):
                copy.wait()


def unpack(mesh, groups, pair, outs, grads, weights, small):
    rows = mesh.shape["rows"]
    me = lax.axis_index("rows")
    crops = rows * groups
    width = weights.shape[1]
    halves = CB // width
    parts = LAYERS * (FF // CB)
    weights = weights.reshape(parts, -1, width)[:, : 2 * D * halves]
    order = lax.rem(jnp.arange(rows, dtype=jnp.int32) + (rows - me), rows)
    large_shape, little_shape = (crops, 1, WL, BL, D), (crops * PER, 1, WS, BS, D)
    shapes = [(LAYERS, 2, NL, D), (LAYERS, FF)] + [(LAYERS, D)] * 5
    hbm, vmem, dma = pl.BlockSpec(memory_space=pl.ANY), pl.BlockSpec(memory_space=pltpu.VMEM), pltpu.SemaphoreType.DMA
    return pl.pallas_call(
        partial(unpack_kernel, groups),
        in_specs=[scalars()] + [hbm] * 3 + [vmem],
        out_specs=[hbm] * 6 + [vmem] * len(shapes),
        out_shape=[jax.ShapeDtypeStruct(s, F32) for s in [large_shape, little_shape] * 2 + [(LAYERS, D, FF), (LAYERS, FF, D)] + shapes],
        scratch_shapes=[pltpu.VMEM((2, rows, groups, BAND, D), BF16), pltpu.VMEM(weights.shape, BF16),
                        pltpu.VMEM((2, rows, groups, 1, WL, BL, D), F32), pltpu.VMEM((2, rows, groups * PER, 1, WS, BS, D), F32),
                        pltpu.VMEM((parts, D, CB), F32), pltpu.VMEM((parts, CB, D), F32),
                        dma((2, rows)), dma((parts,)), dma((2, 2, rows)), dma((2, parts))],
        compiler_params=pltpu.CompilerParams(vmem_limit_bytes=VMEM_LIMIT),
        name="unpack",
    )(order, outs, grads, weights, small)


def wanted_rows():
    t, c = np.arange(T), np.arange(BAND)
    small_t, small_c = t >= TL, c >= BL * WL
    at = np.where(small_t, (t - TL) % TS, t)
    wide = np.where(small_t, WS, WL)
    r, w, crop = at // wide, at % wide, np.where(small_t, (t - TL) // TS, 0)
    at_c = np.where(small_c, (c - BL * WL) % (BS * WS), c)
    slots = np.where(small_c, BS, BL)
    s_c, w_c, crop_c = at_c % slots, at_c // slots, np.where(small_c, (c - BL * WL) // (BS * WS), 0)
    same = (small_t[:, None] == small_c) & (w[:, None] == w_c) & (crop[:, None] == crop_c)
    return np.where(same, r[:, None] - s_c, -99).astype(np.int32), s_c[None].astype(np.int32)


def interp_tables():
    fold_l = np.where((np.arange(FL) == 0) | (2 * np.arange(FL) == WL), 1.0, 2.0)
    fold_s = np.where((np.arange(FS) == 0) | (2 * np.arange(FS) == WS), 1.0, 2.0)
    each = lambda n, times: np.repeat(np.eye(n), times, axis=0)
    again = lambda n, times: np.tile(np.eye(n), (times, 1))
    return [jnp.asarray(a, F32) for a in (each(HS, FS), each(HL, FL).T, again(FS, HS) * np.tile(fold_s, HS)[:, None],
                                          again(FL, HL).T, np.tile(fold_l, HL)[:, None])]


def local(mesh, large_in, small_in, large_cot, small_cot, crop_counts, band_bounds, row_interp, col_interp,
          norm1_gain, norm1_bias, filters, norm2_gain, norm2_bias, fc1_weight, fc1_bias, fc2_weight, fc2_bias):
    rows = mesh.shape["rows"]
    me = lax.axis_index("rows")
    crops = large_in.shape[0]
    groups = crops // rows
    pair = 2 if groups % 2 == 0 else 1
    tabs = tables()
    filters = filters.reshape(LAYERS, 2, NL, D)

    arrays = [a.transpose(0, 1, 3, 2, 4) for a in (large_in, small_in, large_cot, small_cot)]
    need, slot = wanted_rows()
    extras = (jnp.asarray(need), jnp.asarray(slot), row_interp, col_interp, *interp_tables())
    outs, *saved, do, place, filt_l, filt_s, mix = forward(mesh, groups, pair, arrays, crop_counts, band_bounds,
                               (filters, norm1_gain, norm1_bias, norm2_gain, norm2_bias, fc1_weight, fc1_bias, fc2_weight, fc2_bias,
                                *tabs, *extras))
    outs, grads, weights, small = backward(
        mesh, groups, pair, (place, filt_l, filt_s, norm1_gain, norm2_gain, fc1_weight, fc2_weight), tabs,
        mix, extras[-1], outs, do, saved)
    large_out, small_out, large_grad, small_grad, dw1, dw2, dfilter, dhid, *dvec = unpack(
        mesh, groups, pair, outs, grads, weights, small)
    large_out, small_out, large_grad, small_grad = (
        a.transpose(0, 1, 3, 2, 4) for a in (large_out, small_out, large_grad, small_grad))
    return (large_out, small_out, large_grad, small_grad, dvec[0], dvec[1], dfilter.reshape(LAYERS, 2, HL, FL, D), dvec[2], dvec[3],
            dw1, dhid, dw2, dvec[4])


def solution(mesh):
    split = P("batch", "rows", None, None, None)
    return jax.shard_map(partial(local, mesh), mesh=mesh, in_specs=(split,) * 4 + (P("batch", None),) + (P(),) * 12,
                         out_specs=(split,) * 4 + (P(),) * 9, check_vma=False)
```
